128 devices in a mesh: row: 4 (over z_hi, core), col: 32 (over x, y, z_lo).
Axes of the slice: x: 4, y: 4, z: 4 (z_hi: 2, z_lo: 2; z = z_hi * 2 + z_lo), core: 2. Of those that a mesh axis runs over, the one named last changes fastest.
Arguments:
- node_features: float32 [32768, 256], P(('col', 'row')), may hold values from -6 to 6
- self_weight: float32 [256, 256], replicated, may hold values from -0.375 to 0.375
- neighbour_weight: float32 [256, 256], replicated, may hold values from -0.375 to 0.375
- layer_bias: float32 [256], replicated, may hold values from -3 to 3
- tile_values: float32 [4, 32, 192, 128, 128], P('row', 'col'), as said below
- tile_dest: int32 [4, 32, 192], P('row', 'col'), may hold values from 0 to 63
- tile_source: int32 [4, 32, 192], P('row', 'col'), may hold values from 0 to 7
- tile_count: int32 [4, 32], P('row', 'col'), may hold values from 48 to 192, as said below
- cotangent: float32 [32768, 256], P(('col', 'row')), may hold values from -6 to 6
Outputs:
- layer_out: float32 [32768, 256], P(('col', 'row'))
- grad_features: float32 [32768, 256], P(('col', 'row'))
- grad_self_weight: float32 [256, 256], replicated
- grad_neighbour_weight: float32 [256, 256], replicated
- grad_bias: float32 [256], replicated
The draws below stay inside these ranges and needn't reach their ends.
Inputs may be any that keep to these rules, and one draw needn't show every extreme that they name: `tile_count`: list positions at or past a device's count are unused; some device lists exactly 192 tiles. `tile_values`: Non-negative edge weights.
All inputs are finite; a program needn't handle non-finite values.
Results may differ from the reference program's by a relative error of at most 0.0003.
Values sent between devices are 32-bit elements; how exact they have to be, the bound alone decides.
A program may use at most 192 MiB of HBM per device.

```python
import jax
import jax.numpy as jnp
from jax import lax

WIDTH = 256
TILE = 128
BLOCKS_DEV = 2
SLOTS = 192
NODES = 32768
DEST_BLOCKS = 64
SOURCE_BLOCKS = 8
N_ROW = 4
N_COL = 32


def draw_tile_values(key, part):
    key = jax.random.fold_in(key, 5)
    base_key, row_key, col_key = jax.random.split(key, 3)
    shape_all = (N_ROW, N_COL, SLOTS, TILE, TILE)
    base_values = jax.random.uniform(base_key, shape_all, jnp.float32)
    rise_factor = 2.0
    log_top = 2.3
    row_scale = jnp.exp(log_top * jax.random.uniform(row_key, (N_ROW, N_COL, SLOTS, TILE, 1), jnp.float32))
    col_scale = jnp.exp(log_top * jax.random.uniform(col_key, (N_ROW, N_COL, SLOTS, 1, TILE), jnp.float32))
    col_factor = 1.0 + rise_factor * jnp.arange(N_COL, dtype=jnp.float32) / max(N_COL - 1, 1)
    return base_values * row_scale * col_scale * col_factor[None, :, None, None, None]


def draw_tile_count(key, part):
    key = jax.random.fold_in(key, 11)
    hub_key, light_key, heavy_key = jax.random.split(key, 3)
    hub_group = jax.random.randint(hub_key, (), 0, N_ROW)
    light_counts = jax.random.randint(light_key, (N_ROW, N_COL), SLOTS // 4, SLOTS // 2 + 1)
    heavy_counts = SLOTS - jax.random.randint(heavy_key, (N_ROW, N_COL), 0, SLOTS // 8 + 1)
    group_ids = jnp.arange(N_ROW)[:, None]
    shard_ids = jnp.arange(N_COL)[None, :]
    counts = jnp.where(group_ids == hub_group, heavy_counts, light_counts)
    return jnp.where((group_ids == hub_group) & (shard_ids == 0), SLOTS, counts).astype(jnp.int32)


def set_ends(values, stream_key, smallest, largest):
    shape = values.shape
    index_at = [jax.random.randint(jax.random.fold_in(stream_key, axis), (), 0, shape[axis]) for axis in range(len(shape))]
    values = values.at[tuple(index_at)].set(smallest)
    longest = shape.index(max(shape))
    index_at[longest] = (index_at[longest] + 1) % shape[longest]
    return values.at[tuple(index_at)].set(largest)


def steps_of(stream_key, dims, cuts, smallest, largest):
    def one(position, parts):
        steps = jax.random.uniform(jax.random.fold_in(jax.random.fold_in(stream_key, 6), position), (parts,), jnp.float32, smallest / len(cuts), largest / len(cuts))
        return jnp.repeat(jnp.exp(steps), dims[position] // parts).reshape((-1,) + (1,) * (len(dims) - position - 1))

    level = one(*cuts[0])
    for cut in cuts[1:]:
        level = level * one(*cut)
    return level


def centred(rng, dims, width, most, cuts=(), held_as=jnp.bfloat16):
    entries = width * jax.random.normal(rng, dims, jnp.float32)
    if cuts:
        entries = entries * steps_of(rng, dims, cuts, -0.22, 0.18)
    return jnp.clip(entries, -most, most).astype(held_as)


def setup_inputs(seed: int = 0) -> dict:
    arg_keys = jax.random.split(jax.random.key(seed), 10)
    return {
        "node_features": centred(arg_keys[0], (NODES, WIDTH), 1.0, 6.0, ((0, 128),), jnp.float32),
        "self_weight": centred(arg_keys[1], (WIDTH, WIDTH), WIDTH ** -0.5, 0.375, (), jnp.float32),
        "neighbour_weight": centred(arg_keys[2], (WIDTH, WIDTH), WIDTH ** -0.5, 0.375, (), jnp.float32),
        "layer_bias": centred(arg_keys[3], (WIDTH,), 0.5, 3.0, (), jnp.float32),
        "tile_values": draw_tile_values(jax.random.fold_in(arg_keys[9], 71), 0),
        "tile_dest": set_ends(jax.random.randint(arg_keys[5], (N_ROW, N_COL, SLOTS), 0, DEST_BLOCKS), jax.random.fold_in(arg_keys[5], 1), 0, DEST_BLOCKS - 1).astype(jnp.int32),
        "tile_source": set_ends(jax.random.randint(arg_keys[6], (N_ROW, N_COL, SLOTS), 0, SOURCE_BLOCKS), jax.random.fold_in(arg_keys[6], 1), 0, SOURCE_BLOCKS - 1).astype(jnp.int32),
        "tile_count": draw_tile_count(jax.random.fold_in(arg_keys[9], 71), 0),
        "cotangent": centred(arg_keys[8], (NODES, WIDTH), 1.0, 6.0, ((0, 128),), jnp.float32),
    }


EPSILON = 1e-05
HIGHEST = lax.Precision.HIGHEST

def finish(pre_act):
    activated = jax.nn.silu(pre_act)
    return activated * lax.rsqrt(lax.optimization_barrier(jnp.mean(activated * activated, axis=-1, keepdims=True)) + EPSILON)

def output_head(node_rows, neighbour, self_weight, neighbour_weight, layer_bias):
    pre_act = jnp.dot(node_rows, self_weight, precision=HIGHEST) + jnp.dot(neighbour, neighbour_weight, precision=HIGHEST) + layer_bias
    return finish(pre_act)

def one_hot_rows(labels, extent, live_mask):
    return (labels[None, :] == jnp.arange(extent)[:, None]).astype(jnp.float32) * live_mask[None, :]

def reference(node_features, self_weight, neighbour_weight, layer_bias, tile_values, tile_dest, tile_source, tile_count, cotangent):
    blocks = node_features.reshape(N_COL, SOURCE_BLOCKS, TILE, WIDTH)
    slot_ids = jnp.arange(SLOTS)

    def forward_group(row_group):

        def scan_step(state_pair, col_shard):
            running_sum, degree_sum = state_pair
            values = tile_values[row_group, col_shard]
            live_mask = (slot_ids < tile_count[row_group, col_shard]).astype(jnp.float32)
            dest_hot = one_hot_rows(tile_dest[row_group, col_shard], DEST_BLOCKS, live_mask)
            picked = blocks[col_shard][tile_source[row_group, col_shard]]
            products = jnp.einsum('tij,tjf->tif', values, picked, precision=HIGHEST)
            running_sum = running_sum + jnp.dot(dest_hot, products.reshape(SLOTS, TILE * WIDTH), precision=HIGHEST)
            degree_sum = degree_sum + jnp.dot(dest_hot, lax.optimization_barrier(jnp.sum(values, axis=2)), precision=HIGHEST)
            return ((running_sum, degree_sum), None)
        start_state = (jnp.zeros((DEST_BLOCKS, TILE * WIDTH), jnp.float32), jnp.zeros((DEST_BLOCKS, TILE), jnp.float32))
        final_state, _ = lax.scan(scan_step, start_state, jnp.arange(N_COL))
        return final_state
    sums_all, degrees_all = lax.map(forward_group, jnp.arange(N_ROW))
    summed = sums_all.reshape(N_ROW, N_COL, BLOCKS_DEV * TILE, WIDTH).transpose(1, 0, 2, 3).reshape(NODES, WIDTH)
    degree = degrees_all.reshape(N_ROW, N_COL, BLOCKS_DEV * TILE).transpose(1, 0, 2).reshape(NODES, 1)
    inv_root = lax.rsqrt(1.0 + degree)
    neighbour = summed * inv_root
    layer_out, pullback = jax.vjp(output_head, node_features, neighbour, self_weight, neighbour_weight, layer_bias)
    grad_direct, grad_neighbour, grad_self_weight, grad_neighbour_weight, grad_bias = pullback(cotangent)
    spread = (grad_neighbour * inv_root).reshape(N_COL, N_ROW, BLOCKS_DEV * TILE, WIDTH)
    spread = spread.transpose(1, 0, 2, 3).reshape(N_ROW, DEST_BLOCKS, TILE, WIDTH)

    def backward_shard(col_shard):

        def scan_step(running_sum, row_group):
            values = tile_values[row_group, col_shard]
            live_mask = (slot_ids < tile_count[row_group, col_shard]).astype(jnp.float32)
            source_hot = one_hot_rows(tile_source[row_group, col_shard], SOURCE_BLOCKS, live_mask)
            picked = spread[row_group][tile_dest[row_group, col_shard]]
            back_terms = jnp.einsum('tij,tif->tjf', values, picked, precision=HIGHEST)
            running_sum = running_sum + jnp.dot(source_hot, back_terms.reshape(SLOTS, TILE * WIDTH), precision=HIGHEST)
            return (running_sum, None)
        final_sum, _ = lax.scan(scan_step, jnp.zeros((SOURCE_BLOCKS, TILE * WIDTH), jnp.float32), jnp.arange(N_ROW))
        return final_sum
    back_all = lax.map(backward_shard, jnp.arange(N_COL))
    grad_features = grad_direct + back_all.reshape(NODES, WIDTH)
    return (layer_out, grad_features, grad_self_weight, grad_neighbour_weight, grad_bias)
```

```python
import functools

import jax
import jax.numpy as jnp
from jax import lax
from jax.experimental import pallas as pl
from jax.experimental.pallas import tpu as pltpu
from jax.sharding import PartitionSpec as P

EPSILON = 1e-05
F32 = jnp.float32
BF16 = jnp.bfloat16
MESH = pl.DeviceIdType.MESH
TILE = 128
WIDTH = 256
SLOTS = 192
DESTS = 64
SOURCES = 8
ROWS = 264
CHUNK = 16
CHUNKS = SLOTS // CHUNK
UNROLL = 4
RING = 16
LAG = 2
VMEM_LIMIT = 60 * 1024 * 1024

VM = pl.BlockSpec(memory_space=pltpu.VMEM)
SM = pl.BlockSpec(memory_space=pltpu.SMEM)
ANY = pl.BlockSpec(memory_space=pl.ANY)
DMA = pltpu.SemaphoreType.DMA


def split(a):
    hi = a.astype(BF16)
    return hi, (a - hi.astype(F32)).astype(BF16)


def mm(a, b, dims=((1,), (0,))):
    return lax.dot_general(a, b, (dims, ((), ())), preferred_element_type=F32)


def dot3(a, b, dims=((1,), (0,))):
    ah, al = split(a)
    bh, bl = split(b)
    return mm(ah, bh, dims) + (mm(ah, bl, dims) + mm(al, bh, dims))


def enter(devices):
    barrier = pltpu.get_barrier_semaphore()
    for device in devices:
        pl.semaphore_signal(barrier, inc=1, device_id=device, device_id_type=MESH)
    pl.semaphore_wait(barrier, len(devices))


def remote(src, dst, send, recv, device):
    return pltpu.make_async_remote_copy(
        src_ref=src, dst_ref=dst, send_sem=send, recv_sem=recv, device_id=device, device_id_type=MESH
    )


def gather_kernel(x_ref, out_ref, local_sem, send, recv):
    row, col = lax.axis_index("row"), lax.axis_index("col")
    hi, core = lax.div(row, 2), lax.rem(row, 2)
    mate = hi * 2 + (1 - core)
    far = (1 - hi) * 2 + core
    far_mate = (1 - hi) * 2 + (1 - core)
    enter([(mate, col), (far, col)])
    n = x_ref.shape[0]
    at = lambda r: out_ref.at[pl.ds(pl.multiple_of(r * n, n), n)]
    own = pltpu.make_async_copy(x_ref, at(row), local_sem)
    own.start()
    across = remote(x_ref, at(row), send.at[0], recv.at[0], (far, col))
    across.start()
    beside = remote(x_ref, at(row), send.at[1], recv.at[1], (mate, col))
    beside.start()
    across.wait_recv()
    onward = remote(at(far), at(far), send.at[2], recv.at[2], (mate, col))
    onward.start()
    beside.wait_recv()
    onward.wait_recv()
    own.wait()
    across.wait_send()
    beside.wait_send()
    onward.wait_send()


def gather_rows(x):
    return pl.pallas_call(
        gather_kernel,
        out_shape=jax.ShapeDtypeStruct((4 * x.shape[0], x.shape[1]), F32),
        in_specs=[VM],
        out_specs=VM,
        scratch_shapes=[DMA, DMA((3,)), DMA((3,))],
        compiler_params=pltpu.CompilerParams(collective_id=0, has_side_effects=True),
        name="gather_rows",
    )(x)


def tile_copy(tiles_hbm, tiles, sems, c):
    at = pl.ds(c * CHUNK, CHUNK)
    return pltpu.make_async_copy(tiles_hbm.at[at], tiles.at[at], sems.at[c])


def forward_kernel(dest, source, count, x_ref, tiles_hbm, out_hbm, tiles, acc, total, xhh, xlo, sems, out_sem):
    for c in range(CHUNKS):
        tile_copy(tiles_hbm, tiles, sems, c).start()
    live = count[0]
    for s in range(SOURCES):
        hi, lo = split(x_ref[s * TILE : (s + 1) * TILE, :])
        xhh[s, 0:TILE, :] = hi
        xhh[s, TILE:, :] = hi
        xlo[s] = lo

    def clear(d, _):
        acc[d] = jnp.zeros((ROWS, TILE), F32)
        total[d] = jnp.zeros((TILE, TILE), F32)
        return 0

    lax.fori_loop(0, DESTS + 1, clear, 0)

    def one(t):
        s = source[t]
        d = jnp.where(t < live, dest[t], DESTS)
        a = tiles[t]
        hi, lo = split(a)
        p = mm(jnp.concatenate([hi, lo], axis=1), xhh[s]) + mm(hi, xlo[s])
        acc[d, 0:TILE, :] += p[:, 0:TILE]
        acc[d, TILE : 2 * TILE, :] += p[:, TILE:]
        total[d] += a

    def group(g, _):
        for u in range(UNROLL):
            one(g * UNROLL + u)
        return 0

    def chunk(c, _):
        tile_copy(tiles_hbm, tiles, sems, c).wait()
        per = CHUNK // UNROLL
        return lax.fori_loop(c * per, (c + 1) * per, group, 0)

    lax.fori_loop(0, CHUNKS, chunk, 0)
    ones = jnp.ones((8, 2 * TILE), BF16)

    def degrees(g, _):
        for u in range(4):
            d = g * 4 + u
            hi, lo = split(total[d])
            acc[d, 2 * TILE :, :] = mm(ones, jnp.concatenate([hi, lo], axis=1), ((1,), (1,)))
        return 0

    lax.fori_loop(0, DESTS // 4, degrees, 0)
    out = pltpu.make_async_copy(acc.at[pl.ds(0, DESTS)], out_hbm, out_sem)
    out.start()
    out.wait()


def forward_tiles(dest, source, count, slab, values):
    return pl.pallas_call(
        forward_kernel,
        out_shape=jax.ShapeDtypeStruct((DESTS, ROWS, TILE), F32),
        in_specs=[SM, SM, SM, VM, ANY],
        out_specs=ANY,
        scratch_shapes=[
            pltpu.VMEM((SLOTS, TILE, TILE), F32),
            pltpu.VMEM((DESTS + 1, ROWS, TILE), F32),
            pltpu.VMEM((DESTS + 1, TILE, TILE), F32),
            pltpu.VMEM((SOURCES, 2 * TILE, WIDTH), BF16),
            pltpu.VMEM((SOURCES, TILE, WIDTH), BF16),
            DMA((CHUNKS,)),
            DMA,
        ],
        compiler_params=pltpu.CompilerParams(vmem_limit_bytes=VMEM_LIMIT),
        cost_estimate=pl.CostEstimate(
            flops=SLOTS * 6 * TILE * TILE * WIDTH, bytes_accessed=22_000_000, transcendentals=0
        ),
        name="forward_tiles",
    )(dest, source, count, slab, values)


def place(cycle, x, y):
    return (4 * x if cycle == 0 else 4 * y) + lax.rem(x + y, 4)


def chip(cycle, q):
    a = lax.div(q, 4)
    b = lax.rem(lax.rem(q, 4) + 4 - a, 4)
    return (a, b) if cycle == 0 else (b, a)


def step_place(p, k, t):
    return lax.rem(p + RING - t, RING) if k % 2 == 0 else lax.rem(p + t, RING)


SUM_ROWS = {(0, 0): (0, 136), (1, 0): (136, 128), (0, 1): (0, 128), (1, 1): (128, 136)}


def rms_silu(pre, cot):
    sig = 1.0 / (1.0 + jnp.exp(-pre))
    s = pre * sig
    r = lax.rsqrt(jnp.mean(s * s, axis=-1, keepdims=True) + EPSILON)
    inner = jnp.mean(cot * s, axis=-1, keepdims=True)
    ds = r * cot - s * (r * r * r * inner)
    return s * r, ds * sig * (1.0 + pre * (1.0 - sig))


PARTS = 32
PART_ROWS = 40
AR_SENDS = 17


def exchange_kernel(
    part_hbm, x_ref, ws_ref, wn_ref, bias_ref, cot_ref,
    layer_out, direct_out, g_out, gw_out,
    acc, rbuf, zbuf, gath, gwp, gws, r1, r2, r3, r4, own_part,
    load_sem, rs_send, rs_recv, zs_send, zs_recv, ag_send, ag_recv, zg_send, zg_recv, ar_send, ar_recv, out_sem,
):
    row, col = lax.axis_index("row"), lax.axis_index("col")
    zh, core = lax.div(row, 2), lax.rem(row, 2)
    x, y, z = lax.div(col, 8), lax.rem(lax.div(col, 2), 4), lax.rem(col, 2)
    column = lambda xx, yy, zz: xx * 8 + yy * 2 + zz
    places = [place(0, x, y), place(1, x, y)]
    nexts = []
    for k in range(4):
        q = lax.rem(places[k // 2] + (1 if k % 2 == 0 else RING - 1), RING)
        nexts.append((row, column(*chip(k // 2, q), z)))
    z_mate = (row, column(x, y, 1 - z))
    core_mate = (zh * 2 + (1 - core), col)
    x_others = [(row, column(lax.rem(x + d, 4), y, z)) for d in range(1, 4)]
    y_others = [(row, column(x, lax.rem(y + d, 4), z)) for d in range(1, 4)]
    far = (1 - zh) * 2 + core
    z_others = [z_mate, (far, col), (far, column(x, y, 1 - z))]

    def block(k, t, zz):
        bx, by = chip(k // 2, step_place(places[k // 2], k, t))
        return (bx * 4 + by) * 4 + zz * 2 + k % 2

    def load(k, sub, t):
        at = (block(k, t + 1, z if sub == 0 else 1 - z), pl.ds(*SUM_ROWS[k // 2, sub]))
        return pltpu.make_async_copy(part_hbm.at[at], acc.at[at], load_sem.at[k, sub, t])

    for k in range(4):
        for sub in (1, 0):
            load(k, sub, 0).start()
            load(k, sub, 1).start()
    enter([core_mate] + x_others + y_others + z_others)

    def sum_send(k, sub, t):
        at = (block(k, t + 1, z if sub == 0 else 1 - z), pl.ds(*SUM_ROWS[k // 2, sub]))
        to = rbuf.at[k, sub, t, pl.ds(0, SUM_ROWS[k // 2, sub][1])]
        return remote(acc.at[at], to, rs_send.at[k, sub, t], rs_recv.at[k, sub, t], nexts[k])

    def mate_send(k):
        at = pl.ds(*SUM_ROWS[k // 2, 1])
        b = block(k, 0, 1 - z)
        return remote(acc.at[b, at], zbuf.at[k % 2, at], zs_send.at[k], zs_recv.at[k], z_mate)

    def add_arrived(k, sub, t):
        sum_send(k, sub, t - 1).wait_recv()
        first, n = SUM_ROWS[k // 2, sub]
        b = block(k, t + 1, z if sub == 0 else 1 - z)
        acc[b, first : first + n, :] += rbuf[k, sub, t - 1, 0:n, :]

    def sum_step(sub, t):
        for k in range(4):

            @pl.when(t + 2 <= RING - 1)
            def _():
                load(k, sub, t + 2).start()

            load(k, sub, t).wait()

            @pl.when(t >= 1)
            def _():
                add_arrived(k, sub, t)

            @pl.when(t <= RING - 2)
            def _():
                sum_send(k, sub, t).start()

            if sub == 1:

                @pl.when(t == RING - 1)
                def _():
                    mate_send(k).start()

    def sum_loop(i, _):
        @pl.when(i <= RING - 1)
        def _():
            sum_step(1, i)

        @pl.when(i >= LAG)
        def _():
            sum_step(0, i - LAG)

        return 0

    lax.fori_loop(0, RING + LAG, sum_loop, 0)

    own = (x * 4 + y) * 4 + z * 2
    x_own = x_ref[...]
    ws, wn = ws_ref[...], wn_ref[...]
    own_term = dot3(x_own, ws)
    for k in range(4):
        mate_send(k).wait_recv()
    sums, inv = [], []
    for h in range(2):
        s = acc[own + h] + zbuf[h]
        degree = jnp.transpose(jnp.broadcast_to(s[2 * TILE : 2 * TILE + 1, :], (TILE, TILE)))
        root = lax.rsqrt(1.0 + degree)
        inv.append(jnp.concatenate([root, root], axis=1))
        sums.append(jnp.concatenate([s[0:TILE], s[TILE : 2 * TILE]], axis=1))
    inv = jnp.concatenate(inv, axis=0)
    neighbour = jnp.concatenate(sums, axis=0) * inv
    pre = own_term + dot3(neighbour, wn) + bias_ref[...]
    out, grad_pre = rms_silu(pre, cot_ref[...])
    layer_out[...] = out
    spread = dot3(grad_pre, wn, ((1,), (1,))) * inv
    for h in range(2):
        for half in range(2):
            gath[own + h, half * TILE : (half + 1) * TILE, :] = spread[
                h * TILE : (h + 1) * TILE, half * TILE : (half + 1) * TILE
            ]

    def rows_of(k):
        return pl.ds((k // 2) * TILE, TILE)

    def mate_give(k):
        at = (own + k % 2, rows_of(k))
        return remote(gath.at[at], gath.at[at], zg_send.at[k], zg_recv.at[k], z_mate)

    def mate_take(k):
        at = (block(k, 0, 1 - z), rows_of(k))
        return remote(gath.at[at], gath.at[at], zg_send.at[k], zg_recv.at[k], z_mate)

    def pass_on(k, sub, t):
        at = (block(k, t, z if sub == 0 else 1 - z), rows_of(k))
        return remote(gath.at[at], gath.at[at], ag_send.at[k, sub, t], ag_recv.at[k, sub, t], nexts[k])

    def take(k, sub, t):
        at = (block(k, t + 1, z if sub == 0 else 1 - z), rows_of(k))
        return remote(gath.at[at], gath.at[at], ag_send.at[k, sub, t], ag_recv.at[k, sub, t], nexts[k])

    for k in range(4):
        mate_give(k).start()
    for k in range(4):
        pass_on(k, 0, 0).start()

    gs = dot3(x_own, grad_pre, ((0,), (0,)))
    gn = dot3(neighbour, grad_pre, ((0,), (0,)))
    flat = [gs[:, 0:TILE], gs[:, TILE:], gn[:, 0:TILE], gn[:, TILE:]]
    gb = jnp.sum(grad_pre, axis=0, keepdims=True)
    gwp[...] = jnp.zeros_like(gwp)
    for i, f in enumerate(flat):
        gwp[i * WIDTH : (i + 1) * WIDTH, :] = f
    gwp[4 * WIDTH : 4 * WIDTH + 1, :] = gb[:, 0:TILE]
    gwp[4 * WIDTH + 1 : 4 * WIDTH + 2, :] = gb[:, TILE:]
    direct_out[...] = dot3(grad_pre, ws, ((1,), (1,)))

    n_core, n_x, n_y = 16 * PART_ROWS, 4 * PART_ROWS, PART_ROWS
    rows_at = lambda c, xx, yy, n: pl.ds(pl.multiple_of((c * 16 + xx * 4 + yy) * PART_ROWS, 8), n)
    span = lambda *at: gwp.at[rows_at(*at)]
    summed = lambda *at: gws.at[rows_at(*at)]
    hop = lambda i, src, dst, device: remote(src, dst, ar_send.at[i], ar_recv.at[i], device)
    zi = zh * 2 + z

    c1 = [hop(0, span(1 - core, 0, 0, n_core), r1, core_mate)]
    c2 = [hop(d, span(core, lax.rem(x + d, 4), 0, n_x), r2.at[d - 1], x_others[d - 1]) for d in range(1, 4)]
    c3 = [hop(3 + d, span(core, x, lax.rem(y + d, 4), n_y), r3.at[d - 1], y_others[d - 1]) for d in range(1, 4)]
    c4 = [hop(7 + d, own_part, r4.at[d], z_others[d]) for d in range(3)]
    mine = summed(core, x, y, n_y)
    c5 = [hop(9 + d, mine, mine, y_others[d - 1]) for d in range(1, 4)]
    mine_x = summed(core, x, 0, n_x)
    c6 = [hop(12 + d, mine_x, mine_x, x_others[d - 1]) for d in range(1, 4)]
    mine_c = summed(core, 0, 0, n_core)
    c7 = [hop(16, mine_c, mine_c, core_mate)]

    def launch(copies):
        for c in copies:
            c.start()

    def land(copies):
        for c in copies:
            c.wait()

    def add_parts(n, c, xx, terms):
        at = pl.ds(pl.multiple_of((core * 16 + c) * PART_ROWS, 8), n)
        v = gwp[at, :]
        for term in terms:
            v = v + term
        gwp[at, :] = v

    def phase0():
        launch(c1)

    def phase1():
        land(c1)
        add_parts(n_core, 0, 0, [r1[...]])
        launch(c2)

    def phase2():
        land(c2)
        add_parts(n_x, x * 4, 0, [r2[d] for d in range(3)])
        launch(c3)

    def phase3():
        land(c3)
        at = pl.ds(pl.multiple_of((core * 16 + x * 4 + y) * PART_ROWS, 8), n_y)
        own_part[...] = gwp[at, :] + r3[0] + r3[1] + r3[2]
        launch(c4)

    def phase4():
        land(c4)
        at = pl.ds(pl.multiple_of((core * 16 + x * 4 + y) * PART_ROWS, 8), n_y)
        gws[at, :] = (own_part[...] + r4[0]) + (r4[1] + r4[2])
        launch(c5)

    def phase5():
        for d in range(1, 4):
            peer = summed(core, x, lax.rem(y + 4 - d, 4), n_y)
            hop(9 + d, peer, peer, y_others[d - 1]).wait_recv()
        for c in c5:
            c.wait_send()
        launch(c6)

    def phase6():
        for d in range(1, 4):
            peer = summed(core, lax.rem(x + 4 - d, 4), 0, n_x)
            hop(12 + d, peer, peer, x_others[d - 1]).wait_recv()
        launch(c7)

    def phase7():
        peer = summed(1 - core, 0, 0, n_core)
        hop(16, peer, peer, core_mate).wait_recv()

    phases = [phase0, phase1, phase2, phase3, phase4, phase5, phase6, phase7]
    del zi

    def gather_step(sub, t):
        for k in range(4):
            if sub == 0:
                take(k, 0, t - 1).wait_recv()
            else:

                @pl.when(t == 0)
                def _():
                    mate_take(k).wait_recv()

                @pl.when(t >= 1)
                def _():
                    take(k, 1, t - 1).wait_recv()

            @pl.when(t <= RING - 2)
            def _():
                pass_on(k, sub, t).start()

    phase0()

    def gather_loop(i, _):
        @pl.when(i <= RING - 1)
        def _():
            gather_step(0, i)

        @pl.when(i >= LAG)
        def _():
            gather_step(1, i - LAG)

        for n in range(1, 8):

            @pl.when(i == 2 * n + 1)
            def _():
                phases[n]()

        return 0

    lax.fori_loop(1, RING + LAG, gather_loop, 0)
    out = pltpu.make_async_copy(gath, g_out, out_sem)
    out.start()
    gw_out[...] = gws[0 : 4 * WIDTH + 8, :]

    def drain(t, _):
        for k in range(4):
            for sub in range(2):
                sum_send(k, sub, t).wait_send()
                pass_on(k, sub, t).wait_send()
        return 0

    lax.fori_loop(0, RING - 1, drain, 0)
    for k in range(4):
        mate_send(k).wait_send()
        mate_give(k).wait_send()
    for copies in (c6, c7):
        for c in copies:
            c.wait_send()
    out.wait()


def exchange(part, x, ws, wn, bias, cot):
    n = x.shape[0]
    steps = RING - 1
    return pl.pallas_call(
        exchange_kernel,
        out_shape=(
            jax.ShapeDtypeStruct((n, WIDTH), F32),
            jax.ShapeDtypeStruct((n, WIDTH), F32),
            jax.ShapeDtypeStruct((DESTS, 2 * TILE, TILE), F32),
            jax.ShapeDtypeStruct((4 * WIDTH + 8, TILE), F32),
        ),
        in_specs=[ANY, VM, VM, VM, VM, VM],
        out_specs=(VM, VM, ANY, VM),
        scratch_shapes=[
            pltpu.VMEM((DESTS, ROWS, TILE), F32),
            pltpu.VMEM((4, 2, steps, 136, TILE), F32),
            pltpu.VMEM((2, ROWS, TILE), F32),
            pltpu.VMEM((DESTS, 2 * TILE, TILE), F32),
            pltpu.VMEM((PARTS * PART_ROWS, TILE), F32),
            pltpu.VMEM((PARTS * PART_ROWS, TILE), F32),
            pltpu.VMEM((16 * PART_ROWS, TILE), F32),
            pltpu.VMEM((3, 4 * PART_ROWS, TILE), F32),
            pltpu.VMEM((3, PART_ROWS, TILE), F32),
            pltpu.VMEM((3, PART_ROWS, TILE), F32),
            pltpu.VMEM((PART_ROWS, TILE), F32),
            DMA((4, 2, RING)),
            DMA((4, 2, steps)),
            DMA((4, 2, steps)),
            DMA((4,)),
            DMA((4,)),
            DMA((4, 2, steps)),
            DMA((4, 2, steps)),
            DMA((4,)),
            DMA((4,)),
            DMA((AR_SENDS,)),
            DMA((AR_SENDS,)),
            DMA,
        ],
        compiler_params=pltpu.CompilerParams(
            collective_id=1, has_side_effects=True, vmem_limit_bytes=VMEM_LIMIT
        ),
        name="exchange",
    )(part, x, ws, wn, bias.reshape(1, WIDTH), cot)


def backward_kernel(dest, source, count, g_hbm, tiles_hbm, out_ref, tiles, g, ghh, glo, acc, sems, g_sem):
    g_copy = pltpu.make_async_copy(g_hbm, g, g_sem)
    g_copy.start()
    for c in range(CHUNKS):
        tile_copy(tiles_hbm, tiles, sems, c).start()
    live = count[0]

    def clear(s, _):
        acc[s] = jnp.zeros((TILE, WIDTH), F32)
        return 0

    lax.fori_loop(0, SOURCES + 1, clear, 0)
    g_copy.wait()

    def cut(d, _):
        for half in range(2):
            hi, lo = split(g[d, half * TILE : (half + 1) * TILE, :])
            lanes = slice(half * TILE, (half + 1) * TILE)
            ghh[d, 0:TILE, lanes] = hi
            ghh[d, TILE:, lanes] = hi
            glo[d, :, lanes] = lo
        return 0

    lax.fori_loop(0, DESTS, cut, 0)

    def one(t):
        d = dest[t]
        s = jnp.where(t < live, source[t], SOURCES)
        hi, lo = split(tiles[t])
        p = mm(jnp.concatenate([hi, lo], axis=0), ghh[d], ((0,), (0,))) + mm(hi, glo[d], ((0,), (0,)))
        acc[s] += p

    def group(g_, _):
        for u in range(UNROLL):
            one(g_ * UNROLL + u)
        return 0

    def chunk(c, _):
        tile_copy(tiles_hbm, tiles, sems, c).wait()
        per = CHUNK // UNROLL
        return lax.fori_loop(c * per, (c + 1) * per, group, 0)

    lax.fori_loop(0, CHUNKS, chunk, 0)
    for s in range(SOURCES):
        out_ref[s * TILE : (s + 1) * TILE, :] = acc[s]


def backward_tiles(dest, source, count, g, values):
    return pl.pallas_call(
        backward_kernel,
        out_shape=jax.ShapeDtypeStruct((SOURCES * TILE, WIDTH), F32),
        in_specs=[SM, SM, SM, ANY, ANY],
        out_specs=VM,
        scratch_shapes=[
            pltpu.VMEM((SLOTS, TILE, TILE), F32),
            pltpu.VMEM((DESTS, 2 * TILE, TILE), F32),
            pltpu.VMEM((DESTS, 2 * TILE, WIDTH), BF16),
            pltpu.VMEM((DESTS, TILE, WIDTH), BF16),
            pltpu.VMEM((SOURCES + 1, TILE, WIDTH), F32),
            DMA((CHUNKS,)),
            DMA,
        ],
        compiler_params=pltpu.CompilerParams(vmem_limit_bytes=VMEM_LIMIT),
        cost_estimate=pl.CostEstimate(
            flops=SLOTS * 6 * TILE * TILE * WIDTH, bytes_accessed=22_000_000, transcendentals=0
        ),
        name="backward_tiles",
    )(dest, source, count, g, values)


def scatter_kernel(back_ref, direct_ref, out_ref, near, cross, send_buf, send, recv):
    row, col = lax.axis_index("row"), lax.axis_index("col")
    hi, core = lax.div(row, 2), lax.rem(row, 2)
    mate = hi * 2 + (1 - core)
    far = (1 - hi) * 2 + core
    far_mate = (1 - hi) * 2 + (1 - core)
    enter([(mate, col), (far, col)])
    n = direct_ref.shape[0]
    at = lambda r: pl.ds(pl.multiple_of(r * n, n), n)
    first = remote(back_ref.at[at(far_mate)], near.at[0], send.at[0], recv.at[0], (mate, col))
    first.start()
    second = remote(back_ref.at[at(mate)], near.at[1], send.at[1], recv.at[1], (mate, col))
    second.start()
    first.wait_recv()
    send_buf[...] = back_ref[at(far), :] + near[0]
    third = remote(send_buf, cross, send.at[2], recv.at[2], (far, col))
    third.start()
    second.wait_recv()
    total = direct_ref[...] + back_ref[at(row), :] + near[1]
    third.wait_recv()
    out_ref[...] = total + cross[...]
    first.wait_send()
    second.wait_send()
    third.wait_send()


def scatter_rows(back, direct):
    n = direct.shape[0]
    return pl.pallas_call(
        scatter_kernel,
        out_shape=jax.ShapeDtypeStruct((n, WIDTH), F32),
        in_specs=[VM, VM],
        out_specs=VM,
        scratch_shapes=[
            pltpu.VMEM((2, n, WIDTH), F32),
            pltpu.VMEM((n, WIDTH), F32),
            pltpu.VMEM((n, WIDTH), F32),
            DMA((3,)),
            DMA((3,)),
        ],
        compiler_params=pltpu.CompilerParams(collective_id=2, has_side_effects=True),
        name="scatter_rows",
    )(back, direct)


def body(x, ws, wn, bias, tile_values, tile_dest, tile_source, tile_count, cot):
    values = tile_values.reshape(SLOTS, TILE, TILE)
    dest, source, count = tile_dest.reshape(SLOTS), tile_source.reshape(SLOTS), tile_count.reshape(1)
    slab = gather_rows(x)
    part = forward_tiles(dest, source, count, slab, values)
    layer_out, direct, g, gw = exchange(part, x, ws, wn, bias, cot)
    back = backward_tiles(dest, source, count, g, values)
    grad_x = scatter_rows(back, direct)
    w = lambda i: jnp.concatenate([gw[i * WIDTH : (i + 1) * WIDTH], gw[(i + 1) * WIDTH : (i + 2) * WIDTH]], axis=1)
    grad_bias = gw[4 * WIDTH : 4 * WIDTH + 2].reshape(WIDTH)
    return layer_out, grad_x, w(0), w(2), grad_bias


def solution(mesh):
    in_specs = (
        P(("col", "row"), None),
        P(),
        P(),
        P(),
        P("row", "col", None, None, None),
        P("row", "col", None),
        P("row", "col", None),
        P("row", "col"),
        P(("col", "row"), None),
    )
    out_specs = (P(("col", "row"), None), P(("col", "row"), None), P(), P(), P())
    return jax.shard_map(body, mesh=mesh, in_specs=in_specs, out_specs=out_specs, check_vma=False)
```

```python
import functools

import jax
import jax.numpy as jnp
from jax import lax
from jax.experimental import pallas as pl
from jax.experimental.pallas import tpu as pltpu
from jax.sharding import PartitionSpec as P

EPSILON = 1e-05
F32 = jnp.float32
BF16 = jnp.bfloat16
MESH = pl.DeviceIdType.MESH
TILE = 128
WIDTH = 256
SLOTS = 192
DESTS = 64
SOURCES = 8
ROWS = 264
CHUNK = 16
CHUNKS = SLOTS // CHUNK
UNROLL = 16
VMEM_LIMIT = 60 * 1024 * 1024

VM = pl.BlockSpec(memory_space=pltpu.VMEM)
SM = pl.BlockSpec(memory_space=pltpu.SMEM)
ANY = pl.BlockSpec(memory_space=pl.ANY)
DMA = pltpu.SemaphoreType.DMA


def split(a):
    hi = a.astype(BF16)
    return hi, (a - hi.astype(F32)).astype(BF16)


def mm(a, b, dims=((1,), (0,))):
    return lax.dot_general(a, b, (dims, ((), ())), preferred_element_type=F32)


def dot3(a, b, dims=((1,), (0,))):
    ah, al = split(a)
    bh, bl = split(b)
    return mm(ah, bh, dims) + (mm(ah, bl, dims) + mm(al, bh, dims))


def enter(devices):
    barrier = pltpu.get_barrier_semaphore()
    for device in devices:
        pl.semaphore_signal(barrier, inc=1, device_id=device, device_id_type=MESH)
    pl.semaphore_wait(barrier, len(devices))


def remote(src, dst, send, recv, device):
    return pltpu.make_async_remote_copy(
        src_ref=src, dst_ref=dst, send_sem=send, recv_sem=recv, device_id=device, device_id_type=MESH
    )


def gather_kernel(x_ref, out_ref, local_sem, send, recv):
    row, col = lax.axis_index("row"), lax.axis_index("col")
    hi, core = lax.div(row, 2), lax.rem(row, 2)
    mate = hi * 2 + (1 - core)
    far = (1 - hi) * 2 + core
    far_mate = (1 - hi) * 2 + (1 - core)
    enter([(mate, col), (far, col)])
    n = x_ref.shape[0]
    at = lambda r: out_ref.at[pl.ds(pl.multiple_of(r * n, n), n)]
    own = pltpu.make_async_copy(x_ref, at(row), local_sem)
    own.start()
    across = remote(x_ref, at(row), send.at[0], recv.at[0], (far, col))
    across.start()
    beside = remote(x_ref, at(row), send.at[1], recv.at[1], (mate, col))
    beside.start()
    across.wait_recv()
    onward = remote(at(far), at(far), send.at[2], recv.at[2], (mate, col))
    onward.start()
    beside.wait_recv()
    onward.wait_recv()
    own.wait()
    across.wait_send()
    beside.wait_send()
    onward.wait_send()


def gather_rows(x):
    return pl.pallas_call(
        gather_kernel,
        out_shape=jax.ShapeDtypeStruct((4 * x.shape[0], x.shape[1]), F32),
        in_specs=[VM],
        out_specs=VM,
        scratch_shapes=[DMA, DMA((3,)), DMA((3,))],
        compiler_params=pltpu.CompilerParams(collective_id=0, has_side_effects=True),
        name="gather_rows",
    )(x)


def tile_copy(tiles_hbm, tiles, sems, c):
    at = pl.ds(c * CHUNK, CHUNK)
    return pltpu.make_async_copy(tiles_hbm.at[at], tiles.at[at], sems.at[c])


def forward_kernel(dest, source, count, x_ref, tiles_hbm, out_hbm, tiles, acc, total, xhh, xlo, sems, out_sem):
    for c in range(CHUNKS):
        tile_copy(tiles_hbm, tiles, sems, c).start()
    live = count[0]
    for s in range(SOURCES):
        hi, lo = split(x_ref[s * TILE : (s + 1) * TILE, :])
        xhh[s, 0:TILE, :] = hi
        xhh[s, TILE:, :] = hi
        xlo[s] = lo

    def clear(d, _):
        acc[d] = jnp.zeros((ROWS, TILE), F32)
        total[d] = jnp.zeros((TILE, TILE), F32)
        return 0

    lax.fori_loop(0, DESTS + 1, clear, 0)

    def one(t):
        s = source[t]
        d = jnp.where(t < live, dest[t], DESTS)
        a = tiles[t]
        hi, lo = split(a)
        p = mm(jnp.concatenate([hi, lo], axis=1), xhh[s]) + mm(hi, xlo[s])
        acc[d, 0:TILE, :] += p[:, 0:TILE]
        acc[d, TILE : 2 * TILE, :] += p[:, TILE:]
        total[d] += a

    def group(g, _):
        for u in range(UNROLL):
            one(g * UNROLL + u)
        return 0

    def chunk(c, _):
        tile_copy(tiles_hbm, tiles, sems, c).wait()
        per = CHUNK // UNROLL
        return lax.fori_loop(c * per, (c + 1) * per, group, 0)

    lax.fori_loop(0, CHUNKS, chunk, 0)
    ones = jnp.ones((8, 2 * TILE), BF16)

    def degrees(g, _):
        for u in range(4):
            d = g * 4 + u
            hi, lo = split(total[d])
            acc[d, 2 * TILE :, :] = mm(ones, jnp.concatenate([hi, lo], axis=1), ((1,), (1,)))
        return 0

    lax.fori_loop(0, DESTS // 4, degrees, 0)
    out = pltpu.make_async_copy(acc.at[pl.ds(0, DESTS)], out_hbm, out_sem)
    out.start()
    out.wait()


def forward_tiles(dest, source, count, slab, values):
    return pl.pallas_call(
        forward_kernel,
        out_shape=jax.ShapeDtypeStruct((DESTS, ROWS, TILE), F32),
        in_specs=[SM, SM, SM, VM, ANY],
        out_specs=ANY,
        scratch_shapes=[
            pltpu.VMEM((SLOTS, TILE, TILE), F32),
            pltpu.VMEM((DESTS + 1, ROWS, TILE), F32),
            pltpu.VMEM((DESTS + 1, TILE, TILE), F32),
            pltpu.VMEM((SOURCES, 2 * TILE, WIDTH), BF16),
            pltpu.VMEM((SOURCES, TILE, WIDTH), BF16),
            DMA((CHUNKS,)),
            DMA,
        ],
        compiler_params=pltpu.CompilerParams(vmem_limit_bytes=VMEM_LIMIT),
        cost_estimate=pl.CostEstimate(
            flops=SLOTS * 6 * TILE * TILE * WIDTH, bytes_accessed=22_000_000, transcendentals=0
        ),
        name="forward_tiles",
    )(dest, source, count, slab, values)


def rms_silu(pre, cot):
    sig = 1.0 / (1.0 + jnp.exp(-pre))
    s = pre * sig
    r = lax.rsqrt(jnp.mean(s * s, axis=-1, keepdims=True) + EPSILON)
    inner = jnp.mean(cot * s, axis=-1, keepdims=True)
    ds = r * cot - s * (r * r * r * inner)
    return s * r, ds * sig * (1.0 + pre * (1.0 - sig))


PARTS = 32
PART_ROWS = 40
AR_SENDS = 17
FIRST = 64
SUM_ROWS = (((0, 136), (136, 128)), ((FIRST, 104), (FIRST + 104, 96)))
GATH_ROWS = (((0, 128), (128, 128)), ((FIRST, 96), (FIRST + 96, 96)))
SLICES = 20


def exchange_kernel(
    part_hbm, x_ref, ws_ref, wn_ref, bias_ref, cot_ref,
    layer_out, direct_out, g_out, gw_out,
    acc, relays, arrivals, zfirst, zlast, gath, own_term, gwp, gws, r1, r2, r3, r4, own_part,
    load_sem, rs_send, rs_recv, zs_send, zs_recv, ag_send, ag_recv, zg_send, zg_recv, ar_send, ar_recv, out_sem,
):
    row, col = lax.axis_index("row"), lax.axis_index("col")
    zh, core = lax.div(row, 2), lax.rem(row, 2)
    x, y, z = lax.div(col, 8), lax.rem(lax.div(col, 2), 4), lax.rem(col, 2)
    column = lambda xx, yy, zz: xx * 8 + yy * 2 + zz
    ahead = lambda p, d: lax.rem(p + d, 4)
    x_others = [(row, column(ahead(x, d), y, z)) for d in range(1, 4)]
    y_others = [(row, column(x, ahead(y, d), z)) for d in range(1, 4)]
    z_mate = (row, column(x, y, 1 - z))
    core_mate = (zh * 2 + (1 - core), col)
    far = (1 - zh) * 2 + core
    z_others = [z_mate, (far, col), (far, column(x, y, 1 - z))]
    zs = (z, 1 - z)

    def index(order, wide, narrow, mine):
        xx, yy = (wide, narrow) if order == 0 else (narrow, wide)
        return (xx, yy, zs[mine], order)

    def at_place(order, w, which, mine, j):
        p, q = (x, y) if order == 0 else (y, x)
        return index(order, ahead(p, j), ahead(q, which), mine) if w == 0 else index(order, p, ahead(q, j), mine)

    def ring(order, w):
        others = x_others if order == w else y_others
        return others[0], others[2]

    def number(order, w, which, mine):
        return (order * 2 + mine) * 5 + (which if w == 0 else 4)

    class Sum:
        def __init__(self, order, w, which, mine):
            self.n = number(order, w, which, mine)
            self.blk = lambda j: at_place(order, w, which, mine, j % 4)
            self.top, self.low = SUM_ROWS[mine]
            up, down = ring(order, w)
            self.copies = []
            for i, (j, rows, to, device) in enumerate(
                (
                    (2, self.top, relays.at[self.n, 0, pl.ds(0, self.top[1])], up),
                    (2, self.low, relays.at[self.n, 1, pl.ds(0, self.low[1])], down),
                    (1, self.low, arrivals.at[self.n, 0, pl.ds(*self.low)], up),
                    (3, self.top, arrivals.at[self.n, 1, pl.ds(*self.top)], down),
                    (1, self.top, arrivals.at[self.n, 0, pl.ds(*self.top)], up),
                    (3, self.low, arrivals.at[self.n, 1, pl.ds(*self.low)], down),
                )
            ):
                src = acc.at[(*self.blk(j), pl.ds(*rows))]
                self.copies.append(remote(src, to, rs_send.at[self.n, i], rs_recv.at[self.n, i], device))

        def issue(self):
            for c in self.copies[:4]:
                c.start()

        def relay(self):
            for i, (j, rows) in enumerate(((1, self.top), (3, self.low))):
                self.copies[i].wait_recv()
                at = (*self.blk(j), pl.ds(*rows), slice(None))
                acc[at] += relays[self.n, i, 0 : rows[1], :]
                self.copies[4 + i].start()

        def finish(self):
            for c in self.copies[2:]:
                c.wait_recv()
            rows = pl.ds(self.top[0], self.top[1] + self.low[1])
            at = (*self.blk(0), rows, slice(None))
            acc[at] += arrivals[self.n, 0, rows, :] + arrivals[self.n, 1, rows, :]

        def drain(self):
            for c in self.copies:
                c.wait_send()

    class Gather:
        def __init__(self, order, w, which, mine):
            n = number(order, w, which, mine)
            blk = lambda j: at_place(order, w, which, mine, j % 4)
            top, low = GATH_ROWS[mine]
            up, down = ring(order, w)
            self.out, self.come = [], []
            for i, (leaves, comes, rows, device) in enumerate(
                (
                    (0, 3, top, up),
                    (0, 1, low, down),
                    (0, 3, low, up),
                    (0, 1, top, down),
                    (3, 2, top, up),
                    (1, 2, low, down),
                )
            ):
                for j, kept in ((leaves, self.out), (comes, self.come)):
                    ref = gath.at[(*blk(j), pl.ds(*rows))]
                    kept.append(remote(ref, ref, ag_send.at[n, i], ag_recv.at[n, i], device))

        def issue(self):
            for c in self.out[:4]:
                c.start()

        def relay(self):
            for i in range(2):
                self.come[i].wait_recv()
                self.out[4 + i].start()

        def near(self):
            for c in self.come[2:4]:
                c.wait_recv()

        def finish(self):
            for c in self.come[4:]:
                c.wait_recv()

        def drain(self):
            for c in self.out:
                c.wait_send()

    def strip(ref, order, which, mine, rows=None):
        q = ahead(y if order == 0 else x, which)
        lead = (slice(None), q) if order == 0 else (q, slice(None))
        return ref.at[(*lead, zs[mine], order) + (() if rows is None else (pl.ds(*rows),))]

    def load(order, which, mine):
        n = order * 8 + mine * 4 + which
        return pltpu.make_async_copy(strip(part_hbm, order, which, mine), strip(acc, order, which, mine), load_sem.at[n])

    def z_first(order, which):
        to = zfirst.at[order, which]
        i = order * 4 + which
        return remote(strip(part_hbm, order, which, 1, (0, FIRST)), to, zs_send.at[i], zs_recv.at[i], z_mate)

    def z_last(order):
        rows = pl.ds(FIRST, ROWS - FIRST)
        src = acc.at[(*at_place(order, 0, 0, 1, 0), rows)]
        return remote(src, zlast.at[order, rows], zs_send.at[8 + order], zs_recv.at[8 + order], z_mate)

    turn = [(which, 1) for which in (2, 1, 3, 0)] + [(which, 0) for which in (2, 1, 3, 0)]
    for which, mine in turn:
        for order in range(2):
            load(order, which, mine).start()
    enter([core_mate] + x_others + y_others + z_others)
    for which in (2, 1, 3, 0):
        for order in range(2):
            z_first(order, which).start()

    wide = [[Sum(order, 0, which, mine) for order in range(2)] for which, mine in turn]
    narrow = [[Sum(order, 1, 0, mine) for order in range(2)] for mine in range(2)]

    def each(pair, action):
        for s in pair:
            getattr(s, action)()

    def sum_issue(i):
        which, mine = turn[i]
        for order in range(2):
            load(order, which, mine).wait()
            if mine == 0:
                z_first(order, which).wait_recv()
                p = y if order == 0 else x
                for j in range(4):
                    at = (*index(order, j, ahead(p, which), 0), pl.ds(0, FIRST), slice(None))
                    acc[at] += zfirst[order, which, j]
            wide[i][order].issue()

    for i in range(len(turn) + 3):
        if i < len(turn):
            sum_issue(i)
        if i == 0:
            own_term[...] = dot3(x_ref[...], ws_ref[...])
        if 1 <= i <= len(turn):
            each(wide[i - 1], "relay")
        if i == 5:
            each(narrow[1], "relay")
        if i == 9:
            each(narrow[0], "relay")
        if 2 <= i <= len(turn) + 1:
            each(wide[i - 2], "finish")
        if i == 4:
            each(narrow[1], "issue")
        if i == 8:
            each(narrow[0], "issue")
        if i == 6:
            each(narrow[1], "finish")
            for order in range(2):
                z_last(order).start()
        if i == 10:
            each(narrow[0], "finish")

    x_own = x_ref[...]
    ws, wn = ws_ref[...], wn_ref[...]
    sums, inv = [], []
    for order in range(2):
        z_last(order).wait_recv()
        own = at_place(order, 0, 0, 0, 0)
        s = jnp.concatenate([acc[(*own, pl.ds(0, FIRST))], acc[(*own, pl.ds(FIRST, ROWS - FIRST))] + zlast[order, FIRST:, :]], axis=0)
        degree = jnp.transpose(jnp.broadcast_to(s[2 * TILE : 2 * TILE + 1, :], (TILE, TILE)))
        root = lax.rsqrt(1.0 + degree)
        inv.append(jnp.concatenate([root, root], axis=1))
        sums.append(jnp.concatenate([s[0:TILE], s[TILE : 2 * TILE]], axis=1))
    inv = jnp.concatenate(inv, axis=0)
    neighbour = jnp.concatenate(sums, axis=0) * inv
    pre = own_term[...] + dot3(neighbour, wn) + bias_ref[...]
    out, grad_pre = rms_silu(pre, cot_ref[...])
    layer_out[...] = out
    spread = dot3(grad_pre, wn, ((1,), (1,))) * inv
    for order in range(2):
        for half in range(2):
            gath[(*at_place(order, 0, 0, 0, 0), pl.ds(half * TILE, TILE), slice(None))] = spread[
                order * TILE : (order + 1) * TILE, half * TILE : (half + 1) * TILE
            ]

    def give(order, mine):
        ref = gath.at[(*at_place(order, 0, 0, mine, 0), pl.ds(FIRST, 2 * TILE - FIRST))]
        return remote(ref, ref, zg_send.at[8 + order], zg_recv.at[8 + order], z_mate)

    def z_after(order, which, mine):
        ref = strip(gath, order, which, mine, (0, FIRST))
        i = order * 4 + which
        return remote(ref, ref, zg_send.at[i], zg_recv.at[i], z_mate)

    def write(order, which, mine):
        n = order * 8 + mine * 4 + which
        return pltpu.make_async_copy(strip(gath, order, which, mine), strip(g_out, order, which, mine), out_sem.at[n])

    gwide = {(which, mine): [Gather(order, 0, which, mine) for order in range(2)] for which in range(4) for mine in range(2)}
    gnarrow = [[Gather(order, 1, 0, mine) for order in range(2)] for mine in range(2)]

    def done(which, mine):
        each(gwide[which, mine], "near")
        each(gwide[which, mine], "finish")
        for order in range(2):
            if mine == 0:
                z_after(order, which, 0).start()
                write(order, which, 0).start()

    for order in range(2):
        give(order, 0).start()
    each(gnarrow[0], "issue")
    each(gwide[0, 0], "issue")

    gs = dot3(x_own, grad_pre, ((0,), (0,)))
    gn = dot3(neighbour, grad_pre, ((0,), (0,)))
    flat = [gs[:, 0:TILE], gs[:, TILE:], gn[:, 0:TILE], gn[:, TILE:]]
    gb = jnp.sum(grad_pre, axis=0, keepdims=True)
    gwp[...] = jnp.zeros_like(gwp)
    for i, f in enumerate(flat):
        gwp[i * WIDTH : (i + 1) * WIDTH, :] = f
    gwp[4 * WIDTH : 4 * WIDTH + 1, :] = gb[:, 0:TILE]
    gwp[4 * WIDTH + 1 : 4 * WIDTH + 2, :] = gb[:, TILE:]

    n_core, n_x, n_y = 16 * PART_ROWS, 4 * PART_ROWS, PART_ROWS
    rows_at = lambda c, xx, yy, n: pl.ds(pl.multiple_of((c * 16 + xx * 4 + yy) * PART_ROWS, 8), n)
    span = lambda *at: gwp.at[rows_at(*at)]
    summed = lambda *at: gws.at[rows_at(*at)]
    hop = lambda i, src, dst, device: remote(src, dst, ar_send.at[i], ar_recv.at[i], device)

    c1 = [hop(0, span(1 - core, 0, 0, n_core), r1, core_mate)]
    c2 = [hop(d, span(core, ahead(x, d), 0, n_x), r2.at[d - 1], x_others[d - 1]) for d in range(1, 4)]
    c3 = [hop(3 + d, span(core, x, ahead(y, d), n_y), r3.at[d - 1], y_others[d - 1]) for d in range(1, 4)]
    c4 = [hop(7 + d, own_part, r4.at[d], z_others[d]) for d in range(3)]
    mine = summed(core, x, y, n_y)
    c5 = [hop(9 + d, mine, mine, y_others[d - 1]) for d in range(1, 4)]
    mine_x = summed(core, x, 0, n_x)
    c6 = [hop(12 + d, mine_x, mine_x, x_others[d - 1]) for d in range(1, 4)]
    mine_c = summed(core, 0, 0, n_core)
    c7 = [hop(16, mine_c, mine_c, core_mate)]

    def launch(copies):
        for c in copies:
            c.start()

    def land(copies):
        for c in copies:
            c.wait()

    def add_parts(at, terms):
        v = gwp[at, :]
        for term in terms:
            v = v + term
        gwp[at, :] = v

    def phase1():
        land(c1)
        add_parts(rows_at(core, 0, 0, n_core), [r1[...]])
        launch(c2)

    def phase2():
        land(c2)
        add_parts(rows_at(core, x, 0, n_x), [r2[d] for d in range(3)])
        launch(c3)

    def phase3():
        land(c3)
        own_part[...] = gwp[rows_at(core, x, y, n_y), :] + r3[0] + r3[1] + r3[2]
        launch(c4)

    def phase4():
        land(c4)
        gws[rows_at(core, x, y, n_y), :] = (own_part[...] + r4[0]) + (r4[1] + r4[2])
        launch(c5)

    def phase5():
        for d in range(1, 4):
            peer = summed(core, x, ahead(y, 4 - d), n_y)
            hop(9 + d, peer, peer, y_others[d - 1]).wait_recv()
        launch(c6)

    def phase6():
        for d in range(1, 4):
            peer = summed(core, ahead(x, 4 - d), 0, n_x)
            hop(12 + d, peer, peer, x_others[d - 1]).wait_recv()
        launch(c7)

    def phase7():
        peer = summed(1 - core, 0, 0, n_core)
        hop(16, peer, peer, core_mate).wait_recv()
        gw_out[...] = gws[0 : 4 * WIDTH + 8, :]

    launch(c1)
    direct_out[...] = dot3(grad_pre, ws, ((1,), (1,)))

    each(gnarrow[0], "relay")
    each(gwide[0, 0], "relay")
    each(gnarrow[0], "near")
    each(gwide[1, 0], "issue")
    phase1()
    for order in range(2):
        give(order, 1).wait_recv()
    each(gnarrow[1], "issue")
    each(gwide[3, 0], "issue")
    each(gwide[1, 0], "relay")
    done(0, 0)
    phase2()
    each(gnarrow[1], "relay")
    each(gnarrow[0], "finish")
    each(gwide[2, 0], "issue")
    each(gwide[3, 0], "relay")
    done(1, 0)
    phase3()
    each(gwide[0, 1], "issue")
    each(gwide[2, 0], "relay")
    done(3, 0)
    each(gnarrow[1], "near")
    phase4()
    each(gwide[1, 1], "issue")
    each(gwide[0, 1], "relay")
    done(2, 0)
    each(gnarrow[1], "finish")
    phase5()
    each(gwide[3, 1], "issue")
    each(gwide[1, 1], "relay")
    done(0, 1)
    phase6()
    each(gwide[2, 1], "issue")
    each(gwide[3, 1], "relay")
    done(1, 1)
    phase7()
    each(gwide[2, 1], "relay")
    done(3, 1)
    for which in (0, 1, 3):
        for order in range(2):
            z_after(order, which, 1).wait_recv()
            write(order, which, 1).start()
    done(2, 1)
    for order in range(2):
        z_after(order, 2, 1).wait_recv()
        write(order, 2, 1).start()

    for pair in wide + narrow + list(gwide.values()) + gnarrow:
        each(pair, "drain")
    for order in range(2):
        z_last(order).wait_send()
        give(order, 0).wait_send()
        for which in range(4):
            z_first(order, which).wait_send()
            z_after(order, which, 0).wait_send()
    for copies in (c5, c6, c7):
        for c in copies:
            c.wait_send()
    for which in range(4):
        for order in range(2):
            for own_z in range(2):
                write(order, which, own_z).wait()


def exchange(part, x, ws, wn, bias, cot):
    n = x.shape[0]
    layout = (4, 4, 2, 2)
    out = pl.pallas_call(
        exchange_kernel,
        out_shape=(
            jax.ShapeDtypeStruct((n, WIDTH), F32),
            jax.ShapeDtypeStruct((n, WIDTH), F32),
            jax.ShapeDtypeStruct((*layout, 2 * TILE, TILE), F32),
            jax.ShapeDtypeStruct((4 * WIDTH + 8, TILE), F32),
        ),
        in_specs=[ANY, VM, VM, VM, VM, VM],
        out_specs=(VM, VM, ANY, VM),
        scratch_shapes=[
            pltpu.VMEM((*layout, ROWS, TILE), F32),
            pltpu.VMEM((SLICES, 2, 136, TILE), F32),
            pltpu.VMEM((SLICES, 2, ROWS, TILE), F32),
            pltpu.VMEM((2, 4, 4, FIRST, TILE), F32),
            pltpu.VMEM((2, ROWS, TILE), F32),
            pltpu.VMEM((*layout, 2 * TILE, TILE), F32),
            pltpu.VMEM((n, WIDTH), F32),
            pltpu.VMEM((PARTS * PART_ROWS, TILE), F32),
            pltpu.VMEM((PARTS * PART_ROWS, TILE), F32),
            pltpu.VMEM((16 * PART_ROWS, TILE), F32),
            pltpu.VMEM((3, 4 * PART_ROWS, TILE), F32),
            pltpu.VMEM((3, PART_ROWS, TILE), F32),
            pltpu.VMEM((3, PART_ROWS, TILE), F32),
            pltpu.VMEM((PART_ROWS, TILE), F32),
            DMA((16,)),
            DMA((SLICES, 6)),
            DMA((SLICES, 6)),
            DMA((10,)),
            DMA((10,)),
            DMA((SLICES, 6)),
            DMA((SLICES, 6)),
            DMA((10,)),
            DMA((10,)),
            DMA((AR_SENDS,)),
            DMA((AR_SENDS,)),
            DMA((16,)),
        ],
        compiler_params=pltpu.CompilerParams(
            collective_id=1, has_side_effects=True, vmem_limit_bytes=VMEM_LIMIT
        ),
        name="exchange",
    )(part.reshape(*layout, ROWS, TILE), x, ws, wn, bias.reshape(1, WIDTH), cot)
    layer_out, direct, g, gw = out
    return layer_out, direct, g.reshape(DESTS, 2 * TILE, TILE), gw


def backward_kernel(dest, source, count, g_hbm, tiles_hbm, out_ref, tiles, g, ghh, glo, acc, sems, g_sem):
    g_copy = pltpu.make_async_copy(g_hbm, g, g_sem)
    g_copy.start()
    for c in range(CHUNKS):
        tile_copy(tiles_hbm, tiles, sems, c).start()
    live = count[0]

    def clear(s, _):
        acc[s] = jnp.zeros((TILE, WIDTH), F32)
        return 0

    lax.fori_loop(0, SOURCES + 1, clear, 0)
    g_copy.wait()

    def cut(d, _):
        for half in range(2):
            hi, lo = split(g[d, half * TILE : (half + 1) * TILE, :])
            lanes = slice(half * TILE, (half + 1) * TILE)
            ghh[d, 0:TILE, lanes] = hi
            ghh[d, TILE:, lanes] = hi
            glo[d, :, lanes] = lo
        return 0

    lax.fori_loop(0, DESTS, cut, 0)

    def one(t):
        d = dest[t]
        s = jnp.where(t < live, source[t], SOURCES)
        hi, lo = split(tiles[t])
        p = mm(jnp.concatenate([hi, lo], axis=0), ghh[d], ((0,), (0,))) + mm(hi, glo[d], ((0,), (0,)))
        acc[s] += p

    def group(g_, _):
        for u in range(UNROLL):
            one(g_ * UNROLL + u)
        return 0

    def chunk(c, _):
        tile_copy(tiles_hbm, tiles, sems, c).wait()
        per = CHUNK // UNROLL
        return lax.fori_loop(c * per, (c + 1) * per, group, 0)

    lax.fori_loop(0, CHUNKS, chunk, 0)
    for s in range(SOURCES):
        out_ref[s * TILE : (s + 1) * TILE, :] = acc[s]


def backward_tiles(dest, source, count, g, values):
    return pl.pallas_call(
        backward_kernel,
        out_shape=jax.ShapeDtypeStruct((SOURCES * TILE, WIDTH), F32),
        in_specs=[SM, SM, SM, ANY, ANY],
        out_specs=VM,
        scratch_shapes=[
            pltpu.VMEM((SLOTS, TILE, TILE), F32),
            pltpu.VMEM((DESTS, 2 * TILE, TILE), F32),
            pltpu.VMEM((DESTS, 2 * TILE, WIDTH), BF16),
            pltpu.VMEM((DESTS, TILE, WIDTH), BF16),
            pltpu.VMEM((SOURCES + 1, TILE, WIDTH), F32),
            DMA((CHUNKS,)),
            DMA,
        ],
        compiler_params=pltpu.CompilerParams(vmem_limit_bytes=VMEM_LIMIT),
        cost_estimate=pl.CostEstimate(
            flops=SLOTS * 6 * TILE * TILE * WIDTH, bytes_accessed=22_000_000, transcendentals=0
        ),
        name="backward_tiles",
    )(dest, source, count, g, values)


def scatter_kernel(back_ref, direct_ref, out_ref, near, cross, send_buf, send, recv):
    row, col = lax.axis_index("row"), lax.axis_index("col")
    hi, core = lax.div(row, 2), lax.rem(row, 2)
    mate = hi * 2 + (1 - core)
    far = (1 - hi) * 2 + core
    far_mate = (1 - hi) * 2 + (1 - core)
    enter([(mate, col), (far, col)])
    n = direct_ref.shape[0]
    at = lambda r: pl.ds(pl.multiple_of(r * n, n), n)
    first = remote(back_ref.at[at(far_mate)], near.at[0], send.at[0], recv.at[0], (mate, col))
    first.start()
    second = remote(back_ref.at[at(mate)], near.at[1], send.at[1], recv.at[1], (mate, col))
    second.start()
    first.wait_recv()
    send_buf[...] = back_ref[at(far), :] + near[0]
    third = remote(send_buf, cross, send.at[2], recv.at[2], (far, col))
    third.start()
    second.wait_recv()
    total = direct_ref[...] + back_ref[at(row), :] + near[1]
    third.wait_recv()
    out_ref[...] = total + cross[...]
    first.wait_send()
    second.wait_send()
    third.wait_send()


def scatter_rows(back, direct):
    n = direct.shape[0]
    return pl.pallas_call(
        scatter_kernel,
        out_shape=jax.ShapeDtypeStruct((n, WIDTH), F32),
        in_specs=[VM, VM],
        out_specs=VM,
        scratch_shapes=[
            pltpu.VMEM((2, n, WIDTH), F32),
            pltpu.VMEM((n, WIDTH), F32),
            pltpu.VMEM((n, WIDTH), F32),
            DMA((3,)),
            DMA((3,)),
        ],
        compiler_params=pltpu.CompilerParams(collective_id=2, has_side_effects=True),
        name="scatter_rows",
    )(back, direct)


def body(x, ws, wn, bias, tile_values, tile_dest, tile_source, tile_count, cot):
    values = tile_values.reshape(SLOTS, TILE, TILE)
    dest, source, count = tile_dest.reshape(SLOTS), tile_source.reshape(SLOTS), tile_count.reshape(1)
    slab = gather_rows(x)
    part = forward_tiles(dest, source, count, slab, values)
    layer_out, direct, g, gw = exchange(part, x, ws, wn, bias, cot)
    back = backward_tiles(dest, source, count, g, values)
    grad_x = scatter_rows(back, direct)
    w = lambda i: jnp.concatenate([gw[i * WIDTH : (i + 1) * WIDTH], gw[(i + 1) * WIDTH : (i + 2) * WIDTH]], axis=1)
    grad_bias = gw[4 * WIDTH : 4 * WIDTH + 2].reshape(WIDTH)
    return layer_out, grad_x, w(0), w(2), grad_bias


def solution(mesh):
    in_specs = (
        P(("col", "row"), None),
        P(),
        P(),
        P(),
        P("row", "col", None, None, None),
        P("row", "col", None),
        P("row", "col", None),
        P("row", "col"),
        P(("col", "row"), None),
    )
    out_specs = (P(("col", "row"), None), P(("col", "row"), None), P(), P(), P())
    return jax.shard_map(body, mesh=mesh, in_specs=in_specs, out_specs=out_specs, check_vma=False)
```

```python
import functools

import jax
import jax.numpy as jnp
from jax import lax
from jax.experimental import pallas as pl
from jax.experimental.pallas import tpu as pltpu
from jax.sharding import PartitionSpec as P

EPSILON = 1e-05
F32 = jnp.float32
BF16 = jnp.bfloat16
MESH = pl.DeviceIdType.MESH
TILE = 128
WIDTH = 256
SLOTS = 192
DESTS = 64
SOURCES = 8
ROWS = 264
CHUNK = 16
CHUNKS = SLOTS // CHUNK
UNROLL = 16
PIECES = 4
VMEM_LIMIT = 60 * 1024 * 1024

VM = pl.BlockSpec(memory_space=pltpu.VMEM)
SM = pl.BlockSpec(memory_space=pltpu.SMEM)
ANY = pl.BlockSpec(memory_space=pl.ANY)
DMA = pltpu.SemaphoreType.DMA


def split(a):
    hi = a.astype(BF16)
    return hi, (a - hi.astype(F32)).astype(BF16)


def mm(a, b, dims=((1,), (0,))):
    return lax.dot_general(a, b, (dims, ((), ())), preferred_element_type=F32)


def dot3(a, b, dims=((1,), (0,))):
    ah, al = split(a)
    bh, bl = split(b)
    return mm(ah, bh, dims) + (mm(ah, bl, dims) + mm(al, bh, dims))


def enter(devices):
    barrier = pltpu.get_barrier_semaphore()
    for device in devices:
        pl.semaphore_signal(barrier, inc=1, device_id=device, device_id_type=MESH)
    pl.semaphore_wait(barrier, len(devices))


def remote(src, dst, send, recv, device):
    return pltpu.make_async_remote_copy(
        src_ref=src, dst_ref=dst, send_sem=send, recv_sem=recv, device_id=device, device_id_type=MESH
    )


def gather_kernel(x_ref, out_ref, local_sem, send, recv):
    row, col = lax.axis_index("row"), lax.axis_index("col")
    hi, core = lax.div(row, 2), lax.rem(row, 2)
    mate = hi * 2 + (1 - core)
    far = (1 - hi) * 2 + core
    enter([(mate, col), (far, col)])
    n = x_ref.shape[0]
    m = n // PIECES
    at = lambda r, c: out_ref.at[pl.ds(pl.multiple_of(r * n + c * m, m), m)]
    piece = lambda c: x_ref.at[pl.ds(c * m, m)]
    own = pltpu.make_async_copy(x_ref, out_ref.at[pl.ds(pl.multiple_of(row * n, n), n)], local_sem)
    across = [remote(piece(c), at(row, c), send.at[0, c], recv.at[0, c], (far, col)) for c in range(PIECES)]
    beside = [remote(piece(c), at(row, c), send.at[1, c], recv.at[1, c], (mate, col)) for c in range(PIECES)]
    onward = [remote(at(far, c), at(far, c), send.at[2, c], recv.at[2, c], (mate, col)) for c in range(PIECES)]
    for c in across + beside:
        c.start()
    own.start()
    for c in range(PIECES):
        across[c].wait_recv()
        onward[c].start()
    for c in beside + onward:
        c.wait_recv()
    own.wait()
    for c in across + beside + onward:
        c.wait_send()


def gather_rows(x):
    return pl.pallas_call(
        gather_kernel,
        out_shape=jax.ShapeDtypeStruct((4 * x.shape[0], x.shape[1]), F32),
        in_specs=[VM],
        out_specs=VM,
        scratch_shapes=[DMA, DMA((3, PIECES)), DMA((3, PIECES))],
        compiler_params=pltpu.CompilerParams(collective_id=0, has_side_effects=True),
        name="gather_rows",
    )(x)


def tile_copy(tiles_hbm, tiles, sems, c):
    at = pl.ds(c * CHUNK, CHUNK)
    return pltpu.make_async_copy(tiles_hbm.at[at], tiles.at[at], sems.at[c])


def forward_kernel(dest, source, count, x_ref, tiles_hbm, out_hbm, tiles, acc, total, xs, sems, out_sem):
    for c in range(CHUNKS):
        tile_copy(tiles_hbm, tiles, sems, c).start()
    live = count[0]
    for s in range(SOURCES):
        hi, lo = split(x_ref[s * TILE : (s + 1) * TILE, :])
        xs[s, 0:TILE, :] = hi
        xs[s, TILE : 2 * TILE, :] = hi
        xs[s, 2 * TILE :, :] = lo

    def clear(d, _):
        acc[d] = jnp.zeros((ROWS, TILE), F32)
        total[d] = jnp.zeros((TILE, TILE), F32)
        return 0

    lax.fori_loop(0, DESTS + 1, clear, 0)

    def one(t):
        s = source[t]
        d = jnp.where(t < live, dest[t], DESTS)
        a = tiles[t]
        hi, lo = split(a)
        p = mm(jnp.concatenate([hi, lo, hi], axis=1), xs[s])
        acc[d, 0:TILE, :] += p[:, 0:TILE]
        acc[d, TILE : 2 * TILE, :] += p[:, TILE:]
        total[d] += a

    def group(g, _):
        for u in range(UNROLL):
            one(g * UNROLL + u)
        return 0

    def chunk(c, _):
        tile_copy(tiles_hbm, tiles, sems, c).wait()
        per = CHUNK // UNROLL
        return lax.fori_loop(c * per, (c + 1) * per, group, 0)

    lax.fori_loop(0, CHUNKS, chunk, 0)
    ones = jnp.ones((8, 2 * TILE), BF16)
    per = DESTS // 8

    def write(g):
        at = pl.ds(g * per, per)
        return pltpu.make_async_copy(acc.at[at], out_hbm.at[at], out_sem.at[g])

    def degrees(g, _):
        for u in range(per):
            d = g * per + u
            hi, lo = split(total[d])
            acc[d, 2 * TILE :, :] = mm(ones, jnp.concatenate([hi, lo], axis=1), ((1,), (1,)))
        write(g).start()
        return 0

    lax.fori_loop(0, 8, degrees, 0)
    for g in range(8):
        write(g).wait()


def forward_tiles(dest, source, count, slab, values):
    return pl.pallas_call(
        forward_kernel,
        out_shape=jax.ShapeDtypeStruct((DESTS, ROWS, TILE), F32),
        in_specs=[SM, SM, SM, VM, ANY],
        out_specs=ANY,
        scratch_shapes=[
            pltpu.VMEM((SLOTS, TILE, TILE), F32),
            pltpu.VMEM((DESTS + 1, ROWS, TILE), F32),
            pltpu.VMEM((DESTS + 1, TILE, TILE), F32),
            pltpu.VMEM((SOURCES, 3 * TILE, WIDTH), BF16),
            DMA((CHUNKS,)),
            DMA((8,)),
        ],
        compiler_params=pltpu.CompilerParams(vmem_limit_bytes=VMEM_LIMIT),
        cost_estimate=pl.CostEstimate(
            flops=SLOTS * 6 * TILE * TILE * WIDTH, bytes_accessed=22_000_000, transcendentals=0
        ),
        name="forward_tiles",
    )(dest, source, count, slab, values)


def rms_silu(pre, cot):
    sig = 1.0 / (1.0 + jnp.exp(-pre))
    s = pre * sig
    r = lax.rsqrt(jnp.mean(s * s, axis=-1, keepdims=True) + EPSILON)
    inner = jnp.mean(cot * s, axis=-1, keepdims=True)
    ds = r * cot - s * (r * r * r * inner)
    return s * r, ds * sig * (1.0 + pre * (1.0 - sig))


PARTS = 32
PART_ROWS = 40
AR_SENDS = 10
FIRST = 64
SUM_ROWS = (((0, 136), (136, 128)), ((FIRST, 104), (FIRST + 104, 96)))
GATH_ROWS = (((0, 128), (128, 128)), ((FIRST, 96), (FIRST + 96, 96)))
SLICES = 20


def exchange_kernel(
    part_hbm, x_ref, ws_ref, wn_ref, bias_ref, cot_ref,
    layer_out, direct_out, g_out, gw_out,
    acc, relays, arrivals, zfirst, zlast, gath, own_term, gwp, r1, r2, r3, r4, own_part,
    load_sem, rs_send, rs_recv, zs_send, zs_recv, ag_send, ag_recv, zg_send, zg_recv, ar_send, ar_recv, out_sem,
):
    row, col = lax.axis_index("row"), lax.axis_index("col")
    zh, core = lax.div(row, 2), lax.rem(row, 2)
    x, y, z = lax.div(col, 8), lax.rem(lax.div(col, 2), 4), lax.rem(col, 2)
    column = lambda xx, yy, zz: xx * 8 + yy * 2 + zz
    ahead = lambda p, d: lax.rem(p + d, 4)
    x_others = [(row, column(ahead(x, d), y, z)) for d in range(1, 4)]
    y_others = [(row, column(x, ahead(y, d), z)) for d in range(1, 4)]
    z_mate = (row, column(x, y, 1 - z))
    core_mate = (zh * 2 + (1 - core), col)
    far = (1 - zh) * 2 + core
    z_others = [z_mate, (far, col), (far, column(x, y, 1 - z))]
    zs = (z, 1 - z)

    def index(order, wide, narrow, mine):
        xx, yy = (wide, narrow) if order == 0 else (narrow, wide)
        return (xx, yy, zs[mine], order)

    def at_place(order, w, which, mine, j):
        p, q = (x, y) if order == 0 else (y, x)
        return index(order, ahead(p, j), ahead(q, which), mine) if w == 0 else index(order, p, ahead(q, j), mine)

    def ring(order, w):
        others = x_others if order == w else y_others
        return others[0], others[2]

    def number(order, w, which, mine):
        return (order * 2 + mine) * 5 + (which if w == 0 else 4)

    class Sum:
        def __init__(self, order, w, which, mine):
            self.n = number(order, w, which, mine)
            self.blk = lambda j: at_place(order, w, which, mine, j % 4)
            self.top, self.low = SUM_ROWS[mine]
            up, down = ring(order, w)
            self.copies = []
            for i, (j, rows, to, device) in enumerate(
                (
                    (2, self.top, relays.at[self.n, 0, pl.ds(0, self.top[1])], up),
                    (2, self.low, relays.at[self.n, 1, pl.ds(0, self.low[1])], down),
                    (1, self.low, arrivals.at[self.n, 0, pl.ds(*self.low)], up),
                    (3, self.top, arrivals.at[self.n, 1, pl.ds(*self.top)], down),
                    (1, self.top, arrivals.at[self.n, 0, pl.ds(*self.top)], up),
                    (3, self.low, arrivals.at[self.n, 1, pl.ds(*self.low)], down),
                )
            ):
                src = acc.at[(*self.blk(j), pl.ds(*rows))]
                self.copies.append(remote(src, to, rs_send.at[self.n, i], rs_recv.at[self.n, i], device))

        def issue(self):
            for c in self.copies[:4]:
                c.start()

        def relay(self):
            for i, (j, rows) in enumerate(((1, self.top), (3, self.low))):
                self.copies[i].wait_recv()
                at = (*self.blk(j), pl.ds(*rows), slice(None))
                acc[at] += relays[self.n, i, 0 : rows[1], :]
                self.copies[4 + i].start()

        def finish(self):
            for c in self.copies[2:]:
                c.wait_recv()
            rows = pl.ds(self.top[0], self.top[1] + self.low[1])
            at = (*self.blk(0), rows, slice(None))
            acc[at] += arrivals[self.n, 0, rows, :] + arrivals[self.n, 1, rows, :]

        def drain(self):
            for c in self.copies:
                c.wait_send()

    class Gather:
        def __init__(self, order, w, which, mine):
            n = number(order, w, which, mine)
            blk = lambda j: at_place(order, w, which, mine, j % 4)
            top, low = GATH_ROWS[mine]
            up, down = ring(order, w)
            self.out, self.come = [], []
            for i, (leaves, comes, rows, device) in enumerate(
                (
                    (0, 3, top, up),
                    (0, 1, low, down),
                    (0, 3, low, up),
                    (0, 1, top, down),
                    (3, 2, top, up),
                    (1, 2, low, down),
                )
            ):
                for j, kept in ((leaves, self.out), (comes, self.come)):
                    ref = gath.at[(*blk(j), pl.ds(*rows))]
                    kept.append(remote(ref, ref, ag_send.at[n, i], ag_recv.at[n, i], device))

        def issue(self):
            for c in self.out[:4]:
                c.start()

        def relay(self):
            for i in range(2):
                self.come[i].wait_recv()
                self.out[4 + i].start()

        def near(self):
            for c in self.come[2:4]:
                c.wait_recv()

        def finish(self):
            for c in self.come[4:]:
                c.wait_recv()

        def drain(self):
            for c in self.out:
                c.wait_send()

    def strip(ref, order, which, mine, rows=None):
        q = ahead(y if order == 0 else x, which)
        lead = (slice(None), q) if order == 0 else (q, slice(None))
        return ref.at[(*lead, zs[mine], order) + (() if rows is None else (pl.ds(*rows),))]

    def load(order, which, mine):
        n = order * 8 + mine * 4 + which
        return pltpu.make_async_copy(strip(part_hbm, order, which, mine), strip(acc, order, which, mine), load_sem.at[n])

    def z_first(order, which):
        to = zfirst.at[order, which]
        i = order * 4 + which
        return remote(strip(part_hbm, order, which, 1, (0, FIRST)), to, zs_send.at[i], zs_recv.at[i], z_mate)

    def z_last(order):
        rows = pl.ds(FIRST, ROWS - FIRST)
        src = acc.at[(*at_place(order, 0, 0, 1, 0), rows)]
        return remote(src, zlast.at[order, rows], zs_send.at[8 + order], zs_recv.at[8 + order], z_mate)

    turn = [(2, 1), (1, 1), (3, 1), (2, 0), (0, 1), (1, 0), (3, 0), (0, 0)]
    for which, mine in turn:
        for order in range(2):
            load(order, which, mine).start()
    enter([core_mate] + x_others + y_others + z_others)
    for which in (2, 1, 3, 0):
        for order in range(2):
            z_first(order, which).start()

    wide = [[Sum(order, 0, which, mine) for order in range(2)] for which, mine in turn]
    narrow = [[Sum(order, 1, 0, mine) for order in range(2)] for mine in range(2)]

    def each(pair, action):
        for s in pair:
            getattr(s, action)()

    def sum_issue(i):
        which, mine = turn[i]
        for order in range(2):
            load(order, which, mine).wait()
            if mine == 0:
                z_first(order, which).wait_recv()
                p = y if order == 0 else x
                for j in range(4):
                    at = (*index(order, j, ahead(p, which), 0), pl.ds(0, FIRST), slice(None))
                    acc[at] += zfirst[order, which, j]
            wide[i][order].issue()

    for i in range(len(turn) + 1):
        if i < len(turn):
            sum_issue(i)
        if i == 0:
            own_term[...] = dot3(x_ref[...], ws_ref[...])
        if i >= 1:
            each(wide[i - 1], "relay")
        if i == 5:
            for n in range(3):
                each(wide[n], "finish")
            each(narrow[1], "issue")
        if i == 6:
            each(narrow[1], "relay")
        if i == 7:
            each(wide[4], "finish")
            each(narrow[1], "finish")
            for order in range(2):
                z_last(order).start()
    for n in (3, 5, 6):
        each(wide[n], "finish")
    each(narrow[0], "issue")
    each(wide[7], "finish")
    each(narrow[0], "relay")
    each(narrow[0], "finish")

    x_own = x_ref[...]
    ws, wn = ws_ref[...], wn_ref[...]
    sums, inv = [], []
    for order in range(2):
        z_last(order).wait_recv()
        own = at_place(order, 0, 0, 0, 0)
        s = jnp.concatenate([acc[(*own, pl.ds(0, FIRST))], acc[(*own, pl.ds(FIRST, ROWS - FIRST))] + zlast[order, FIRST:, :]], axis=0)
        degree = jnp.transpose(jnp.broadcast_to(s[2 * TILE : 2 * TILE + 1, :], (TILE, TILE)))
        root = lax.rsqrt(1.0 + degree)
        inv.append(jnp.concatenate([root, root], axis=1))
        sums.append(jnp.concatenate([s[0:TILE], s[TILE : 2 * TILE]], axis=1))
    inv = jnp.concatenate(inv, axis=0)
    neighbour = jnp.concatenate(sums, axis=0) * inv
    pre = own_term[...] + dot3(neighbour, wn) + bias_ref[...]
    out, grad_pre = rms_silu(pre, cot_ref[...])
    layer_out[...] = out
    spread = dot3(grad_pre, wn, ((1,), (1,))) * inv
    for order in range(2):
        for half in range(2):
            gath[(*at_place(order, 0, 0, 0, 0), pl.ds(half * TILE, TILE), slice(None))] = spread[
                order * TILE : (order + 1) * TILE, half * TILE : (half + 1) * TILE
            ]

    def give(order, mine):
        ref = gath.at[(*at_place(order, 0, 0, mine, 0), pl.ds(FIRST, 2 * TILE - FIRST))]
        return remote(ref, ref, zg_send.at[8 + order], zg_recv.at[8 + order], z_mate)

    def z_after(order, which, mine):
        ref = strip(gath, order, which, mine, (0, FIRST))
        i = order * 4 + which
        return remote(ref, ref, zg_send.at[i], zg_recv.at[i], z_mate)

    def write(order, which, mine):
        n = order * 8 + mine * 4 + which
        return pltpu.make_async_copy(strip(gath, order, which, mine), strip(g_out, order, which, mine), out_sem.at[n])

    gwide = {(which, mine): [Gather(order, 0, which, mine) for order in range(2)] for which in range(4) for mine in range(2)}
    gnarrow = [[Gather(order, 1, 0, mine) for order in range(2)] for mine in range(2)]

    def done(which, mine):
        each(gwide[which, mine], "near")
        each(gwide[which, mine], "finish")
        for order in range(2):
            if mine == 0:
                z_after(order, which, 0).start()
                write(order, which, 0).start()

    for order in range(2):
        give(order, 0).start()
    each(gnarrow[0], "issue")
    each(gwide[0, 0], "issue")

    gs = dot3(x_own, grad_pre, ((0,), (0,)))
    gn = dot3(neighbour, grad_pre, ((0,), (0,)))
    flat = [gs[:, 0:TILE], gs[:, TILE:], gn[:, 0:TILE], gn[:, TILE:]]
    gb = jnp.sum(grad_pre, axis=0, keepdims=True)
    gwp[...] = jnp.zeros_like(gwp)
    for i, f in enumerate(flat):
        gwp[i * WIDTH : (i + 1) * WIDTH, :] = f
    gwp[4 * WIDTH : 4 * WIDTH + 1, :] = gb[:, 0:TILE]
    gwp[4 * WIDTH + 1 : 4 * WIDTH + 2, :] = gb[:, TILE:]

    n_core, n_x, n_y = 16 * PART_ROWS, 4 * PART_ROWS, PART_ROWS
    rows_at = lambda c, xx, yy, n: pl.ds(pl.multiple_of((c * 16 + xx * 4 + yy) * PART_ROWS, 8), n)
    span = lambda *at: gwp.at[rows_at(*at)]
    hop = lambda i, src, dst, device: remote(src, dst, ar_send.at[i], ar_recv.at[i], device)

    c1 = [hop(0, span(1 - core, 0, 0, n_core), r1, core_mate)]
    c2 = [hop(d, span(core, ahead(x, d), 0, n_x), r2.at[d - 1], x_others[d - 1]) for d in range(1, 4)]
    c3 = [hop(3 + d, span(core, x, ahead(y, d), n_y), r3.at[d - 1], y_others[d - 1]) for d in range(1, 4)]
    c4 = [hop(7 + d, own_part, r4.at[d], z_others[d]) for d in range(3)]

    def launch(copies):
        for c in copies:
            c.start()

    def land(copies):
        for c in copies:
            c.wait()

    def add_parts(at, terms):
        v = gwp[at, :]
        for term in terms:
            v = v + term
        gwp[at, :] = v

    def phase1():
        land(c1)
        add_parts(rows_at(core, 0, 0, n_core), [r1[...]])
        launch(c2)

    def phase2():
        land(c2)
        add_parts(rows_at(core, x, 0, n_x), [r2[d] for d in range(3)])
        launch(c3)

    def phase3():
        land(c3)
        own_part[...] = gwp[rows_at(core, x, y, n_y), :] + r3[0] + r3[1] + r3[2]
        launch(c4)

    def phase4():
        land(c4)
        gw_out[...] = (own_part[...] + r4[0]) + (r4[1] + r4[2])

    launch(c1)
    direct_out[...] = dot3(grad_pre, ws, ((1,), (1,)))

    each(gnarrow[0], "relay")
    each(gwide[0, 0], "relay")
    each(gnarrow[0], "near")
    each(gwide[1, 0], "issue")
    for order in range(2):
        give(order, 1).wait_recv()
    each(gnarrow[1], "issue")
    each(gwide[3, 0], "issue")
    each(gwide[1, 0], "relay")
    phase1()
    each(gnarrow[1], "relay")
    each(gnarrow[0], "finish")
    each(gwide[2, 0], "issue")
    each(gwide[3, 0], "relay")
    done(0, 0)
    each(gwide[0, 1], "issue")
    each(gwide[2, 0], "relay")
    done(1, 0)
    each(gnarrow[1], "near")
    each(gwide[1, 1], "issue")
    each(gwide[0, 1], "relay")
    done(3, 0)
    phase2()
    each(gnarrow[1], "finish")
    each(gwide[3, 1], "issue")
    each(gwide[1, 1], "relay")
    done(2, 0)
    each(gwide[2, 1], "issue")
    each(gwide[3, 1], "relay")
    phase3()
    each(gwide[2, 1], "relay")
    for which in (0, 1, 3, 2):
        done(which, 1)
        for order in range(2):
            z_after(order, which, 1).wait_recv()
            write(order, which, 1).start()
    phase4()

    for pair in wide + narrow + list(gwide.values()) + gnarrow:
        each(pair, "drain")
    for order in range(2):
        z_last(order).wait_send()
        give(order, 0).wait_send()
        for which in range(4):
            z_first(order, which).wait_send()
            z_after(order, which, 0).wait_send()
    for which in range(4):
        for order in range(2):
            for own_z in range(2):
                write(order, which, own_z).wait()


def exchange(part, x, ws, wn, bias, cot):
    n = x.shape[0]
    layout = (4, 4, 2, 2)
    out = pl.pallas_call(
        exchange_kernel,
        out_shape=(
            jax.ShapeDtypeStruct((n, WIDTH), F32),
            jax.ShapeDtypeStruct((n, WIDTH), F32),
            jax.ShapeDtypeStruct((*layout, 2 * TILE, TILE), F32),
            jax.ShapeDtypeStruct((PART_ROWS, TILE), F32),
        ),
        in_specs=[ANY, VM, VM, VM, VM, VM],
        out_specs=(VM, VM, ANY, VM),
        scratch_shapes=[
            pltpu.VMEM((*layout, ROWS, TILE), F32),
            pltpu.VMEM((SLICES, 2, 136, TILE), F32),
            pltpu.VMEM((SLICES, 2, ROWS, TILE), F32),
            pltpu.VMEM((2, 4, 4, FIRST, TILE), F32),
            pltpu.VMEM((2, ROWS, TILE), F32),
            pltpu.VMEM((*layout, 2 * TILE, TILE), F32),
            pltpu.VMEM((n, WIDTH), F32),
            pltpu.VMEM((PARTS * PART_ROWS, TILE), F32),
            pltpu.VMEM((16 * PART_ROWS, TILE), F32),
            pltpu.VMEM((3, 4 * PART_ROWS, TILE), F32),
            pltpu.VMEM((3, PART_ROWS, TILE), F32),
            pltpu.VMEM((3, PART_ROWS, TILE), F32),
            pltpu.VMEM((PART_ROWS, TILE), F32),
            DMA((16,)),
            DMA((SLICES, 6)),
            DMA((SLICES, 6)),
            DMA((10,)),
            DMA((10,)),
            DMA((SLICES, 6)),
            DMA((SLICES, 6)),
            DMA((10,)),
            DMA((10,)),
            DMA((AR_SENDS,)),
            DMA((AR_SENDS,)),
            DMA((16,)),
        ],
        compiler_params=pltpu.CompilerParams(
            collective_id=1, has_side_effects=True, vmem_limit_bytes=VMEM_LIMIT
        ),
        name="exchange",
    )(part.reshape(*layout, ROWS, TILE), x, ws, wn, bias.reshape(1, WIDTH), cot)
    layer_out, direct, g, gw = out
    return layer_out, direct, g.reshape(DESTS, 2 * TILE, TILE), gw


def backward_kernel(
    dest, source, count, g_hbm, tiles_hbm, kept_hbm, out_ref, kept_out, tiles, g, acc, sems, g_sem, kept_sem
):
    g_copy = pltpu.make_async_copy(g_hbm, g, g_sem)
    g_copy.start()
    for c in range(CHUNKS):
        tile_copy(tiles_hbm, tiles, sems, c).start()
    kept = pltpu.make_async_copy(kept_hbm, kept_out, kept_sem)
    kept.start()
    live = count[0]

    def clear(s, _):
        acc[s] = jnp.zeros((TILE, WIDTH), F32)
        return 0

    lax.fori_loop(0, SOURCES + 1, clear, 0)
    g_copy.wait()

    def one(t):
        d = dest[t]
        s = jnp.where(t < live, source[t], SOURCES)
        hi, lo = split(tiles[t])
        ghi, glo = split(jnp.concatenate([g[d, 0:TILE, :], g[d, TILE:, :]], axis=1))
        a = jnp.concatenate([hi, lo, hi], axis=0)
        acc[s] += mm(a, jnp.concatenate([ghi, ghi, glo], axis=0), ((0,), (0,)))

    def group(g_, _):
        for u in range(UNROLL):
            one(g_ * UNROLL + u)
        return 0

    def chunk(c, _):
        tile_copy(tiles_hbm, tiles, sems, c).wait()
        per = CHUNK // UNROLL
        return lax.fori_loop(c * per, (c + 1) * per, group, 0)

    lax.fori_loop(0, CHUNKS, chunk, 0)
    for s in range(SOURCES):
        out_ref[s * TILE : (s + 1) * TILE, :] = acc[s]
    kept.wait()


def backward_tiles(dest, source, count, g, values, kept):
    return pl.pallas_call(
        backward_kernel,
        out_shape=(jax.ShapeDtypeStruct((SOURCES * TILE, WIDTH), F32), jax.ShapeDtypeStruct(kept.shape, F32)),
        in_specs=[SM, SM, SM, ANY, ANY, ANY],
        out_specs=(VM, ANY),
        scratch_shapes=[
            pltpu.VMEM((SLOTS, TILE, TILE), F32),
            pltpu.VMEM((DESTS, 2 * TILE, TILE), F32),
            pltpu.VMEM((SOURCES + 1, TILE, WIDTH), F32),
            DMA((CHUNKS,)),
            DMA,
            DMA,
        ],
        compiler_params=pltpu.CompilerParams(vmem_limit_bytes=VMEM_LIMIT),
        cost_estimate=pl.CostEstimate(
            flops=SLOTS * 6 * TILE * TILE * WIDTH, bytes_accessed=22_000_000, transcendentals=0
        ),
        name="backward_tiles",
    )(dest, source, count, g, values, kept)


def scatter_kernel(back_ref, part_ref, out_ref, gw_out, near, cross, send_buf, gws, send, recv, ar_send, ar_recv):
    row, col = lax.axis_index("row"), lax.axis_index("col")
    hi, core = lax.div(row, 2), lax.rem(row, 2)
    x, y, z = lax.div(col, 8), lax.rem(lax.div(col, 2), 4), lax.rem(col, 2)
    column = lambda xx, yy, zz: xx * 8 + yy * 2 + zz
    ahead = lambda p, d: lax.rem(p + d, 4)
    x_others = [(row, column(ahead(x, d), y, z)) for d in range(1, 4)]
    y_others = [(row, column(x, ahead(y, d), z)) for d in range(1, 4)]
    mate = (hi * 2 + (1 - core), col)
    far = ((1 - hi) * 2 + core, col)
    enter([mate, far] + x_others + y_others)
    n = out_ref.shape[0]
    m = n // PIECES
    at = lambda r, c: pl.ds(pl.multiple_of(r * n + c * m, m), m)
    piece = lambda c: pl.ds(c * m, m)
    far_row, far_mate = (1 - hi) * 2 + core, (1 - hi) * 2 + (1 - core)
    first, second, third = [], [], []
    for c in range(PIECES):
        src = back_ref.at[at(far_mate, c)]
        first.append(remote(src, near.at[0, piece(c)], send.at[0, c], recv.at[0, c], mate))
        src = back_ref.at[at(hi * 2 + (1 - core), c)]
        second.append(remote(src, near.at[1, piece(c)], send.at[1, c], recv.at[1, c], mate))
        third.append(remote(send_buf.at[piece(c)], cross.at[piece(c)], send.at[2, c], recv.at[2, c], far))
    for c in first + second:
        c.start()

    rows_at = lambda c, xx, yy, k: pl.ds(pl.multiple_of((c * 16 + xx * 4 + yy) * PART_ROWS, 8), k)
    summed = lambda *w: gws.at[rows_at(*w)]
    hop = lambda i, ref, device: remote(ref, ref, ar_send.at[i], ar_recv.at[i], device)
    gws[rows_at(core, x, y, PART_ROWS), :] = part_ref[...]
    c5 = [hop(d, summed(core, x, y, PART_ROWS), y_others[d]) for d in range(3)]
    c6 = [hop(3 + d, summed(core, x, 0, 4 * PART_ROWS), x_others[d]) for d in range(3)]
    c7 = [hop(6, summed(core, 0, 0, 16 * PART_ROWS), mate)]
    for c in c5:
        c.start()
    for c in range(PIECES):
        first[c].wait_recv()
        send_buf[piece(c), :] = back_ref[at(far_row, c), :] + near[0, piece(c), :]
        third[c].start()
    for d in range(3):
        hop(d, summed(core, x, ahead(y, 3 - d), PART_ROWS), y_others[d]).wait_recv()
    for c in c6:
        c.start()
    for d in range(3):
        hop(3 + d, summed(core, ahead(x, 3 - d), 0, 4 * PART_ROWS), x_others[d]).wait_recv()
    for c in c7:
        c.start()
    for c in range(PIECES):
        second[c].wait_recv()
        third[c].wait_recv()
        out_ref[piece(c), :] = back_ref[at(row, c), :] + near[1, piece(c), :] + cross[piece(c), :]
    hop(6, summed(1 - core, 0, 0, 16 * PART_ROWS), mate).wait_recv()
    gw_out[...] = gws[0 : 4 * WIDTH + 8, :]
    for c in first + second + third + c5 + c6 + c7:
        c.wait_send()


def scatter_rows(back, part):
    n = back.shape[0] // 4
    return pl.pallas_call(
        scatter_kernel,
        out_shape=(jax.ShapeDtypeStruct((n, WIDTH), F32), jax.ShapeDtypeStruct((4 * WIDTH + 8, TILE), F32)),
        in_specs=[VM, VM],
        out_specs=(VM, VM),
        scratch_shapes=[
            pltpu.VMEM((2, n, WIDTH), F32),
            pltpu.VMEM((n, WIDTH), F32),
            pltpu.VMEM((n, WIDTH), F32),
            pltpu.VMEM((PARTS * PART_ROWS, TILE), F32),
            DMA((3, PIECES)),
            DMA((3, PIECES)),
            DMA((7,)),
            DMA((7,)),
        ],
        compiler_params=pltpu.CompilerParams(collective_id=2, has_side_effects=True),
        name="scatter_rows",
    )(back, part)


def body(x, ws, wn, bias, tile_values, tile_dest, tile_source, tile_count, cot):
    values = tile_values.reshape(SLOTS, TILE, TILE)
    dest, source, count = tile_dest.reshape(SLOTS), tile_source.reshape(SLOTS), tile_count.reshape(1)
    slab = gather_rows(x)
    part = forward_tiles(dest, source, count, slab, values)
    layer_out, direct, g, gw_part = exchange(part, x, ws, wn, bias, cot)
    back, layer_out = backward_tiles(dest, source, count, g, values, layer_out)
    back, gw = scatter_rows(back, gw_part)
    grad_x = direct + back
    w = lambda i: jnp.concatenate([gw[i * WIDTH : (i + 1) * WIDTH], gw[(i + 1) * WIDTH : (i + 2) * WIDTH]], axis=1)
    grad_bias = gw[4 * WIDTH : 4 * WIDTH + 2].reshape(WIDTH)
    return layer_out, grad_x, w(0), w(2), grad_bias


def solution(mesh):
    in_specs = (
        P(("col", "row"), None),
        P(),
        P(),
        P(),
        P("row", "col", None, None, None),
        P("row", "col", None),
        P("row", "col", None),
        P("row", "col"),
        P(("col", "row"), None),
    )
    out_specs = (P(("col", "row"), None), P(("col", "row"), None), P(), P(), P())
    return jax.shard_map(body, mesh=mesh, in_specs=in_specs, out_specs=out_specs, check_vma=False)
```

```python
import functools

import jax
import jax.numpy as jnp
from jax import lax
from jax.experimental import pallas as pl
from jax.experimental.pallas import tpu as pltpu
from jax.sharding import PartitionSpec as P

EPSILON = 1e-05
F32 = jnp.float32
BF16 = jnp.bfloat16
MESH = pl.DeviceIdType.MESH
TILE = 128
WIDTH = 256
SLOTS = 192
DESTS = 64
SOURCES = 8
ROWS = 264
CHUNK = 16
CHUNKS = SLOTS // CHUNK
UNROLL = 16
PIECES = 4
FIT = 8
KEYS = 4 * SOURCES
PLAN_TILE, PLAN_BLOCK, PLAN_COUNT = 0, KEYS * FIT, 2 * KEYS * FIT
PLAN_REST, PLAN_LIST = PLAN_COUNT + KEYS, PLAN_COUNT + 2 * KEYS
PLAN_SIZE = 1024
PLAN_VOID = PLAN_SIZE - 1
REST_SLOTS = 16
VMEM_LIMIT = 60 * 1024 * 1024

VM = pl.BlockSpec(memory_space=pltpu.VMEM)
SM = pl.BlockSpec(memory_space=pltpu.SMEM)
ANY = pl.BlockSpec(memory_space=pl.ANY)
DMA = pltpu.SemaphoreType.DMA


def split(a):
    hi = a.astype(BF16)
    return hi, (a - hi.astype(F32)).astype(BF16)


def mm(a, b, dims=((1,), (0,))):
    return lax.dot_general(a, b, (dims, ((), ())), preferred_element_type=F32)


def dot3(a, b, dims=((1,), (0,))):
    ah, al = split(a)
    bh, bl = split(b)
    return mm(ah, bh, dims) + (mm(ah, bl, dims) + mm(al, bh, dims))


def enter(devices):
    barrier = pltpu.get_barrier_semaphore()
    for device in devices:
        pl.semaphore_signal(barrier, inc=1, device_id=device, device_id_type=MESH)
    pl.semaphore_wait(barrier, len(devices))


def remote(src, dst, send, recv, device):
    return pltpu.make_async_remote_copy(
        src_ref=src, dst_ref=dst, send_sem=send, recv_sem=recv, device_id=device, device_id_type=MESH
    )


def arrival(q, col):
    x, y, z = lax.div(col, 8), lax.rem(lax.div(col, 2), 4), lax.rem(col, 2)
    bx, by, order = lax.shift_right_logical(q, 4), lax.shift_right_logical(q, 2) & 3, q & 1
    other = (lax.shift_right_logical(q, 1) & 1) ^ z
    which = jnp.where(order == 0, by - y, bx - x) & 3
    wide = jnp.where(order == 0, bx, by)
    half = lax.shift_right_logical(which, 1)
    local = (which & 1) ^ half
    return other * 2 + half, (local * 4 + wide) * 2 + order


def gather_kernel(count, dest_ref, source_ref, x_ref, out_ref, keys_out, local_sem, send, recv):
    row, col = lax.axis_index("row"), lax.axis_index("col")
    hi, core = lax.div(row, 2), lax.rem(row, 2)
    mate = hi * 2 + (1 - core)
    far = (1 - hi) * 2 + core
    enter([(mate, col), (far, col)])
    n = x_ref.shape[0]
    m = n // PIECES
    at = lambda r, c: out_ref.at[pl.ds(pl.multiple_of(r * n + c * m, m), m)]
    piece = lambda c: x_ref.at[pl.ds(c * m, m)]
    own = pltpu.make_async_copy(x_ref, out_ref.at[pl.ds(pl.multiple_of(row * n, n), n)], local_sem)
    across = [remote(piece(c), at(row, c), send.at[0, c], recv.at[0, c], (far, col)) for c in range(PIECES)]
    beside = [remote(piece(c), at(row, c), send.at[1, c], recv.at[1, c], (mate, col)) for c in range(PIECES)]
    onward = [remote(at(far, c), at(far, c), send.at[2, c], recv.at[2, c], (mate, col)) for c in range(PIECES)]
    for c in across + beside:
        c.start()
    own.start()
    dest = dest_ref[...]
    quarter, block = arrival(dest, col)
    listed = lax.broadcasted_iota(jnp.int32, dest.shape, 1) < count[0]
    keys_out[0:1, :] = jnp.where(listed, quarter * SOURCES + source_ref[...], KEYS)
    keys_out[1:2, :] = quarter * 16 + block
    for c in range(PIECES):
        across[c].wait_recv()
        onward[c].start()
    for c in beside + onward:
        c.wait_recv()
    own.wait()
    for c in across + beside + onward:
        c.wait_send()


def gather_rows(count, dest, source, x):
    return pl.pallas_call(
        gather_kernel,
        out_shape=(jax.ShapeDtypeStruct((4 * x.shape[0], x.shape[1]), F32), jax.ShapeDtypeStruct((2, SLOTS), jnp.int32)),
        in_specs=[SM, VM, VM, VM],
        out_specs=(VM, VM),
        scratch_shapes=[DMA, DMA((3, PIECES)), DMA((3, PIECES))],
        compiler_params=pltpu.CompilerParams(collective_id=0, has_side_effects=True),
        name="gather_rows",
    )(count, dest, source, x)


def tile_copy(tiles_hbm, tiles, sems, c):
    at = pl.ds(c * CHUNK, CHUNK)
    return pltpu.make_async_copy(tiles_hbm.at[at], tiles.at[at], sems.at[c])


def forward_kernel(
    dest, source, keys, count, x_ref, tiles_hbm, out_hbm, plan, tiles, acc, total, xs, held, sems, out_sem
):
    for c in range(CHUNKS):
        tile_copy(tiles_hbm, tiles, sems, c).start()
    live = count[0]
    for s in range(SOURCES):
        hi, lo = split(x_ref[s * TILE : (s + 1) * TILE, :])
        xs[s, 0:TILE, :] = hi
        xs[s, TILE : 2 * TILE, :] = hi
        xs[s, 2 * TILE :, :] = lo

    def clear(d, _):
        acc[d] = jnp.zeros((ROWS, TILE), F32)
        total[d] = jnp.zeros((TILE, TILE), F32)
        for u in range(2 * KEYS * FIT // DESTS):
            plan[jnp.minimum(d, DESTS - 1) * (2 * KEYS * FIT // DESTS) + u] = 0
        held[jnp.minimum(d, KEYS + 1)] = 0
        return 0

    lax.fori_loop(0, DESTS + 1, clear, 0)

    def enlist(t):
        key = keys[0, t]
        n, rest = held[key], held[KEYS + 1]
        late = jnp.logical_and(key < KEYS, n >= FIT)
        fits = jnp.logical_and(key < KEYS, n < FIT)
        slot = jnp.where(fits, key * FIT + n, PLAN_VOID - PLAN_BLOCK)
        plan[jnp.where(late, PLAN_LIST + rest, PLAN_TILE + slot)] = t
        plan[PLAN_BLOCK + slot] = keys[1, t]
        held[key] = n + 1
        held[KEYS + 1] = rest + jnp.where(late, 1, 0)

    def one(t):
        enlist(t)
        s = source[0, t]
        d = jnp.where(t < live, dest[0, t], DESTS)
        a = tiles[t]
        hi, lo = split(a)
        p = mm(jnp.concatenate([hi, lo, hi], axis=1), xs[s])
        acc[d, 0:TILE, :] += p[:, 0:TILE]
        acc[d, TILE : 2 * TILE, :] += p[:, TILE:]
        total[d] += a

    def group(g, _):
        for u in range(UNROLL):
            one(g * UNROLL + u)
        return 0

    def chunk(c, _):
        tile_copy(tiles_hbm, tiles, sems, c).wait()
        per = CHUNK // UNROLL
        return lax.fori_loop(c * per, (c + 1) * per, group, 0)

    lax.fori_loop(0, CHUNKS, chunk, 0)
    ones = jnp.ones((8, 2 * TILE), BF16)
    per = DESTS // 8

    def write(g):
        at = pl.ds(g * per, per)
        return pltpu.make_async_copy(acc.at[at], out_hbm.at[at], out_sem.at[g])

    def degrees(g, _):
        for u in range(per):
            d = g * per + u
            hi, lo = split(total[d])
            acc[d, 2 * TILE :, :] = mm(ones, jnp.concatenate([hi, lo], axis=1), ((1,), (1,)))
        write(g).start()
        return 0

    lax.fori_loop(0, 8, degrees, 0)

    def counts(k, _):
        plan[PLAN_COUNT + k] = jnp.minimum(held[k], FIT)
        return 0

    lax.fori_loop(0, KEYS, counts, 0)
    plan[PLAN_REST] = held[KEYS + 1]
    for g in range(8):
        write(g).wait()


def forward_tiles(dest, source, keys, count, slab, values):
    return pl.pallas_call(
        forward_kernel,
        out_shape=(jax.ShapeDtypeStruct((DESTS, ROWS, TILE), F32), jax.ShapeDtypeStruct((PLAN_SIZE,), jnp.int32)),
        in_specs=[SM, SM, SM, SM, VM, ANY],
        out_specs=(ANY, SM),
        scratch_shapes=[
            pltpu.VMEM((SLOTS, TILE, TILE), F32),
            pltpu.VMEM((DESTS + 1, ROWS, TILE), F32),
            pltpu.VMEM((DESTS + 1, TILE, TILE), F32),
            pltpu.VMEM((SOURCES, 3 * TILE, WIDTH), BF16),
            pltpu.SMEM((KEYS + 2,), jnp.int32),
            DMA((CHUNKS,)),
            DMA((8,)),
        ],
        compiler_params=pltpu.CompilerParams(vmem_limit_bytes=VMEM_LIMIT),
        cost_estimate=pl.CostEstimate(
            flops=SLOTS * 6 * TILE * TILE * WIDTH, bytes_accessed=22_000_000, transcendentals=0
        ),
        name="forward_tiles",
    )(dest, source, keys, count, slab, values)


def rms_silu(pre, cot):
    sig = 1.0 / (1.0 + jnp.exp(-pre))
    s = pre * sig
    r = lax.rsqrt(jnp.mean(s * s, axis=-1, keepdims=True) + EPSILON)
    inner = jnp.mean(cot * s, axis=-1, keepdims=True)
    ds = r * cot - s * (r * r * r * inner)
    return s * r, ds * sig * (1.0 + pre * (1.0 - sig))


PARTS = 32
PART_ROWS = 40
AR_SENDS = 10
FIRST = 64
SUM_ROWS = (((0, 136), (136, 128)), ((FIRST, 104), (FIRST + 104, 96)))
GATH_ROWS = (((0, 128), (128, 128)), ((FIRST, 96), (FIRST + 96, 96)))
SLICES = 20


def exchange_kernel(
    plan, part_hbm, x_ref, ws_ref, wn_ref, bias_ref, cot_ref, tiles_hbm,
    layer_out, direct_out, g_out, gw_out, back_out,
    acc, relays, arrivals, zfirst, zlast, g0, g1, g2, g3, tiles, own_term, gwp, r1, r2, r3, r4, own_part,
    load_sem, rs_send, rs_recv, zs_send, zs_recv, ag_send, ag_recv, zg_send, zg_recv, ar_send, ar_recv, out_sem, tile_sem,
):
    quarters = (g0, g1, g2, g3)
    row, col = lax.axis_index("row"), lax.axis_index("col")
    zh, core = lax.div(row, 2), lax.rem(row, 2)
    x, y, z = lax.div(col, 8), lax.rem(lax.div(col, 2), 4), lax.rem(col, 2)
    column = lambda xx, yy, zz: xx * 8 + yy * 2 + zz
    ahead = lambda p, d: lax.rem(p + d, 4)
    x_others = [(row, column(ahead(x, d), y, z)) for d in range(1, 4)]
    y_others = [(row, column(x, ahead(y, d), z)) for d in range(1, 4)]
    z_mate = (row, column(x, y, 1 - z))
    core_mate = (zh * 2 + (1 - core), col)
    far = (1 - zh) * 2 + core
    z_others = [z_mate, (far, col), (far, column(x, y, 1 - z))]
    zs = (z, 1 - z)

    def index(order, wide, narrow, mine):
        xx, yy = (wide, narrow) if order == 0 else (narrow, wide)
        return (xx, yy, zs[mine], order)

    def at_place(order, w, which, mine, j):
        p, q = (x, y) if order == 0 else (y, x)
        return index(order, ahead(p, j), ahead(q, which), mine) if w == 0 else index(order, p, ahead(q, j), mine)

    def ring(order, w):
        others = x_others if order == w else y_others
        return others[0], others[2]

    def number(order, w, which, mine):
        return (order * 2 + mine) * 5 + (which if w == 0 else 4)

    class Sum:
        def __init__(self, order, w, which, mine):
            self.n = number(order, w, which, mine)
            self.blk = lambda j: at_place(order, w, which, mine, j % 4)
            self.top, self.low = SUM_ROWS[mine]
            up, down = ring(order, w)
            self.copies = []
            for i, (j, rows, to, device) in enumerate(
                (
                    (2, self.top, relays.at[self.n, 0, pl.ds(0, self.top[1])], up),
                    (2, self.low, relays.at[self.n, 1, pl.ds(0, self.low[1])], down),
                    (1, self.low, arrivals.at[self.n, 0, pl.ds(*self.low)], up),
                    (3, self.top, arrivals.at[self.n, 1, pl.ds(*self.top)], down),
                    (1, self.top, arrivals.at[self.n, 0, pl.ds(*self.top)], up),
                    (3, self.low, arrivals.at[self.n, 1, pl.ds(*self.low)], down),
                )
            ):
                src = acc.at[(*self.blk(j), pl.ds(*rows))]
                self.copies.append(remote(src, to, rs_send.at[self.n, i], rs_recv.at[self.n, i], device))

        def issue(self):
            for c in self.copies[:4]:
                c.start()

        def relay(self):
            for i, (j, rows) in enumerate(((1, self.top), (3, self.low))):
                self.copies[i].wait_recv()
                at = (*self.blk(j), pl.ds(*rows), slice(None))
                acc[at] += relays[self.n, i, 0 : rows[1], :]
                self.copies[4 + i].start()

        def finish(self):
            for c in self.copies[2:]:
                c.wait_recv()
            rows = pl.ds(self.top[0], self.top[1] + self.low[1])
            at = (*self.blk(0), rows, slice(None))
            acc[at] += arrivals[self.n, 0, rows, :] + arrivals[self.n, 1, rows, :]

        def drain(self):
            for c in self.copies:
                c.wait_send()

    def quarter_of(which, mine):
        return mine * 2 + which // 2, (which & 1) ^ (which // 2)

    def held(order, wide, which, mine):
        quarter, local = quarter_of(which, mine)
        return quarters[quarter].at[local, wide, order]

    class Gather:
        def __init__(self, order, w, which, mine):
            n = number(order, w, which, mine)
            p = x if order == 0 else y

            def blk(j):
                return held(order, ahead(p, j), which, mine) if w == 0 else held(order, p, j, mine)

            top, low = GATH_ROWS[mine]
            up, down = ring(order, w)
            self.out, self.come = [], []
            for i, (leaves, comes, rows, device) in enumerate(
                (
                    (0, 3, top, up),
                    (0, 1, low, down),
                    (0, 3, low, up),
                    (0, 1, top, down),
                    (3, 2, top, up),
                    (1, 2, low, down),
                )
            ):
                src, come = blk(leaves).at[pl.ds(*rows)], blk(comes).at[pl.ds(*rows)]
                dst = src if w == 0 else come
                self.out.append(remote(src, dst, ag_send.at[n, i], ag_recv.at[n, i], device))
                self.come.append(remote(come, come, ag_send.at[n, i], ag_recv.at[n, i], device))

        def issue(self):
            for c in self.out[:4]:
                c.start()

        def relay(self):
            for i in range(2):
                self.come[i].wait_recv()
                self.out[4 + i].start()

        def near(self):
            for c in self.come[2:4]:
                c.wait_recv()

        def finish(self):
            for c in self.come[4:]:
                c.wait_recv()

        def drain(self):
            for c in self.out:
                c.wait_send()

    def strip(ref, order, which, mine, rows=None):
        q = ahead(y if order == 0 else x, which)
        lead = (slice(None), q) if order == 0 else (q, slice(None))
        return ref.at[(*lead, zs[mine], order) + (() if rows is None else (pl.ds(*rows),))]

    def load(order, which, mine):
        n = order * 8 + mine * 4 + which
        return pltpu.make_async_copy(strip(part_hbm, order, which, mine), strip(acc, order, which, mine), load_sem.at[n])

    def z_first(order, which):
        to = zfirst.at[order, which]
        i = order * 4 + which
        return remote(strip(part_hbm, order, which, 1, (0, FIRST)), to, zs_send.at[i], zs_recv.at[i], z_mate)

    def z_last(order):
        rows = pl.ds(FIRST, ROWS - FIRST)
        src = acc.at[(*at_place(order, 0, 0, 1, 0), rows)]
        return remote(src, zlast.at[order, rows], zs_send.at[8 + order], zs_recv.at[8 + order], z_mate)

    turn = [(2, 1), (1, 1), (3, 1), (2, 0), (0, 1), (1, 0), (3, 0), (0, 0)]
    for which, mine in turn:
        for order in range(2):
            load(order, which, mine).start()
    tile_load = pltpu.make_async_copy(tiles_hbm, tiles, tile_sem)
    tile_load.start()
    enter([core_mate] + x_others + y_others + z_others)
    for which in (2, 1, 3, 0):
        for order in range(2):
            z_first(order, which).start()

    wide = [[Sum(order, 0, which, mine) for order in range(2)] for which, mine in turn]
    narrow = [[Sum(order, 1, 0, mine) for order in range(2)] for mine in range(2)]

    def each(pair, action):
        for s in pair:
            getattr(s, action)()

    def sum_issue(i):
        which, mine = turn[i]
        for order in range(2):
            load(order, which, mine).wait()
            if mine == 0:
                z_first(order, which).wait_recv()
                p = y if order == 0 else x
                for j in range(4):
                    at = (*index(order, j, ahead(p, which), 0), pl.ds(0, FIRST), slice(None))
                    acc[at] += zfirst[order, which, j]
            wide[i][order].issue()

    for i in range(len(turn) + 1):
        if i < len(turn):
            sum_issue(i)
        if i == 0:
            own_term[...] = dot3(x_ref[...], ws_ref[...])
        if i >= 1:
            each(wide[i - 1], "relay")
        if i == 5:
            for n in range(3):
                each(wide[n], "finish")
            each(narrow[1], "issue")
        if i == 6:
            each(narrow[1], "relay")
        if i == 7:
            each(wide[4], "finish")
            each(narrow[1], "finish")
            for order in range(2):
                z_last(order).start()
    for n in (3, 5, 6):
        each(wide[n], "finish")
    each(narrow[0], "issue")
    each(wide[7], "finish")
    each(narrow[0], "relay")
    each(narrow[0], "finish")

    x_own = x_ref[...]
    ws, wn = ws_ref[...], wn_ref[...]
    sums, inv = [], []
    for order in range(2):
        z_last(order).wait_recv()
        own = at_place(order, 0, 0, 0, 0)
        s = jnp.concatenate([acc[(*own, pl.ds(0, FIRST))], acc[(*own, pl.ds(FIRST, ROWS - FIRST))] + zlast[order, FIRST:, :]], axis=0)
        degree = jnp.transpose(jnp.broadcast_to(s[2 * TILE : 2 * TILE + 1, :], (TILE, TILE)))
        root = lax.rsqrt(1.0 + degree)
        inv.append(jnp.concatenate([root, root], axis=1))
        sums.append(jnp.concatenate([s[0:TILE], s[TILE : 2 * TILE]], axis=1))
    inv = jnp.concatenate(inv, axis=0)
    neighbour = jnp.concatenate(sums, axis=0) * inv
    pre = own_term[...] + dot3(neighbour, wn) + bias_ref[...]
    out, grad_pre = rms_silu(pre, cot_ref[...])
    layer_out[...] = out
    spread = dot3(grad_pre, wn, ((1,), (1,))) * inv
    for order in range(2):
        for half in range(2):
            held(order, x if order == 0 else y, 0, 0)[half * TILE : (half + 1) * TILE, :] = spread[
                order * TILE : (order + 1) * TILE, half * TILE : (half + 1) * TILE
            ]

    def give(order):
        src, dst = [held(order, x if order == 0 else y, 0, mine).at[pl.ds(FIRST, 2 * TILE - FIRST)] for mine in range(2)]
        return remote(src, dst, zg_send.at[8 + order], zg_recv.at[8 + order], z_mate)

    def strip_held(order, which, mine):
        quarter, local = quarter_of(which, mine)
        return quarters[quarter].at[local, :, order]

    def z_after(order, which):
        i = order * 4 + which
        src, dst = [strip_held(order, which, mine).at[:, pl.ds(0, FIRST)] for mine in range(2)]
        return remote(src, dst, zg_send.at[i], zg_recv.at[i], z_mate)

    def write(order, which, mine):
        n = order * 8 + mine * 4 + which
        quarter, local = quarter_of(which, mine)
        return pltpu.make_async_copy(strip_held(order, which, mine), g_out.at[quarter, local, :, order], out_sem.at[n])

    def products(quarter, sources):
        for s in sources:
            key = quarter * SOURCES + s
            n = plan[PLAN_COUNT + key]
            total = None
            for i in range(FIT):
                t, b = plan[PLAN_TILE + key * FIT + i], plan[PLAN_BLOCK + key * FIT + i]
                a = tiles[t] * jnp.where(i < n, 1.0, 0.0)
                hi, lo = split(a)
                g = quarters[quarter][lax.shift_right_logical(b, 3) & 1, lax.shift_right_logical(b, 1) & 3, b & 1]
                ghi, glo = split(jnp.concatenate([g[0:TILE], g[TILE:]], axis=1))
                p = mm(jnp.concatenate([hi, lo, hi], axis=0), jnp.concatenate([ghi, ghi, glo], axis=0), ((0,), (0,)))
                total = p if total is None else total + p
            at = slice(s * TILE, (s + 1) * TILE)
            back_out[at, :] = total if quarter == 0 else back_out[at, :] + total

    gwide = {(which, mine): [Gather(order, 0, which, mine) for order in range(2)] for which in range(4) for mine in range(2)}
    gnarrow = [[Gather(order, 1, 0, mine) for order in range(2)] for mine in range(2)]

    def done(which, mine):
        each(gwide[which, mine], "near")
        each(gwide[which, mine], "finish")
        for order in range(2):
            if mine == 0:
                z_after(order, which).start()
                write(order, which, 0).start()

    for order in range(2):
        give(order).start()
    each(gnarrow[0], "issue")
    each(gwide[0, 0], "issue")

    gs = dot3(x_own, grad_pre, ((0,), (0,)))
    gn = dot3(neighbour, grad_pre, ((0,), (0,)))
    flat = [gs[:, 0:TILE], gs[:, TILE:], gn[:, 0:TILE], gn[:, TILE:]]
    gb = jnp.sum(grad_pre, axis=0, keepdims=True)
    gwp[...] = jnp.zeros_like(gwp)
    for i, f in enumerate(flat):
        gwp[i * WIDTH : (i + 1) * WIDTH, :] = f
    gwp[4 * WIDTH : 4 * WIDTH + 1, :] = gb[:, 0:TILE]
    gwp[4 * WIDTH + 1 : 4 * WIDTH + 2, :] = gb[:, TILE:]

    n_core, n_x, n_y = 16 * PART_ROWS, 4 * PART_ROWS, PART_ROWS
    rows_at = lambda c, xx, yy, n: pl.ds(pl.multiple_of((c * 16 + xx * 4 + yy) * PART_ROWS, 8), n)
    span = lambda *at: gwp.at[rows_at(*at)]
    hop = lambda i, src, dst, device: remote(src, dst, ar_send.at[i], ar_recv.at[i], device)

    c1 = [hop(0, span(1 - core, 0, 0, n_core), r1, core_mate)]
    c2 = [hop(d, span(core, ahead(x, d), 0, n_x), r2.at[d - 1], x_others[d - 1]) for d in range(1, 4)]
    c3 = [hop(3 + d, span(core, x, ahead(y, d), n_y), r3.at[d - 1], y_others[d - 1]) for d in range(1, 4)]
    c4 = [hop(7 + d, own_part, r4.at[d], z_others[d]) for d in range(3)]

    def launch(copies):
        for c in copies:
            c.start()

    def land(copies):
        for c in copies:
            c.wait()

    def add_parts(at, terms):
        v = gwp[at, :]
        for term in terms:
            v = v + term
        gwp[at, :] = v

    def phase1():
        land(c1)
        add_parts(rows_at(core, 0, 0, n_core), [r1[...]])
        launch(c2)

    def phase2():
        land(c2)
        add_parts(rows_at(core, x, 0, n_x), [r2[d] for d in range(3)])
        launch(c3)

    def phase3():
        land(c3)
        own_part[...] = gwp[rows_at(core, x, y, n_y), :] + r3[0] + r3[1] + r3[2]
        launch(c4)

    def phase4():
        land(c4)
        gw_out[...] = (own_part[...] + r4[0]) + (r4[1] + r4[2])

    launch(c1)
    direct_out[...] = dot3(grad_pre, ws, ((1,), (1,)))

    each(gnarrow[0], "relay")
    each(gwide[0, 0], "relay")
    each(gnarrow[0], "near")
    each(gwide[1, 0], "issue")
    for order in range(2):
        give(order).wait_recv()
    each(gnarrow[1], "issue")
    each(gwide[3, 0], "issue")
    each(gwide[1, 0], "relay")
    phase1()
    each(gnarrow[1], "relay")
    each(gnarrow[0], "finish")
    each(gwide[2, 0], "issue")
    each(gwide[3, 0], "relay")
    done(0, 0)
    each(gwide[0, 1], "issue")
    each(gwide[2, 0], "relay")
    done(1, 0)
    each(gnarrow[1], "near")
    each(gwide[1, 1], "issue")
    each(gwide[0, 1], "relay")
    tile_load.wait()
    products(0, (0, 1, 2))
    done(3, 0)
    phase2()
    each(gnarrow[1], "finish")
    each(gwide[3, 1], "issue")
    each(gwide[1, 1], "relay")
    products(0, (3, 4, 5))
    done(2, 0)
    each(gwide[2, 1], "issue")
    each(gwide[3, 1], "relay")
    products(0, (6, 7))
    phase3()
    each(gwide[2, 1], "relay")
    products(1, (0, 1, 2, 3))
    for which in range(4):
        if which == 2:
            products(1, (4, 5, 6, 7))
            products(2, range(SOURCES))
        done(which, 1)
        for order in range(2):
            z_after(order, which).wait_recv()
            write(order, which, 1).start()
    products(3, range(SOURCES))
    phase4()

    for pair in wide + narrow + list(gwide.values()) + gnarrow:
        each(pair, "drain")
    for order in range(2):
        z_last(order).wait_send()
        give(order).wait_send()
        for which in range(4):
            z_first(order, which).wait_send()
            z_after(order, which).wait_send()
    for which in range(4):
        for order in range(2):
            for own_z in range(2):
                write(order, which, own_z).wait()


def exchange(plan, part, x, ws, wn, bias, cot, values):
    n = x.shape[0]
    layout = (4, 4, 2, 2)
    out = pl.pallas_call(
        exchange_kernel,
        out_shape=(
            jax.ShapeDtypeStruct((n, WIDTH), F32),
            jax.ShapeDtypeStruct((n, WIDTH), F32),
            jax.ShapeDtypeStruct((4, 2, 4, 2, 2 * TILE, TILE), F32),
            jax.ShapeDtypeStruct((PART_ROWS, TILE), F32),
            jax.ShapeDtypeStruct((SOURCES * TILE, WIDTH), F32),
        ),
        in_specs=[SM, ANY, VM, VM, VM, VM, VM, ANY],
        out_specs=(VM, VM, ANY, VM, VM),
        scratch_shapes=[
            pltpu.VMEM((*layout, ROWS, TILE), F32),
            pltpu.VMEM((SLICES, 2, 136, TILE), F32),
            pltpu.VMEM((SLICES, 2, ROWS, TILE), F32),
            pltpu.VMEM((2, 4, 4, FIRST, TILE), F32),
            pltpu.VMEM((2, ROWS, TILE), F32),
            *[pltpu.VMEM((2, 4, 2, 2 * TILE, TILE), F32) for _ in range(4)],
            pltpu.VMEM((SLOTS, TILE, TILE), F32),
            pltpu.VMEM((n, WIDTH), F32),
            pltpu.VMEM((PARTS * PART_ROWS, TILE), F32),
            pltpu.VMEM((16 * PART_ROWS, TILE), F32),
            pltpu.VMEM((3, 4 * PART_ROWS, TILE), F32),
            pltpu.VMEM((3, PART_ROWS, TILE), F32),
            pltpu.VMEM((3, PART_ROWS, TILE), F32),
            pltpu.VMEM((PART_ROWS, TILE), F32),
            DMA((16,)),
            DMA((SLICES, 6)),
            DMA((SLICES, 6)),
            DMA((10,)),
            DMA((10,)),
            DMA((SLICES, 6)),
            DMA((SLICES, 6)),
            DMA((10,)),
            DMA((10,)),
            DMA((AR_SENDS,)),
            DMA((AR_SENDS,)),
            DMA((16,)),
            DMA,
        ],
        compiler_params=pltpu.CompilerParams(
            collective_id=1, has_side_effects=True, vmem_limit_bytes=VMEM_LIMIT
        ),
        name="exchange",
    )(plan, part.reshape(*layout, ROWS, TILE), x, ws, wn, bias.reshape(1, WIDTH), cot, values)
    layer_out, direct, g, gw, back = out
    return layer_out, direct, g.reshape(DESTS, 2 * TILE, TILE), gw, back


def rest_kernel(
    plan, source, keys, g_hbm, tiles_hbm, back_ref, out_ref, tiles, g, tile_sem, g_sem
):
    n = plan[PLAN_REST]

    def copies(i):
        slot = lax.rem(i, REST_SLOTS)
        t = plan[PLAN_LIST + i]
        return (
            pltpu.make_async_copy(tiles_hbm.at[t], tiles.at[slot], tile_sem.at[slot]),
            pltpu.make_async_copy(g_hbm.at[keys[1, t]], g.at[slot], g_sem.at[slot]),
        )

    def begin(i, _):
        for c in copies(i):
            c.start()
        return 0

    lax.fori_loop(0, jnp.minimum(n, REST_SLOTS), begin, 0)
    out_ref[...] = back_ref[...]

    def one(i, _):
        for c in copies(i):
            c.wait()
        slot = lax.rem(i, REST_SLOTS)
        rows = pl.ds(pl.multiple_of(source[0, plan[PLAN_LIST + i]] * TILE, TILE), TILE)
        hi, lo = split(tiles[slot])
        ghi, glo = split(jnp.concatenate([g[slot, 0:TILE, :], g[slot, TILE:, :]], axis=1))
        a = jnp.concatenate([hi, lo, hi], axis=0)
        out_ref[rows, :] += mm(a, jnp.concatenate([ghi, ghi, glo], axis=0), ((0,), (0,)))

        @pl.when(i + REST_SLOTS < n)
        def _():
            begin(i + REST_SLOTS, 0)

        return 0

    lax.fori_loop(0, n, one, 0)


def backward_rest(plan, source, keys, g, values, back):
    return pl.pallas_call(
        rest_kernel,
        out_shape=jax.ShapeDtypeStruct(back.shape, F32),
        in_specs=[SM, SM, SM, ANY, ANY, VM],
        out_specs=VM,
        scratch_shapes=[
            pltpu.VMEM((REST_SLOTS, TILE, TILE), F32),
            pltpu.VMEM((REST_SLOTS, 2 * TILE, TILE), F32),
            DMA((REST_SLOTS,)),
            DMA((REST_SLOTS,)),
        ],
        compiler_params=pltpu.CompilerParams(vmem_limit_bytes=VMEM_LIMIT),
        name="backward_rest",
    )(plan, source, keys, g, values, back)


def scatter_kernel(back_ref, part_ref, out_ref, gw_out, near, cross, send_buf, gws, send, recv, ar_send, ar_recv):
    row, col = lax.axis_index("row"), lax.axis_index("col")
    hi, core = lax.div(row, 2), lax.rem(row, 2)
    x, y, z = lax.div(col, 8), lax.rem(lax.div(col, 2), 4), lax.rem(col, 2)
    column = lambda xx, yy, zz: xx * 8 + yy * 2 + zz
    ahead = lambda p, d: lax.rem(p + d, 4)
    x_others = [(row, column(ahead(x, d), y, z)) for d in range(1, 4)]
    y_others = [(row, column(x, ahead(y, d), z)) for d in range(1, 4)]
    mate = (hi * 2 + (1 - core), col)
    far = ((1 - hi) * 2 + core, col)
    enter([mate, far] + x_others + y_others)
    n = out_ref.shape[0]
    m = n // PIECES
    at = lambda r, c: pl.ds(pl.multiple_of(r * n + c * m, m), m)
    piece = lambda c: pl.ds(c * m, m)
    far_row, far_mate = (1 - hi) * 2 + core, (1 - hi) * 2 + (1 - core)
    first, second, third = [], [], []
    for c in range(PIECES):
        src = back_ref.at[at(far_mate, c)]
        first.append(remote(src, near.at[0, piece(c)], send.at[0, c], recv.at[0, c], mate))
        src = back_ref.at[at(hi * 2 + (1 - core), c)]
        second.append(remote(src, near.at[1, piece(c)], send.at[1, c], recv.at[1, c], mate))
        third.append(remote(send_buf.at[piece(c)], cross.at[piece(c)], send.at[2, c], recv.at[2, c], far))
    for c in first + second:
        c.start()

    rows_at = lambda c, xx, yy, k: pl.ds(pl.multiple_of((c * 16 + xx * 4 + yy) * PART_ROWS, 8), k)
    summed = lambda *w: gws.at[rows_at(*w)]
    hop = lambda i, ref, device: remote(ref, ref, ar_send.at[i], ar_recv.at[i], device)
    gws[rows_at(core, x, y, PART_ROWS), :] = part_ref[...]
    c5 = [hop(d, summed(core, x, y, PART_ROWS), y_others[d]) for d in range(3)]
    c6 = [hop(3 + d, summed(core, x, 0, 4 * PART_ROWS), x_others[d]) for d in range(3)]
    c7 = [hop(6, summed(core, 0, 0, 16 * PART_ROWS), mate)]
    for c in c5:
        c.start()
    for c in range(PIECES):
        first[c].wait_recv()
        send_buf[piece(c), :] = back_ref[at(far_row, c), :] + near[0, piece(c), :]
        third[c].start()
    for d in range(3):
        hop(d, summed(core, x, ahead(y, 3 - d), PART_ROWS), y_others[d]).wait_recv()
    for c in c6:
        c.start()
    for d in range(3):
        hop(3 + d, summed(core, ahead(x, 3 - d), 0, 4 * PART_ROWS), x_others[d]).wait_recv()
    for c in c7:
        c.start()
    for c in range(PIECES):
        second[c].wait_recv()
        third[c].wait_recv()
        out_ref[piece(c), :] = back_ref[at(row, c), :] + near[1, piece(c), :] + cross[piece(c), :]
    hop(6, summed(1 - core, 0, 0, 16 * PART_ROWS), mate).wait_recv()
    gw_out[...] = gws[0 : 4 * WIDTH + 8, :]
    for c in first + second + third + c5 + c6 + c7:
        c.wait_send()


def scatter_rows(back, part):
    n = back.shape[0] // 4
    return pl.pallas_call(
        scatter_kernel,
        out_shape=(jax.ShapeDtypeStruct((n, WIDTH), F32), jax.ShapeDtypeStruct((4 * WIDTH + 8, TILE), F32)),
        in_specs=[VM, VM],
        out_specs=(VM, VM),
        scratch_shapes=[
            pltpu.VMEM((2, n, WIDTH), F32),
            pltpu.VMEM((n, WIDTH), F32),
            pltpu.VMEM((n, WIDTH), F32),
            pltpu.VMEM((PARTS * PART_ROWS, TILE), F32),
            DMA((3, PIECES)),
            DMA((3, PIECES)),
            DMA((7,)),
            DMA((7,)),
        ],
        compiler_params=pltpu.CompilerParams(collective_id=2, has_side_effects=True),
        name="scatter_rows",
    )(back, part)


def finish_kernel(kept, direct, back, gw, kept_out, grad_x, grad_ws, grad_wn, grad_bias):
    kept_out[...] = kept[...]
    grad_x[...] = direct[...] + back[...]
    for i, out in enumerate((grad_ws, grad_wn)):
        for half in range(2):
            first = (2 * i + half) * WIDTH
            out[:, half * TILE : (half + 1) * TILE] = gw[first : first + WIDTH, :]
    for half in range(2):
        grad_bias[:, half * TILE : (half + 1) * TILE] = gw[4 * WIDTH + half : 4 * WIDTH + half + 1, :]


def finish(kept, direct, back, gw):
    rows, square = jax.ShapeDtypeStruct(direct.shape, F32), jax.ShapeDtypeStruct((WIDTH, WIDTH), F32)
    return pl.pallas_call(
        finish_kernel,
        out_shape=(rows, rows, square, square, jax.ShapeDtypeStruct((1, WIDTH), F32)),
        in_specs=[VM] * 4,
        out_specs=(VM,) * 5,
        name="finish",
    )(kept, direct, back, gw)


def body(x, ws, wn, bias, tile_values, tile_dest, tile_source, tile_count, cot):
    values = tile_values.reshape(SLOTS, TILE, TILE)
    dest, source = tile_dest.reshape(1, SLOTS), tile_source.reshape(1, SLOTS)
    count = tile_count.reshape(1)
    slab, keys = gather_rows(count, dest, source, x)
    part, plan = forward_tiles(dest, source, keys, count, slab, values)
    layer_out, direct, g, gw_part, back = exchange(plan, part, x, ws, wn, bias, cot, values)
    back = backward_rest(plan, source, keys, g, values, back)
    back, gw = scatter_rows(back, gw_part)
    layer_out, grad_x, grad_ws, grad_wn, grad_bias = finish(layer_out, direct, back, gw)
    return layer_out, grad_x, grad_ws, grad_wn, grad_bias.reshape(WIDTH)


def solution(mesh):
    in_specs = (
        P(("col", "row"), None),
        P(),
        P(),
        P(),
        P("row", "col", None, None, None),
        P("row", "col", None),
        P("row", "col", None),
        P("row", "col"),
        P(("col", "row"), None),
    )
    out_specs = (P(("col", "row"), None), P(("col", "row"), None), P(), P(), P())
    return jax.shard_map(body, mesh=mesh, in_specs=in_specs, out_specs=out_specs, check_vma=False)
```

```python
import functools

import jax
import jax.numpy as jnp
from jax import lax
from jax.experimental import pallas as pl
from jax.experimental.pallas import tpu as pltpu
from jax.sharding import PartitionSpec as P

EPSILON = 1e-05
F32 = jnp.float32
BF16 = jnp.bfloat16
MESH = pl.DeviceIdType.MESH
TILE = 128
WIDTH = 256
SLOTS = 192
DESTS = 64
SOURCES = 8
ROWS = 264
CHUNK = 16
CHUNKS = SLOTS // CHUNK
UNROLL = 16
PIECES = 4
FIT = 8
KEYS = 4 * SOURCES
PLAN_TILE, PLAN_BLOCK, PLAN_COUNT = 0, KEYS * FIT, 2 * KEYS * FIT
PLAN_REST, PLAN_LIST = PLAN_COUNT + KEYS, PLAN_COUNT + 2 * KEYS
PLAN_SIZE = 1024
PLAN_VOID = PLAN_SIZE - 1
REST_SLOTS = 16
REST_UNROLL = 4
VMEM_LIMIT = 60 * 1024 * 1024

VM = pl.BlockSpec(memory_space=pltpu.VMEM)
SM = pl.BlockSpec(memory_space=pltpu.SMEM)
ANY = pl.BlockSpec(memory_space=pl.ANY)
DMA = pltpu.SemaphoreType.DMA


def split(a):
    hi = a.astype(BF16)
    return hi, (a - hi.astype(F32)).astype(BF16)


def mm(a, b, dims=((1,), (0,))):
    return lax.dot_general(a, b, (dims, ((), ())), preferred_element_type=F32)


def dot3(a, b, dims=((1,), (0,))):
    ah, al = split(a)
    bh, bl = split(b)
    return mm(ah, bh, dims) + (mm(ah, bl, dims) + mm(al, bh, dims))


def greet(devices):
    barrier = pltpu.get_barrier_semaphore()
    for device in devices:
        pl.semaphore_signal(barrier, inc=1, device_id=device, device_id_type=MESH)


def enter(devices):
    pl.semaphore_wait(pltpu.get_barrier_semaphore(), len(devices))


def remote(src, dst, send, recv, device):
    return pltpu.make_async_remote_copy(
        src_ref=src, dst_ref=dst, send_sem=send, recv_sem=recv, device_id=device, device_id_type=MESH
    )


def arrival(q, col):
    x, y, z = lax.div(col, 8), lax.rem(lax.div(col, 2), 4), lax.rem(col, 2)
    bx, by, order = lax.shift_right_logical(q, 4), lax.shift_right_logical(q, 2) & 3, q & 1
    other = (lax.shift_right_logical(q, 1) & 1) ^ z
    which = jnp.where(order == 0, by - y, bx - x) & 3
    wide = jnp.where(order == 0, bx, by)
    half = lax.shift_right_logical(which, 1)
    local = (which & 1) ^ half
    return other * 2 + half, (local * 4 + wide) * 2 + order


def gather_kernel(count, dest_ref, source_ref, x_ref, out_ref, keys_out, local_sem, send, recv):
    row, col = lax.axis_index("row"), lax.axis_index("col")
    hi, core = lax.div(row, 2), lax.rem(row, 2)
    mate = hi * 2 + (1 - core)
    far = (1 - hi) * 2 + core
    peers = [(mate, col), (far, col)]
    greet(peers)
    enter(peers)
    n = x_ref.shape[0]
    m = n // PIECES
    at = lambda r, c: out_ref.at[pl.ds(pl.multiple_of(r * n + c * m, m), m)]
    piece = lambda c: x_ref.at[pl.ds(c * m, m)]
    own = pltpu.make_async_copy(x_ref, out_ref.at[pl.ds(pl.multiple_of(row * n, n), n)], local_sem)
    across = [remote(piece(c), at(row, c), send.at[0, c], recv.at[0, c], (far, col)) for c in range(PIECES)]
    beside = [remote(piece(c), at(row, c), send.at[1, c], recv.at[1, c], (mate, col)) for c in range(PIECES)]
    onward = [remote(at(far, c), at(far, c), send.at[2, c], recv.at[2, c], (mate, col)) for c in range(PIECES)]
    for c in across + beside:
        c.start()
    own.start()
    dest = dest_ref[...]
    quarter, block = arrival(dest, col)
    listed = lax.broadcasted_iota(jnp.int32, dest.shape, 1) < count[0]
    keys_out[0:1, :] = jnp.where(listed, quarter * SOURCES + source_ref[...], KEYS)
    keys_out[1:2, :] = quarter * 16 + block
    for c in range(PIECES):
        across[c].wait_recv()
        onward[c].start()
    for c in beside + onward:
        c.wait_recv()
    own.wait()
    for c in across + beside + onward:
        c.wait_send()


def gather_rows(count, dest, source, x):
    return pl.pallas_call(
        gather_kernel,
        out_shape=(jax.ShapeDtypeStruct((4 * x.shape[0], x.shape[1]), F32), jax.ShapeDtypeStruct((2, SLOTS), jnp.int32)),
        in_specs=[SM, VM, VM, VM],
        out_specs=(VM, VM),
        scratch_shapes=[DMA, DMA((3, PIECES)), DMA((3, PIECES))],
        compiler_params=pltpu.CompilerParams(collective_id=0, has_side_effects=True),
        name="gather_rows",
    )(count, dest, source, x)


def tile_copy(tiles_hbm, tiles, sems, c):
    at = pl.ds(c * CHUNK, CHUNK)
    return pltpu.make_async_copy(tiles_hbm.at[at], tiles.at[at], sems.at[c])


def forward_kernel(
    dest, source, keys, count, x_ref, tiles_hbm, out_hbm, plan, tiles, acc, total, xs, held, sems, out_sem
):
    for c in range(CHUNKS):
        tile_copy(tiles_hbm, tiles, sems, c).start()
    live = count[0]
    for s in range(SOURCES):
        hi, lo = split(x_ref[s * TILE : (s + 1) * TILE, :])
        xs[s, 0:TILE, :] = hi
        xs[s, TILE : 2 * TILE, :] = hi
        xs[s, 2 * TILE :, :] = lo

    def clear(d, _):
        acc[d] = jnp.zeros((ROWS, TILE), F32)
        total[d] = jnp.zeros((TILE, TILE), F32)
        for u in range(2 * KEYS * FIT // DESTS):
            plan[jnp.minimum(d, DESTS - 1) * (2 * KEYS * FIT // DESTS) + u] = 0
        held[jnp.minimum(d, KEYS + 1)] = 0
        return 0

    lax.fori_loop(0, DESTS + 1, clear, 0)

    def enlist(t):
        key = keys[0, t]
        n, rest = held[key], held[KEYS + 1]
        late = jnp.logical_and(key < KEYS, n >= FIT)
        fits = jnp.logical_and(key < KEYS, n < FIT)
        slot = jnp.where(fits, key * FIT + n, PLAN_VOID - PLAN_BLOCK)
        plan[jnp.where(late, PLAN_LIST + rest, PLAN_TILE + slot)] = t
        plan[PLAN_BLOCK + slot] = keys[1, t]
        held[key] = n + 1
        held[KEYS + 1] = rest + jnp.where(late, 1, 0)

    def one(t):
        enlist(t)
        s = source[0, t]
        d = jnp.where(t < live, dest[0, t], DESTS)
        a = tiles[t]
        hi, lo = split(a)
        p = mm(jnp.concatenate([hi, lo, hi], axis=1), xs[s])
        acc[d, 0:TILE, :] += p[:, 0:TILE]
        acc[d, TILE : 2 * TILE, :] += p[:, TILE:]
        total[d] += a

    def group(g, _):
        for u in range(UNROLL):
            one(g * UNROLL + u)
        return 0

    def chunk(c, _):
        tile_copy(tiles_hbm, tiles, sems, c).wait()
        per = CHUNK // UNROLL
        return lax.fori_loop(c * per, (c + 1) * per, group, 0)

    lax.fori_loop(0, CHUNKS, chunk, 0)
    ones = jnp.ones((8, 2 * TILE), BF16)
    per = DESTS // 8

    def write(g):
        at = pl.ds(g * per, per)
        return pltpu.make_async_copy(acc.at[at], out_hbm.at[at], out_sem.at[g])

    def degrees(g, _):
        for u in range(per):
            d = g * per + u
            hi, lo = split(total[d])
            acc[d, 2 * TILE :, :] = mm(ones, jnp.concatenate([hi, lo], axis=1), ((1,), (1,)))
        write(g).start()
        return 0

    lax.fori_loop(0, 8, degrees, 0)

    def counts(k, _):
        plan[PLAN_COUNT + k] = jnp.minimum(held[k], FIT)
        return 0

    lax.fori_loop(0, KEYS, counts, 0)
    plan[PLAN_REST] = held[KEYS + 1]
    for g in range(8):
        write(g).wait()


def forward_tiles(dest, source, keys, count, slab, values):
    return pl.pallas_call(
        forward_kernel,
        out_shape=(jax.ShapeDtypeStruct((DESTS, ROWS, TILE), F32), jax.ShapeDtypeStruct((PLAN_SIZE,), jnp.int32)),
        in_specs=[SM, SM, SM, SM, VM, ANY],
        out_specs=(ANY, SM),
        scratch_shapes=[
            pltpu.VMEM((SLOTS, TILE, TILE), F32),
            pltpu.VMEM((DESTS + 1, ROWS, TILE), F32),
            pltpu.VMEM((DESTS + 1, TILE, TILE), F32),
            pltpu.VMEM((SOURCES, 3 * TILE, WIDTH), BF16),
            pltpu.SMEM((KEYS + 2,), jnp.int32),
            DMA((CHUNKS,)),
            DMA((8,)),
        ],
        compiler_params=pltpu.CompilerParams(vmem_limit_bytes=VMEM_LIMIT),
        cost_estimate=pl.CostEstimate(
            flops=SLOTS * 6 * TILE * TILE * WIDTH, bytes_accessed=22_000_000, transcendentals=0
        ),
        name="forward_tiles",
    )(dest, source, keys, count, slab, values)


def rms_silu(pre, cot):
    sig = 1.0 / (1.0 + jnp.exp(-pre))
    s = pre * sig
    r = lax.rsqrt(jnp.mean(s * s, axis=-1, keepdims=True) + EPSILON)
    inner = jnp.mean(cot * s, axis=-1, keepdims=True)
    ds = r * cot - s * (r * r * r * inner)
    return s * r, ds * sig * (1.0 + pre * (1.0 - sig))


PARTS = 32
PART_ROWS = 40
AR_SENDS = 10
FIRST = 64
SUM_ROWS = (((0, 136), (136, 128)), ((FIRST, 104), (FIRST + 104, 96)))
GATH_ROWS = (((0, 128), (128, 128)), ((FIRST, 96), (FIRST + 96, 96)))
SLICES = 20


def exchange_kernel(
    plan, part_hbm, x_ref, ws_ref, wn_ref, bias_ref, cot_ref, tiles_hbm,
    layer_out, direct_out, g_out, gw_out, back_out,
    acc, relays, arrivals, zfirst, zlast, g0, g1, g2, g3, tiles, own_term, gwp, r1, r2, r3, r4, own_part,
    load_sem, rs_send, rs_recv, zs_send, zs_recv, ag_send, ag_recv, zg_send, zg_recv, ar_send, ar_recv, out_sem, tile_sem,
):
    quarters = (g0, g1, g2, g3)
    row, col = lax.axis_index("row"), lax.axis_index("col")
    zh, core = lax.div(row, 2), lax.rem(row, 2)
    x, y, z = lax.div(col, 8), lax.rem(lax.div(col, 2), 4), lax.rem(col, 2)
    column = lambda xx, yy, zz: xx * 8 + yy * 2 + zz
    ahead = lambda p, d: lax.rem(p + d, 4)
    x_others = [(row, column(ahead(x, d), y, z)) for d in range(1, 4)]
    y_others = [(row, column(x, ahead(y, d), z)) for d in range(1, 4)]
    z_mate = (row, column(x, y, 1 - z))
    core_mate = (zh * 2 + (1 - core), col)
    far = (1 - zh) * 2 + core
    z_others = [z_mate, (far, col), (far, column(x, y, 1 - z))]
    zs = (z, 1 - z)

    def index(order, wide, narrow, mine):
        xx, yy = (wide, narrow) if order == 0 else (narrow, wide)
        return (xx, yy, zs[mine], order)

    def at_place(order, w, which, mine, j):
        p, q = (x, y) if order == 0 else (y, x)
        return index(order, ahead(p, j), ahead(q, which), mine) if w == 0 else index(order, p, ahead(q, j), mine)

    def ring(order, w):
        others = x_others if order == w else y_others
        return others[0], others[2]

    def number(order, w, which, mine):
        return (order * 2 + mine) * 5 + (which if w == 0 else 4)

    class Sum:
        def __init__(self, order, w, which, mine):
            self.n = number(order, w, which, mine)
            self.blk = lambda j: at_place(order, w, which, mine, j % 4)
            self.top, self.low = SUM_ROWS[mine]
            up, down = ring(order, w)
            self.copies = []
            for i, (j, rows, to, device) in enumerate(
                (
                    (2, self.top, relays.at[self.n, 0, pl.ds(0, self.top[1])], up),
                    (2, self.low, relays.at[self.n, 1, pl.ds(0, self.low[1])], down),
                    (1, self.low, arrivals.at[self.n, 0, pl.ds(*self.low)], up),
                    (3, self.top, arrivals.at[self.n, 1, pl.ds(*self.top)], down),
                    (1, self.top, arrivals.at[self.n, 0, pl.ds(*self.top)], up),
                    (3, self.low, arrivals.at[self.n, 1, pl.ds(*self.low)], down),
                )
            ):
                src = acc.at[(*self.blk(j), pl.ds(*rows))]
                self.copies.append(remote(src, to, rs_send.at[self.n, i], rs_recv.at[self.n, i], device))

        def issue(self):
            for c in self.copies[:4]:
                c.start()

        def relay(self):
            for i, (j, rows) in enumerate(((1, self.top), (3, self.low))):
                self.copies[i].wait_recv()
                at = (*self.blk(j), pl.ds(*rows), slice(None))
                acc[at] += relays[self.n, i, 0 : rows[1], :]
                self.copies[4 + i].start()

        def finish(self):
            for c in self.copies[2:]:
                c.wait_recv()
            rows = pl.ds(self.top[0], self.top[1] + self.low[1])
            at = (*self.blk(0), rows, slice(None))
            acc[at] += arrivals[self.n, 0, rows, :] + arrivals[self.n, 1, rows, :]

        def drain(self):
            for c in self.copies:
                c.wait_send()

    def quarter_of(which, mine):
        return mine * 2 + which // 2, (which & 1) ^ (which // 2)

    def held(order, wide, which, mine):
        quarter, local = quarter_of(which, mine)
        return quarters[quarter].at[local, wide, order]

    class Gather:
        def __init__(self, order, w, which, mine):
            n = number(order, w, which, mine)
            p = x if order == 0 else y

            def blk(j):
                return held(order, ahead(p, j), which, mine) if w == 0 else held(order, p, j, mine)

            top, low = GATH_ROWS[mine]
            up, down = ring(order, w)
            self.out, self.come = [], []
            for i, (leaves, comes, rows, device) in enumerate(
                (
                    (0, 3, top, up),
                    (0, 1, low, down),
                    (0, 3, low, up),
                    (0, 1, top, down),
                    (3, 2, top, up),
                    (1, 2, low, down),
                )
            ):
                src, come = blk(leaves).at[pl.ds(*rows)], blk(comes).at[pl.ds(*rows)]
                dst = src if w == 0 else come
                self.out.append(remote(src, dst, ag_send.at[n, i], ag_recv.at[n, i], device))
                self.come.append(remote(come, come, ag_send.at[n, i], ag_recv.at[n, i], device))

        def issue(self):
            for c in self.out[:4]:
                c.start()

        def relay(self):
            for i in range(2):
                self.come[i].wait_recv()
                self.out[4 + i].start()

        def near(self):
            for c in self.come[2:4]:
                c.wait_recv()

        def finish(self):
            for c in self.come[4:]:
                c.wait_recv()

        def drain(self):
            for c in self.out:
                c.wait_send()

    def strip(ref, order, which, mine, rows=None):
        q = ahead(y if order == 0 else x, which)
        lead = (slice(None), q) if order == 0 else (q, slice(None))
        return ref.at[(*lead, zs[mine], order) + (() if rows is None else (pl.ds(*rows),))]

    def load(order, which, mine):
        n = order * 8 + mine * 4 + which
        return pltpu.make_async_copy(strip(part_hbm, order, which, mine), strip(acc, order, which, mine), load_sem.at[n])

    def z_first(order, which):
        to = zfirst.at[order, which]
        i = order * 4 + which
        return remote(strip(part_hbm, order, which, 1, (0, FIRST)), to, zs_send.at[i], zs_recv.at[i], z_mate)

    def z_last(order):
        rows = pl.ds(FIRST, ROWS - FIRST)
        src = acc.at[(*at_place(order, 0, 0, 1, 0), rows)]
        return remote(src, zlast.at[order, rows], zs_send.at[8 + order], zs_recv.at[8 + order], z_mate)

    turn = [(2, 1), (1, 1), (3, 1), (2, 0), (0, 1), (1, 0), (3, 0), (0, 0)]
    peers = [core_mate] + x_others + y_others + z_others
    greet(peers)
    for which, mine in turn:
        for order in range(2):
            load(order, which, mine).start()
    tile_load = pltpu.make_async_copy(tiles_hbm, tiles, tile_sem)
    tile_load.start()
    enter(peers)
    for which in (2, 1, 3, 0):
        for order in range(2):
            z_first(order, which).start()

    wide = [[Sum(order, 0, which, mine) for order in range(2)] for which, mine in turn]
    narrow = [[Sum(order, 1, 0, mine) for order in range(2)] for mine in range(2)]

    def each(pair, action):
        for s in pair:
            getattr(s, action)()

    def sum_issue(i):
        which, mine = turn[i]
        for order in range(2):
            load(order, which, mine).wait()
            if mine == 0:
                z_first(order, which).wait_recv()
                p = y if order == 0 else x
                for j in range(4):
                    at = (*index(order, j, ahead(p, which), 0), pl.ds(0, FIRST), slice(None))
                    acc[at] += zfirst[order, which, j]
            wide[i][order].issue()

    for i in range(len(turn) + 1):
        if i < len(turn):
            sum_issue(i)
        if i == 0:
            own_term[...] = dot3(x_ref[...], ws_ref[...])
        if i >= 1:
            each(wide[i - 1], "relay")
        if i == 5:
            for n in range(3):
                each(wide[n], "finish")
            each(narrow[1], "issue")
        if i == 6:
            each(narrow[1], "relay")
        if i == 7:
            each(wide[4], "finish")
            each(narrow[1], "finish")
            for order in range(2):
                z_last(order).start()
    for n in (3, 5, 6):
        each(wide[n], "finish")
    each(narrow[0], "issue")
    each(wide[7], "finish")
    each(narrow[0], "relay")
    each(narrow[0], "finish")

    x_own = x_ref[...]
    ws, wn = ws_ref[...], wn_ref[...]
    sums, inv = [], []
    for order in range(2):
        z_last(order).wait_recv()
        own = at_place(order, 0, 0, 0, 0)
        s = jnp.concatenate([acc[(*own, pl.ds(0, FIRST))], acc[(*own, pl.ds(FIRST, ROWS - FIRST))] + zlast[order, FIRST:, :]], axis=0)
        degree = jnp.transpose(jnp.broadcast_to(s[2 * TILE : 2 * TILE + 1, :], (TILE, TILE)))
        root = lax.rsqrt(1.0 + degree)
        inv.append(jnp.concatenate([root, root], axis=1))
        sums.append(jnp.concatenate([s[0:TILE], s[TILE : 2 * TILE]], axis=1))
    inv = jnp.concatenate(inv, axis=0)
    neighbour = jnp.concatenate(sums, axis=0) * inv
    pre = own_term[...] + dot3(neighbour, wn) + bias_ref[...]
    out, grad_pre = rms_silu(pre, cot_ref[...])
    layer_out[...] = out
    spread = dot3(grad_pre, wn, ((1,), (1,))) * inv
    for order in range(2):
        for half in range(2):
            held(order, x if order == 0 else y, 0, 0)[half * TILE : (half + 1) * TILE, :] = spread[
                order * TILE : (order + 1) * TILE, half * TILE : (half + 1) * TILE
            ]

    def give(order):
        src, dst = [held(order, x if order == 0 else y, 0, mine).at[pl.ds(FIRST, 2 * TILE - FIRST)] for mine in range(2)]
        return remote(src, dst, zg_send.at[8 + order], zg_recv.at[8 + order], z_mate)

    def strip_held(order, which, mine):
        quarter, local = quarter_of(which, mine)
        return quarters[quarter].at[local, :, order]

    def z_after(order, which):
        i = order * 4 + which
        src, dst = [strip_held(order, which, mine).at[:, pl.ds(0, FIRST)] for mine in range(2)]
        return remote(src, dst, zg_send.at[i], zg_recv.at[i], z_mate)

    def write(order, which, mine):
        n = order * 8 + mine * 4 + which
        quarter, local = quarter_of(which, mine)
        return pltpu.make_async_copy(strip_held(order, which, mine), g_out.at[quarter, local, :, order], out_sem.at[n])

    def products(quarter, sources):
        for s in sources:
            key = quarter * SOURCES + s
            n = plan[PLAN_COUNT + key]
            total = None
            for i in range(FIT):
                t, b = plan[PLAN_TILE + key * FIT + i], plan[PLAN_BLOCK + key * FIT + i]
                a = tiles[t] * jnp.where(i < n, 1.0, 0.0)
                hi, lo = split(a)
                g = quarters[quarter][lax.shift_right_logical(b, 3) & 1, lax.shift_right_logical(b, 1) & 3, b & 1]
                ghi, glo = split(jnp.concatenate([g[0:TILE], g[TILE:]], axis=1))
                p = mm(jnp.concatenate([hi, lo, hi], axis=0), jnp.concatenate([ghi, ghi, glo], axis=0), ((0,), (0,)))
                total = p if total is None else total + p
            at = slice(s * TILE, (s + 1) * TILE)
            back_out[at, :] = total if quarter == 0 else back_out[at, :] + total

    gwide = {(which, mine): [Gather(order, 0, which, mine) for order in range(2)] for which in range(4) for mine in range(2)}
    gnarrow = [[Gather(order, 1, 0, mine) for order in range(2)] for mine in range(2)]

    def done(which, mine):
        each(gwide[which, mine], "near")
        each(gwide[which, mine], "finish")
        for order in range(2):
            if mine == 0:
                z_after(order, which).start()
                write(order, which, 0).start()

    for order in range(2):
        give(order).start()
    each(gnarrow[0], "issue")
    each(gwide[0, 0], "issue")

    gs = dot3(x_own, grad_pre, ((0,), (0,)))
    gn = dot3(neighbour, grad_pre, ((0,), (0,)))
    flat = [gs[:, 0:TILE], gs[:, TILE:], gn[:, 0:TILE], gn[:, TILE:]]
    gb = jnp.sum(grad_pre, axis=0, keepdims=True)
    blank = jnp.zeros((PARTS * PART_ROWS - 4 * WIDTH - 2, TILE), F32)
    gwp[...] = jnp.concatenate(flat + [gb[:, 0:TILE], gb[:, TILE:], blank], axis=0).reshape(gwp.shape)

    hop = lambda i, src, dst, device: remote(src, dst, ar_send.at[i], ar_recv.at[i], device)
    zg = zh * 2 + z
    c1 = [hop(0, gwp.at[1 - core], r1, core_mate)]
    z_ring = []
    for d in range(1, 4):
        to = ahead(zg, d)
        z_ring.append((lax.div(to, 2) * 2 + core, column(x, y, lax.rem(to, 2))))
    c2 = [hop(d, gwp.at[core, :, ahead(zg, d)], r2.at[d - 1], z_ring[d - 1]) for d in range(1, 4)]
    c3 = [hop(3 + d, gwp.at[core, ahead(x, d), zg], r3.at[d - 1], x_others[d - 1]) for d in range(1, 4)]
    c4 = [hop(6 + d, own_part, r4.at[y], y_others[d - 1]) for d in range(1, 4)]
    c4_come = [hop(6 + d, own_part, r4.at[ahead(y, 4 - d)], y_others[d - 1]) for d in range(1, 4)]

    def launch(copies):
        for c in copies:
            c.start()

    def land(copies):
        for c in copies:
            c.wait()

    def phase1():
        land(c1)
        gwp[core] += r1[...]
        launch(c2)

    def phase2():
        land(c2)
        gwp[core, :, zg] += (r2[0] + r2[1]) + r2[2]
        launch(c3)

    def phase3():
        land(c3)
        own_part[...] = gwp[core, x, zg] + r3[0] + r3[1] + r3[2]
        launch(c4)

    def phase4():
        for c in c4_come:
            c.wait_recv()
        for c in c4:
            c.wait_send()
        terms = [jnp.where(y == i, own_part[...], r4[i]) for i in range(4)]
        gw_out[...] = (terms[0] + terms[1]) + (terms[2] + terms[3])

    launch(c1)
    direct_out[...] = dot3(grad_pre, ws, ((1,), (1,)))

    each(gnarrow[0], "relay")
    each(gwide[0, 0], "relay")
    each(gnarrow[0], "near")
    each(gwide[1, 0], "issue")
    for order in range(2):
        give(order).wait_recv()
    each(gnarrow[1], "issue")
    each(gwide[3, 0], "issue")
    each(gwide[1, 0], "relay")
    phase1()
    each(gnarrow[1], "relay")
    each(gnarrow[0], "finish")
    each(gwide[2, 0], "issue")
    each(gwide[3, 0], "relay")
    done(0, 0)
    each(gwide[0, 1], "issue")
    each(gwide[2, 0], "relay")
    done(1, 0)
    each(gnarrow[1], "near")
    each(gwide[1, 1], "issue")
    each(gwide[0, 1], "relay")
    tile_load.wait()
    products(0, (0, 1, 2))
    done(3, 0)
    phase2()
    each(gnarrow[1], "finish")
    each(gwide[3, 1], "issue")
    each(gwide[1, 1], "relay")
    products(0, (3, 4, 5))
    done(2, 0)
    each(gwide[2, 1], "issue")
    each(gwide[3, 1], "relay")
    products(0, (6, 7))
    phase3()
    each(gwide[2, 1], "relay")
    products(1, (0, 1, 2, 3))
    for which in range(4):
        if which == 2:
            products(1, (4, 5, 6, 7))
            products(2, range(SOURCES))
        done(which, 1)
        for order in range(2):
            z_after(order, which).wait_recv()
            write(order, which, 1).start()
    products(3, range(SOURCES))
    phase4()

    for pair in wide + narrow + list(gwide.values()) + gnarrow:
        each(pair, "drain")
    for order in range(2):
        z_last(order).wait_send()
        give(order).wait_send()
        for which in range(4):
            z_first(order, which).wait_send()
            z_after(order, which).wait_send()
    for which in range(4):
        for order in range(2):
            for own_z in range(2):
                write(order, which, own_z).wait()


def exchange(plan, part, x, ws, wn, bias, cot, values):
    n = x.shape[0]
    layout = (4, 4, 2, 2)
    out = pl.pallas_call(
        exchange_kernel,
        out_shape=(
            jax.ShapeDtypeStruct((n, WIDTH), F32),
            jax.ShapeDtypeStruct((n, WIDTH), F32),
            jax.ShapeDtypeStruct((4, 2, 4, 2, 2 * TILE, TILE), F32),
            jax.ShapeDtypeStruct((PART_ROWS, TILE), F32),
            jax.ShapeDtypeStruct((SOURCES * TILE, WIDTH), F32),
        ),
        in_specs=[SM, ANY, VM, VM, VM, VM, VM, ANY],
        out_specs=(VM, VM, ANY, VM, VM),
        scratch_shapes=[
            pltpu.VMEM((*layout, ROWS, TILE), F32),
            pltpu.VMEM((SLICES, 2, 136, TILE), F32),
            pltpu.VMEM((SLICES, 2, ROWS, TILE), F32),
            pltpu.VMEM((2, 4, 4, FIRST, TILE), F32),
            pltpu.VMEM((2, ROWS, TILE), F32),
            *[pltpu.VMEM((2, 4, 2, 2 * TILE, TILE), F32) for _ in range(4)],
            pltpu.VMEM((SLOTS, TILE, TILE), F32),
            pltpu.VMEM((n, WIDTH), F32),
            pltpu.VMEM((2, 4, 4, PART_ROWS, TILE), F32),
            pltpu.VMEM((4, 4, PART_ROWS, TILE), F32),
            pltpu.VMEM((3, 4, PART_ROWS, TILE), F32),
            pltpu.VMEM((3, PART_ROWS, TILE), F32),
            pltpu.VMEM((4, PART_ROWS, TILE), F32),
            pltpu.VMEM((PART_ROWS, TILE), F32),
            DMA((16,)),
            DMA((SLICES, 6)),
            DMA((SLICES, 6)),
            DMA((10,)),
            DMA((10,)),
            DMA((SLICES, 6)),
            DMA((SLICES, 6)),
            DMA((10,)),
            DMA((10,)),
            DMA((AR_SENDS,)),
            DMA((AR_SENDS,)),
            DMA((16,)),
            DMA,
        ],
        compiler_params=pltpu.CompilerParams(
            collective_id=1, has_side_effects=True, vmem_limit_bytes=VMEM_LIMIT
        ),
        name="exchange",
    )(plan, part.reshape(*layout, ROWS, TILE), x, ws, wn, bias.reshape(1, WIDTH), cot, values)
    layer_out, direct, g, gw, back = out
    return layer_out, direct, g.reshape(DESTS, 2 * TILE, TILE), gw, back


def rest_kernel(
    plan, source, keys, g_hbm, tiles_hbm, back_ref, out_ref, tiles, g, tile_sem, g_sem
):
    n = plan[PLAN_REST]

    def copies(i):
        slot = lax.rem(i, REST_SLOTS)
        t = plan[PLAN_LIST + i]
        return (
            pltpu.make_async_copy(tiles_hbm.at[t], tiles.at[slot], tile_sem.at[slot]),
            pltpu.make_async_copy(g_hbm.at[keys[1, t]], g.at[slot], g_sem.at[slot]),
        )

    def begin(i, _):
        for c in copies(i):
            c.start()
        return 0

    lax.fori_loop(0, jnp.minimum(n, REST_SLOTS), begin, 0)
    out_ref[...] = back_ref[...]

    def some(k, _):
        first = k * REST_UNROLL
        for u in range(REST_UNROLL):

            @pl.when(first + u < n)
            def _():
                for c in copies(first + u):
                    c.wait()

        products = []
        for u in range(REST_UNROLL):
            i = jnp.minimum(first + u, n - 1)
            slot = lax.rem(i, REST_SLOTS)
            hi, lo = split(tiles[slot] * jnp.where(first + u < n, 1.0, 0.0))
            ghi, glo = split(jnp.concatenate([g[slot, 0:TILE, :], g[slot, TILE:, :]], axis=1))
            a = jnp.concatenate([hi, lo, hi], axis=0)
            products.append((i, mm(a, jnp.concatenate([ghi, ghi, glo], axis=0), ((0,), (0,)))))
        for i, p in products:
            rows = pl.ds(pl.multiple_of(source[0, plan[PLAN_LIST + i]] * TILE, TILE), TILE)
            out_ref[rows, :] += p
        for u in range(REST_UNROLL):

            @pl.when(first + u + REST_SLOTS < n)
            def _():
                begin(first + u + REST_SLOTS, 0)

        return 0

    lax.fori_loop(0, lax.div(n + REST_UNROLL - 1, REST_UNROLL), some, 0)


def backward_rest(plan, source, keys, g, values, back):
    return pl.pallas_call(
        rest_kernel,
        out_shape=jax.ShapeDtypeStruct(back.shape, F32),
        in_specs=[SM, SM, SM, ANY, ANY, VM],
        out_specs=VM,
        scratch_shapes=[
            pltpu.VMEM((REST_SLOTS, TILE, TILE), F32),
            pltpu.VMEM((REST_SLOTS, 2 * TILE, TILE), F32),
            DMA((REST_SLOTS,)),
            DMA((REST_SLOTS,)),
        ],
        compiler_params=pltpu.CompilerParams(vmem_limit_bytes=VMEM_LIMIT),
        name="backward_rest",
    )(plan, source, keys, g, values, back)


def scatter_kernel(
    back_hbm, part_ref, out_hbm, gw_hbm,
    back_ref, out_ref, near, cross, send_buf, gws, send, recv, ar_send, ar_recv, load_sem, out_sem,
):
    row, col = lax.axis_index("row"), lax.axis_index("col")
    hi, core = lax.div(row, 2), lax.rem(row, 2)
    x, y, z = lax.div(col, 8), lax.rem(lax.div(col, 2), 4), lax.rem(col, 2)
    column = lambda xx, yy, zz: xx * 8 + yy * 2 + zz
    ahead = lambda p, d: lax.rem(p + d, 4)
    x_others = [(row, column(ahead(x, d), y, z)) for d in range(1, 4)]
    zg = hi * 2 + z
    z_others = []
    for d in range(1, 4):
        to = ahead(zg, d)
        z_others.append((lax.div(to, 2) * 2 + core, column(x, y, lax.rem(to, 2))))
    mate = (hi * 2 + (1 - core), col)
    far = z_others[1]
    peers = [mate] + x_others + z_others
    greet(peers)
    load = pltpu.make_async_copy(back_hbm, back_ref, load_sem)
    load.start()
    enter(peers)
    n = out_ref.shape[0]
    m = n // PIECES
    at = lambda r, c: pl.ds(pl.multiple_of(r * n + c * m, m), m)
    piece = lambda c: pl.ds(c * m, m)
    far_row, far_mate = (1 - hi) * 2 + core, (1 - hi) * 2 + (1 - core)
    write = lambda c: pltpu.make_async_copy(out_ref.at[piece(c)], out_hbm.at[piece(c)], out_sem.at[c])
    first, second, third = [], [], []
    for c in range(PIECES):
        src = back_ref.at[at(far_mate, c)]
        first.append(remote(src, near.at[0, piece(c)], send.at[0, c], recv.at[0, c], mate))
        src = back_ref.at[at(hi * 2 + (1 - core), c)]
        second.append(remote(src, near.at[1, piece(c)], send.at[1, c], recv.at[1, c], mate))
        third.append(remote(send_buf.at[piece(c)], cross.at[piece(c)], send.at[2, c], recv.at[2, c], far))
    load.wait()
    for c in first + second:
        c.start()

    hop = lambda i, ref, device: remote(ref, ref, ar_send.at[i], ar_recv.at[i], device)
    gws[core, x, zg] = part_ref[...]
    c5 = [hop(d, gws.at[core, x, zg], z_others[d]) for d in range(3)]
    c6 = [hop(3 + d, gws.at[core, x], x_others[d]) for d in range(3)]
    c7 = [hop(6, gws.at[core], mate)]
    for c in c5:
        c.start()
    for c in range(PIECES):
        first[c].wait_recv()
        send_buf[piece(c), :] = back_ref[at(far_row, c), :] + near[0, piece(c), :]
        third[c].start()
    for d in range(3):
        hop(d, gws.at[core, x, ahead(zg, 3 - d)], z_others[d]).wait_recv()
    for c in c6:
        c.start()
    for d in range(3):
        hop(3 + d, gws.at[core, ahead(x, 3 - d)], x_others[d]).wait_recv()
    for c in c7:
        c.start()
    for c in range(PIECES):
        second[c].wait_recv()
        third[c].wait_recv()
        out_ref[piece(c), :] = back_ref[at(row, c), :] + near[1, piece(c), :] + cross[piece(c), :]
        write(c).start()
    hop(6, gws.at[1 - core], mate).wait_recv()
    gw_write = pltpu.make_async_copy(gws, gw_hbm, out_sem.at[PIECES])
    gw_write.start()
    for c in range(PIECES):
        write(c).wait()
    gw_write.wait()
    for c in first + second + third + c5 + c6 + c7:
        c.wait_send()


def scatter_rows(back, part):
    n = back.shape[0] // 4
    parts = (2, 4, 4, PART_ROWS, TILE)
    back, gw = pl.pallas_call(
        scatter_kernel,
        out_shape=(jax.ShapeDtypeStruct((n, WIDTH), F32), jax.ShapeDtypeStruct(parts, F32)),
        in_specs=[ANY, VM],
        out_specs=(ANY, ANY),
        scratch_shapes=[
            pltpu.VMEM(back.shape, F32),
            pltpu.VMEM((n, WIDTH), F32),
            pltpu.VMEM((2, n, WIDTH), F32),
            pltpu.VMEM((n, WIDTH), F32),
            pltpu.VMEM((n, WIDTH), F32),
            pltpu.VMEM(parts, F32),
            DMA((3, PIECES)),
            DMA((3, PIECES)),
            DMA((7,)),
            DMA((7,)),
            DMA,
            DMA((PIECES + 1,)),
        ],
        compiler_params=pltpu.CompilerParams(collective_id=2, has_side_effects=True),
        name="scatter_rows",
    )(back, part)
    return back, gw.reshape(PARTS * PART_ROWS, TILE)


def finish_kernel(kept, direct, back, gw, kept_out, grad_x, grad_ws, grad_wn, grad_bias):
    kept_out[...] = kept[...]
    grad_x[...] = direct[...] + back[...]
    for i, out in enumerate((grad_ws, grad_wn)):
        for half in range(2):
            first = (2 * i + half) * WIDTH
            out[:, half * TILE : (half + 1) * TILE] = gw[first : first + WIDTH, :]
    for half in range(2):
        grad_bias[:, half * TILE : (half + 1) * TILE] = gw[4 * WIDTH + half : 4 * WIDTH + half + 1, :]


def finish(kept, direct, back, gw):
    rows, square = jax.ShapeDtypeStruct(direct.shape, F32), jax.ShapeDtypeStruct((WIDTH, WIDTH), F32)
    return pl.pallas_call(
        finish_kernel,
        out_shape=(rows, rows, square, square, jax.ShapeDtypeStruct((1, WIDTH), F32)),
        in_specs=[VM] * 4,
        out_specs=(VM,) * 5,
        name="finish",
    )(kept, direct, back, gw)


def body(x, ws, wn, bias, tile_values, tile_dest, tile_source, tile_count, cot):
    values = tile_values.reshape(SLOTS, TILE, TILE)
    dest, source = tile_dest.reshape(1, SLOTS), tile_source.reshape(1, SLOTS)
    count = tile_count.reshape(1)
    slab, keys = gather_rows(count, dest, source, x)
    part, plan = forward_tiles(dest, source, keys, count, slab, values)
    layer_out, direct, g, gw_part, back = exchange(plan, part, x, ws, wn, bias, cot, values)
    back = backward_rest(plan, source, keys, g, values, back)
    back, gw = scatter_rows(back, gw_part)
    layer_out, grad_x, grad_ws, grad_wn, grad_bias = finish(layer_out, direct, back, gw)
    return layer_out, grad_x, grad_ws, grad_wn, grad_bias.reshape(WIDTH)


def solution(mesh):
    in_specs = (
        P(("col", "row"), None),
        P(),
        P(),
        P(),
        P("row", "col", None, None, None),
        P("row", "col", None),
        P("row", "col", None),
        P("row", "col"),
        P(("col", "row"), None),
    )
    out_specs = (P(("col", "row"), None), P(("col", "row"), None), P(), P(), P())
    return jax.shard_map(body, mesh=mesh, in_specs=in_specs, out_specs=out_specs, check_vma=False)
```

```python
import functools

import jax
import jax.numpy as jnp
from jax import lax
from jax.experimental import pallas as pl
from jax.experimental.pallas import tpu as pltpu
from jax.sharding import PartitionSpec as P

EPSILON = 1e-05
F32 = jnp.float32
BF16 = jnp.bfloat16
MESH = pl.DeviceIdType.MESH
TILE = 128
WIDTH = 256
SLOTS = 192
DESTS = 64
SOURCES = 8
ROWS = 264
CHUNK = 16
CHUNKS = SLOTS // CHUNK
UNROLL = 16
PIECES = 4
FIT = 8
KEYS = 4 * SOURCES
PLAN_TILE, PLAN_BLOCK, PLAN_COUNT = 0, KEYS * FIT, 2 * KEYS * FIT
PLAN_REST, PLAN_LIST = PLAN_COUNT + KEYS, PLAN_COUNT + 2 * KEYS
PLAN_SIZE = 1024
PLAN_VOID = PLAN_SIZE - 1
REST_SLOTS = 16
REST_UNROLL = 4
VMEM_LIMIT = 60 * 1024 * 1024

VM = pl.BlockSpec(memory_space=pltpu.VMEM)
SM = pl.BlockSpec(memory_space=pltpu.SMEM)
ANY = pl.BlockSpec(memory_space=pl.ANY)
DMA = pltpu.SemaphoreType.DMA


def split(a):
    hi = a.astype(BF16)
    return hi, (a - hi.astype(F32)).astype(BF16)


def mm(a, b, dims=((1,), (0,))):
    return lax.dot_general(a, b, (dims, ((), ())), preferred_element_type=F32)


def dot3(a, b, dims=((1,), (0,))):
    ah, al = split(a)
    bh, bl = split(b)
    return mm(ah, bh, dims) + (mm(ah, bl, dims) + mm(al, bh, dims))


def greet(devices):
    barrier = pltpu.get_barrier_semaphore()
    for device in devices:
        pl.semaphore_signal(barrier, inc=1, device_id=device, device_id_type=MESH)


def enter(devices):
    pl.semaphore_wait(pltpu.get_barrier_semaphore(), len(devices))


def remote(src, dst, send, recv, device):
    return pltpu.make_async_remote_copy(
        src_ref=src, dst_ref=dst, send_sem=send, recv_sem=recv, device_id=device, device_id_type=MESH
    )


def arrival(q, col):
    x, y, z = lax.div(col, 8), lax.rem(lax.div(col, 2), 4), lax.rem(col, 2)
    bx, by, order = lax.shift_right_logical(q, 4), lax.shift_right_logical(q, 2) & 3, q & 1
    other = (lax.shift_right_logical(q, 1) & 1) ^ z
    which = jnp.where(order == 0, by - y, bx - x) & 3
    wide = jnp.where(order == 0, bx, by)
    half = lax.shift_right_logical(which, 1)
    local = (which & 1) ^ half
    return other * 2 + half, (local * 4 + wide) * 2 + order


def gather_kernel(count, dest_ref, source_ref, x_ref, out_ref, keys_out, local_sem, send, recv):
    row, col = lax.axis_index("row"), lax.axis_index("col")
    hi, core = lax.div(row, 2), lax.rem(row, 2)
    mate = hi * 2 + (1 - core)
    far = (1 - hi) * 2 + core
    peers = [(mate, col), (far, col)]
    greet(peers)
    enter(peers)
    n = x_ref.shape[0]
    m = n // PIECES
    at = lambda r, c: out_ref.at[pl.ds(pl.multiple_of(r * n + c * m, m), m)]
    piece = lambda c: x_ref.at[pl.ds(c * m, m)]
    own = pltpu.make_async_copy(x_ref, out_ref.at[pl.ds(pl.multiple_of(row * n, n), n)], local_sem)
    across = [remote(piece(c), at(row, c), send.at[0, c], recv.at[0, c], (far, col)) for c in range(PIECES)]
    beside = [remote(piece(c), at(row, c), send.at[1, c], recv.at[1, c], (mate, col)) for c in range(PIECES)]
    onward = [remote(at(far, c), at(far, c), send.at[2, c], recv.at[2, c], (mate, col)) for c in range(PIECES)]
    for c in across + beside:
        c.start()
    own.start()
    dest = dest_ref[...]
    quarter, block = arrival(dest, col)
    listed = lax.broadcasted_iota(jnp.int32, dest.shape, 1) < count[0]
    keys_out[0:1, :] = jnp.where(listed, quarter * SOURCES + source_ref[...], KEYS)
    keys_out[1:2, :] = quarter * 16 + block
    for c in range(PIECES):
        across[c].wait_recv()
        onward[c].start()
    for c in beside + onward:
        c.wait_recv()
    own.wait()
    for c in across + beside + onward:
        c.wait_send()


def gather_rows(count, dest, source, x):
    return pl.pallas_call(
        gather_kernel,
        out_shape=(jax.ShapeDtypeStruct((4 * x.shape[0], x.shape[1]), F32), jax.ShapeDtypeStruct((2, SLOTS), jnp.int32)),
        in_specs=[SM, VM, VM, VM],
        out_specs=(VM, VM),
        scratch_shapes=[DMA, DMA((3, PIECES)), DMA((3, PIECES))],
        compiler_params=pltpu.CompilerParams(collective_id=0, has_side_effects=True),
        name="gather_rows",
    )(count, dest, source, x)


def tile_copy(tiles_hbm, tiles, sems, c):
    at = pl.ds(c * CHUNK, CHUNK)
    return pltpu.make_async_copy(tiles_hbm.at[at], tiles.at[at], sems.at[c])


def forward_kernel(
    dest, source, keys, count, x_ref, tiles_hbm, out_hbm, plan, tiles, acc, total, xs, held, sems, out_sem
):
    for c in range(CHUNKS):
        tile_copy(tiles_hbm, tiles, sems, c).start()
    live = count[0]
    for s in range(SOURCES):
        hi, lo = split(x_ref[s * TILE : (s + 1) * TILE, :])
        xs[s, 0:TILE, :] = hi
        xs[s, TILE : 2 * TILE, :] = hi
        xs[s, 2 * TILE :, :] = lo

    def clear(d, _):
        acc[d] = jnp.zeros((ROWS, TILE), F32)
        total[d] = jnp.zeros((TILE, TILE), F32)
        for u in range(2 * KEYS * FIT // DESTS):
            plan[jnp.minimum(d, DESTS - 1) * (2 * KEYS * FIT // DESTS) + u] = 0
        held[jnp.minimum(d, KEYS + 1)] = 0
        return 0

    lax.fori_loop(0, DESTS + 1, clear, 0)

    def enlist(t):
        key = keys[0, t]
        n, rest = held[key], held[KEYS + 1]
        late = jnp.logical_and(key < KEYS, n >= FIT)
        fits = jnp.logical_and(key < KEYS, n < FIT)
        slot = jnp.where(fits, key * FIT + n, PLAN_VOID - PLAN_BLOCK)
        plan[jnp.where(late, PLAN_LIST + rest, PLAN_TILE + slot)] = t
        plan[PLAN_BLOCK + slot] = keys[1, t]
        held[key] = n + 1
        held[KEYS + 1] = rest + jnp.where(late, 1, 0)

    def one(t):
        enlist(t)
        s = source[0, t]
        d = jnp.where(t < live, dest[0, t], DESTS)
        a = tiles[t]
        hi, lo = split(a)
        p = mm(jnp.concatenate([hi, lo, hi], axis=1), xs[s])
        acc[d, 0:TILE, :] += p[:, 0:TILE]
        acc[d, TILE : 2 * TILE, :] += p[:, TILE:]
        total[d] += a

    def group(g, _):
        for u in range(UNROLL):
            one(g * UNROLL + u)
        return 0

    def chunk(c, _):
        tile_copy(tiles_hbm, tiles, sems, c).wait()
        per = CHUNK // UNROLL
        return lax.fori_loop(c * per, (c + 1) * per, group, 0)

    lax.fori_loop(0, CHUNKS, chunk, 0)
    ones = jnp.ones((8, 2 * TILE), BF16)
    per = DESTS // 8

    def write(g):
        at = pl.ds(g * per, per)
        return pltpu.make_async_copy(acc.at[at], out_hbm.at[at], out_sem.at[g])

    def degrees(g, _):
        for u in range(per):
            d = g * per + u
            hi, lo = split(total[d])
            acc[d, 2 * TILE :, :] = mm(ones, jnp.concatenate([hi, lo], axis=1), ((1,), (1,)))
        write(g).start()
        return 0

    lax.fori_loop(0, 8, degrees, 0)

    def counts(k, _):
        plan[PLAN_COUNT + k] = jnp.minimum(held[k], FIT)
        return 0

    lax.fori_loop(0, KEYS, counts, 0)
    plan[PLAN_REST] = held[KEYS + 1]
    for g in range(8):
        write(g).wait()


def forward_tiles(dest, source, keys, count, slab, values):
    return pl.pallas_call(
        forward_kernel,
        out_shape=(jax.ShapeDtypeStruct((DESTS, ROWS, TILE), F32), jax.ShapeDtypeStruct((PLAN_SIZE,), jnp.int32)),
        in_specs=[SM, SM, SM, SM, VM, ANY],
        out_specs=(ANY, SM),
        scratch_shapes=[
            pltpu.VMEM((SLOTS, TILE, TILE), F32),
            pltpu.VMEM((DESTS + 1, ROWS, TILE), F32),
            pltpu.VMEM((DESTS + 1, TILE, TILE), F32),
            pltpu.VMEM((SOURCES, 3 * TILE, WIDTH), BF16),
            pltpu.SMEM((KEYS + 2,), jnp.int32),
            DMA((CHUNKS,)),
            DMA((8,)),
        ],
        compiler_params=pltpu.CompilerParams(vmem_limit_bytes=VMEM_LIMIT),
        cost_estimate=pl.CostEstimate(
            flops=SLOTS * 6 * TILE * TILE * WIDTH, bytes_accessed=22_000_000, transcendentals=0
        ),
        name="forward_tiles",
    )(dest, source, keys, count, slab, values)


def rms_silu(pre, cot):
    sig = 1.0 / (1.0 + jnp.exp(-pre))
    s = pre * sig
    r = lax.rsqrt(jnp.mean(s * s, axis=-1, keepdims=True) + EPSILON)
    inner = jnp.mean(cot * s, axis=-1, keepdims=True)
    ds = r * cot - s * (r * r * r * inner)
    return s * r, ds * sig * (1.0 + pre * (1.0 - sig))


PARTS = 32
PART_ROWS = 40
AR_SENDS = 10
FIRST = 64
SUM_ROWS = (((0, 136), (136, 128)), ((FIRST, 104), (FIRST + 104, 96)))
GATH_ROWS = (((0, 128), (128, 128)), ((FIRST, 96), (FIRST + 96, 96)))
SLICES = 20


def exchange_kernel(
    plan, part_hbm, x_ref, ws_ref, wn_ref, bias_ref, cot_ref, tiles_hbm,
    layer_out, direct_out, g_out, gw_out, back_out,
    acc, relays, arrivals, zfirst, zlast, g0, g1, g2, g3, tiles, own_term, gwp, r1, r2, r3, r4, own_part,
    load_sem, rs_send, rs_recv, zs_send, zs_recv, ag_send, ag_recv, zg_send, zg_recv, ar_send, ar_recv, out_sem, tile_sem,
):
    quarters = (g0, g1, g2, g3)
    row, col = lax.axis_index("row"), lax.axis_index("col")
    zh, core = lax.div(row, 2), lax.rem(row, 2)
    x, y, z = lax.div(col, 8), lax.rem(lax.div(col, 2), 4), lax.rem(col, 2)
    column = lambda xx, yy, zz: xx * 8 + yy * 2 + zz
    ahead = lambda p, d: lax.rem(p + d, 4)
    x_others = [(row, column(ahead(x, d), y, z)) for d in range(1, 4)]
    y_others = [(row, column(x, ahead(y, d), z)) for d in range(1, 4)]
    z_mate = (row, column(x, y, 1 - z))
    core_mate = (zh * 2 + (1 - core), col)
    far = (1 - zh) * 2 + core
    z_others = [z_mate, (far, col), (far, column(x, y, 1 - z))]
    zs = (z, 1 - z)

    def index(order, wide, narrow, mine):
        xx, yy = (wide, narrow) if order == 0 else (narrow, wide)
        return (xx, yy, zs[mine], order)

    def at_place(order, w, which, mine, j):
        p, q = (x, y) if order == 0 else (y, x)
        return index(order, ahead(p, j), ahead(q, which), mine) if w == 0 else index(order, p, ahead(q, j), mine)

    def ring(order, w):
        others = x_others if order == w else y_others
        return others[0], others[2]

    def number(order, w, which, mine):
        return (order * 2 + mine) * 5 + (which if w == 0 else 4)

    class Sum:
        def __init__(self, order, w, which, mine):
            self.n = number(order, w, which, mine)
            self.blk = lambda j: at_place(order, w, which, mine, j % 4)
            self.top, self.low = SUM_ROWS[mine]
            up, down = ring(order, w)
            self.copies = []
            for i, (j, rows, to, device) in enumerate(
                (
                    (2, self.top, relays.at[self.n, 0, pl.ds(0, self.top[1])], up),
                    (2, self.low, relays.at[self.n, 1, pl.ds(0, self.low[1])], down),
                    (1, self.low, arrivals.at[self.n, 0, pl.ds(*self.low)], up),
                    (3, self.top, arrivals.at[self.n, 1, pl.ds(*self.top)], down),
                    (1, self.top, arrivals.at[self.n, 0, pl.ds(*self.top)], up),
                    (3, self.low, arrivals.at[self.n, 1, pl.ds(*self.low)], down),
                )
            ):
                src = acc.at[(*self.blk(j), pl.ds(*rows))]
                self.copies.append(remote(src, to, rs_send.at[self.n], rs_recv.at[self.n, min(i, 2)], device))
            rows = pl.ds(self.top[0], self.top[1] + self.low[1])
            come, gone = arrivals.at[self.n, :, rows], acc.at[0, pl.ds(0, 3), 0, 0, rows]
            self.come = remote(come, come, rs_send.at[self.n], rs_recv.at[self.n, 2], up)
            self.gone = remote(gone, gone, rs_send.at[self.n], rs_recv.at[self.n, 2], up)

        def issue(self):
            for c in self.copies[:4]:
                c.start()

        def relay(self):
            for i, (j, rows) in enumerate(((1, self.top), (3, self.low))):
                self.copies[i].wait_recv()
                at = (*self.blk(j), pl.ds(*rows), slice(None))
                acc[at] += relays[self.n, i, 0 : rows[1], :]
                self.copies[4 + i].start()

        def finish(self):
            self.come.wait_recv()
            rows = pl.ds(self.top[0], self.top[1] + self.low[1])
            at = (*self.blk(0), rows, slice(None))
            acc[at] += arrivals[self.n, 0, rows, :] + arrivals[self.n, 1, rows, :]

        def drain(self):
            self.gone.wait_send()

    def quarter_of(which, mine):
        return mine * 2 + which // 2, (which & 1) ^ (which // 2)

    def held(order, wide, which, mine):
        quarter, local = quarter_of(which, mine)
        return quarters[quarter].at[local, wide, order]

    class Gather:
        def __init__(self, order, w, which, mine):
            n = number(order, w, which, mine)
            p = x if order == 0 else y

            def blk(j):
                return held(order, ahead(p, j), which, mine) if w == 0 else held(order, p, j, mine)

            top, low = GATH_ROWS[mine]
            up, down = ring(order, w)
            self.out, self.come = [], []
            for i, (leaves, comes, rows, device) in enumerate(
                (
                    (0, 3, top, up),
                    (0, 1, low, down),
                    (0, 3, low, up),
                    (0, 1, top, down),
                    (3, 2, top, up),
                    (1, 2, low, down),
                )
            ):
                src, come = blk(leaves).at[pl.ds(*rows)], blk(comes).at[pl.ds(*rows)]
                dst = src if w == 0 else come
                kind = i if i < 2 else i // 2 + 1
                self.out.append(remote(src, dst, ag_send.at[n], ag_recv.at[n, kind], device))
                if i < 2:
                    self.come.append(remote(come, come, ag_send.at[n], ag_recv.at[n, kind], device))
            rows = pl.ds(top[0], top[1] + low[1])
            one, three = g0.at[0, 0, 0, rows], g0.at[0, pl.ds(0, 3), 0, rows]
            self.beside = remote(one, one, ag_send.at[n], ag_recv.at[n, 2], up)
            self.across = remote(blk(2).at[rows], blk(2).at[rows], ag_send.at[n], ag_recv.at[n, 3], up)
            self.gone = remote(three, three, ag_send.at[n], ag_recv.at[n, 3], up)

        def issue(self):
            for c in self.out[:4]:
                c.start()

        def relay(self):
            for i in range(2):
                self.come[i].wait_recv()
                self.out[4 + i].start()

        def near(self):
            self.beside.wait_recv()

        def finish(self):
            self.across.wait_recv()

        def drain(self):
            self.gone.wait_send()

    def strip(ref, order, which, mine, rows=None):
        q = ahead(y if order == 0 else x, which)
        lead = (slice(None), q) if order == 0 else (q, slice(None))
        return ref.at[(*lead, zs[mine], order) + (() if rows is None else (pl.ds(*rows),))]

    def load(order, which, mine):
        n = order * 8 + mine * 4 + which
        return pltpu.make_async_copy(strip(part_hbm, order, which, mine), strip(acc, order, which, mine), load_sem.at[n])

    def z_first(order, which):
        to = zfirst.at[order, which]
        i = order * 4 + which
        return remote(strip(part_hbm, order, which, 1, (0, FIRST)), to, zs_send.at[i], zs_recv.at[i], z_mate)

    def z_last(order):
        rows = pl.ds(FIRST, ROWS - FIRST)
        src = acc.at[(*at_place(order, 0, 0, 1, 0), rows)]
        return remote(src, zlast.at[order, rows], zs_send.at[8 + order], zs_recv.at[8 + order], z_mate)

    turn = [(2, 1), (1, 1), (3, 1), (2, 0), (0, 1), (1, 0), (3, 0), (0, 0)]
    peers = [core_mate] + x_others + y_others + z_others
    greet(peers)
    for which, mine in turn:
        for order in range(2):
            load(order, which, mine).start()
    tile_load = pltpu.make_async_copy(tiles_hbm, tiles, tile_sem)
    tile_load.start()
    enter(peers)
    for which in (2, 1, 3, 0):
        for order in range(2):
            z_first(order, which).start()

    wide = [[Sum(order, 0, which, mine) for order in range(2)] for which, mine in turn]
    narrow = [[Sum(order, 1, 0, mine) for order in range(2)] for mine in range(2)]

    def each(pair, action):
        for s in pair:
            getattr(s, action)()

    def sum_issue(i):
        which, mine = turn[i]
        for order in range(2):
            load(order, which, mine).wait()
            if mine == 0:
                z_first(order, which).wait_recv()
                p = y if order == 0 else x
                for j in range(4):
                    at = (*index(order, j, ahead(p, which), 0), pl.ds(0, FIRST), slice(None))
                    acc[at] += zfirst[order, which, j]
            wide[i][order].issue()

    for i in range(len(turn) + 1):
        if i < len(turn):
            sum_issue(i)
        if i == 0:
            own_term[...] = dot3(x_ref[...], ws_ref[...])
        if i >= 1:
            each(wide[i - 1], "relay")
        if i == 5:
            for n in range(3):
                each(wide[n], "finish")
            each(narrow[1], "issue")
        if i == 6:
            each(narrow[1], "relay")
        if i == 7:
            each(wide[4], "finish")
            each(narrow[1], "finish")
            for order in range(2):
                z_last(order).start()
    for n in (3, 5, 6):
        each(wide[n], "finish")
    each(narrow[0], "issue")
    each(wide[7], "finish")
    each(narrow[0], "relay")
    each(narrow[0], "finish")

    x_own = x_ref[...]
    ws, wn = ws_ref[...], wn_ref[...]
    sums, inv = [], []
    for order in range(2):
        z_last(order).wait_recv()
        own = at_place(order, 0, 0, 0, 0)
        s = jnp.concatenate([acc[(*own, pl.ds(0, FIRST))], acc[(*own, pl.ds(FIRST, ROWS - FIRST))] + zlast[order, FIRST:, :]], axis=0)
        degree = jnp.transpose(jnp.broadcast_to(s[2 * TILE : 2 * TILE + 1, :], (TILE, TILE)))
        root = lax.rsqrt(1.0 + degree)
        inv.append(jnp.concatenate([root, root], axis=1))
        sums.append(jnp.concatenate([s[0:TILE], s[TILE : 2 * TILE]], axis=1))
    inv = jnp.concatenate(inv, axis=0)
    neighbour = jnp.concatenate(sums, axis=0) * inv
    pre = own_term[...] + dot3(neighbour, wn) + bias_ref[...]
    out, grad_pre = rms_silu(pre, cot_ref[...])
    layer_out[...] = out
    spread = dot3(grad_pre, wn, ((1,), (1,))) * inv
    for order in range(2):
        for half in range(2):
            held(order, x if order == 0 else y, 0, 0)[half * TILE : (half + 1) * TILE, :] = spread[
                order * TILE : (order + 1) * TILE, half * TILE : (half + 1) * TILE
            ]

    def give(order):
        src, dst = [held(order, x if order == 0 else y, 0, mine).at[pl.ds(FIRST, 2 * TILE - FIRST)] for mine in range(2)]
        return remote(src, dst, zg_send.at[8 + order], zg_recv.at[8 + order], z_mate)

    def strip_held(order, which, mine):
        quarter, local = quarter_of(which, mine)
        return quarters[quarter].at[local, :, order]

    def z_after(order, which):
        i = order * 4 + which
        src, dst = [strip_held(order, which, mine).at[:, pl.ds(0, FIRST)] for mine in range(2)]
        return remote(src, dst, zg_send.at[i], zg_recv.at[i], z_mate)

    def write(order, which, mine):
        n = order * 8 + mine * 4 + which
        quarter, local = quarter_of(which, mine)
        return pltpu.make_async_copy(strip_held(order, which, mine), g_out.at[quarter, local, :, order], out_sem.at[n])

    def products(quarter, sources):
        for s in sources:
            key = quarter * SOURCES + s
            n = plan[PLAN_COUNT + key]
            total = None
            for i in range(FIT):
                t, b = plan[PLAN_TILE + key * FIT + i], plan[PLAN_BLOCK + key * FIT + i]
                a = tiles[t] * jnp.where(i < n, 1.0, 0.0)
                hi, lo = split(a)
                g = quarters[quarter][lax.shift_right_logical(b, 3) & 1, lax.shift_right_logical(b, 1) & 3, b & 1]
                ghi, glo = split(jnp.concatenate([g[0:TILE], g[TILE:]], axis=1))
                p = mm(jnp.concatenate([hi, lo, hi], axis=0), jnp.concatenate([ghi, ghi, glo], axis=0), ((0,), (0,)))
                total = p if total is None else total + p
            at = slice(s * TILE, (s + 1) * TILE)
            back_out[at, :] = total if quarter == 0 else back_out[at, :] + total

    gwide = {(which, mine): [Gather(order, 0, which, mine) for order in range(2)] for which in range(4) for mine in range(2)}
    gnarrow = [[Gather(order, 1, 0, mine) for order in range(2)] for mine in range(2)]

    def done(which, mine):
        each(gwide[which, mine], "near")
        each(gwide[which, mine], "finish")
        for order in range(2):
            if mine == 0:
                z_after(order, which).start()
                write(order, which, 0).start()

    for order in range(2):
        give(order).start()
    each(gnarrow[0], "issue")
    each(gwide[0, 0], "issue")

    gs = dot3(x_own, grad_pre, ((0,), (0,)))
    gn = dot3(neighbour, grad_pre, ((0,), (0,)))
    flat = [gs[:, 0:TILE], gs[:, TILE:], gn[:, 0:TILE], gn[:, TILE:]]
    gb = jnp.sum(grad_pre, axis=0, keepdims=True)
    blank = jnp.zeros((PARTS * PART_ROWS - 4 * WIDTH - 2, TILE), F32)
    gwp[...] = jnp.concatenate(flat + [gb[:, 0:TILE], gb[:, TILE:], blank], axis=0).reshape(gwp.shape)

    hop = lambda i, src, dst, device: remote(src, dst, ar_send.at[i], ar_recv.at[i], device)
    zg = zh * 2 + z
    c1 = [hop(0, gwp.at[1 - core], r1, core_mate)]
    z_ring = []
    for d in range(1, 4):
        to = ahead(zg, d)
        z_ring.append((lax.div(to, 2) * 2 + core, column(x, y, lax.rem(to, 2))))
    c2 = [hop(d, gwp.at[core, :, ahead(zg, d)], r2.at[d - 1], z_ring[d - 1]) for d in range(1, 4)]
    c3 = [hop(3 + d, gwp.at[core, ahead(x, d), zg], r3.at[d - 1], x_others[d - 1]) for d in range(1, 4)]
    c4 = [hop(6 + d, own_part, r4.at[y], y_others[d - 1]) for d in range(1, 4)]
    c4_come = [hop(6 + d, own_part, r4.at[ahead(y, 4 - d)], y_others[d - 1]) for d in range(1, 4)]

    def launch(copies):
        for c in copies:
            c.start()

    def land(copies):
        for c in copies:
            c.wait()

    def phase1():
        land(c1)
        gwp[core] += r1[...]
        launch(c2)

    def phase2():
        land(c2)
        gwp[core, :, zg] += (r2[0] + r2[1]) + r2[2]
        launch(c3)

    def phase3():
        land(c3)
        own_part[...] = gwp[core, x, zg] + r3[0] + r3[1] + r3[2]
        launch(c4)

    def phase4():
        for c in c4_come:
            c.wait_recv()
        for c in c4:
            c.wait_send()
        terms = [jnp.where(y == i, own_part[...], r4[i]) for i in range(4)]
        gw_out[...] = (terms[0] + terms[1]) + (terms[2] + terms[3])

    launch(c1)
    direct_out[...] = dot3(grad_pre, ws, ((1,), (1,)))

    each(gnarrow[0], "relay")
    each(gwide[0, 0], "relay")
    each(gnarrow[0], "near")
    each(gwide[1, 0], "issue")
    for order in range(2):
        give(order).wait_recv()
    each(gnarrow[1], "issue")
    each(gwide[3, 0], "issue")
    each(gwide[1, 0], "relay")
    phase1()
    each(gnarrow[1], "relay")
    each(gnarrow[0], "finish")
    each(gwide[2, 0], "issue")
    each(gwide[3, 0], "relay")
    done(0, 0)
    each(gwide[0, 1], "issue")
    each(gwide[2, 0], "relay")
    done(1, 0)
    each(gnarrow[1], "near")
    each(gwide[1, 1], "issue")
    each(gwide[0, 1], "relay")
    tile_load.wait()
    products(0, (0, 1, 2))
    done(3, 0)
    phase2()
    each(gnarrow[1], "finish")
    each(gwide[3, 1], "issue")
    each(gwide[1, 1], "relay")
    products(0, (3, 4, 5))
    done(2, 0)
    each(gwide[2, 1], "issue")
    each(gwide[3, 1], "relay")
    products(0, (6, 7))
    phase3()
    each(gwide[2, 1], "relay")
    products(1, (0, 1, 2, 3))
    for which in range(4):
        if which == 2:
            products(1, (4, 5, 6, 7))
            products(2, range(SOURCES))
        done(which, 1)
        for order in range(2):
            z_after(order, which).wait_recv()
            write(order, which, 1).start()
    products(3, range(SOURCES))
    phase4()

    for pair in wide + narrow + list(gwide.values()) + gnarrow:
        each(pair, "drain")
    for order in range(2):
        z_last(order).wait_send()
        give(order).wait_send()
        for which in range(4):
            z_first(order, which).wait_send()
            z_after(order, which).wait_send()
    for which in range(4):
        for order in range(2):
            for own_z in range(2):
                write(order, which, own_z).wait()


def exchange(plan, part, x, ws, wn, bias, cot, values):
    n = x.shape[0]
    layout = (4, 4, 2, 2)
    out = pl.pallas_call(
        exchange_kernel,
        out_shape=(
            jax.ShapeDtypeStruct((n, WIDTH), F32),
            jax.ShapeDtypeStruct((n, WIDTH), F32),
            jax.ShapeDtypeStruct((4, 2, 4, 2, 2 * TILE, TILE), F32),
            jax.ShapeDtypeStruct((PART_ROWS, TILE), F32),
            jax.ShapeDtypeStruct((SOURCES * TILE, WIDTH), F32),
        ),
        in_specs=[SM, ANY, VM, VM, VM, VM, VM, ANY],
        out_specs=(VM, VM, ANY, VM, VM),
        scratch_shapes=[
            pltpu.VMEM((*layout, ROWS, TILE), F32),
            pltpu.VMEM((SLICES, 2, 136, TILE), F32),
            pltpu.VMEM((SLICES, 2, ROWS, TILE), F32),
            pltpu.VMEM((2, 4, 4, FIRST, TILE), F32),
            pltpu.VMEM((2, ROWS, TILE), F32),
            *[pltpu.VMEM((2, 4, 2, 2 * TILE, TILE), F32) for _ in range(4)],
            pltpu.VMEM((SLOTS, TILE, TILE), F32),
            pltpu.VMEM((n, WIDTH), F32),
            pltpu.VMEM((2, 4, 4, PART_ROWS, TILE), F32),
            pltpu.VMEM((4, 4, PART_ROWS, TILE), F32),
            pltpu.VMEM((3, 4, PART_ROWS, TILE), F32),
            pltpu.VMEM((3, PART_ROWS, TILE), F32),
            pltpu.VMEM((4, PART_ROWS, TILE), F32),
            pltpu.VMEM((PART_ROWS, TILE), F32),
            DMA((16,)),
            DMA((SLICES,)),
            DMA((SLICES, 3)),
            DMA((10,)),
            DMA((10,)),
            DMA((SLICES,)),
            DMA((SLICES, 4)),
            DMA((10,)),
            DMA((10,)),
            DMA((AR_SENDS,)),
            DMA((AR_SENDS,)),
            DMA((16,)),
            DMA,
        ],
        compiler_params=pltpu.CompilerParams(
            collective_id=1, has_side_effects=True, vmem_limit_bytes=VMEM_LIMIT
        ),
        name="exchange",
    )(plan, part.reshape(*layout, ROWS, TILE), x, ws, wn, bias.reshape(1, WIDTH), cot, values)
    layer_out, direct, g, gw, back = out
    return layer_out, direct, g.reshape(DESTS, 2 * TILE, TILE), gw, back


def rest_kernel(
    plan, source, keys, g_hbm, tiles_hbm, back_ref, out_ref, tiles, g, tile_sem, g_sem
):
    n = plan[PLAN_REST]

    def copies(i):
        slot = lax.rem(i, REST_SLOTS)
        t = plan[PLAN_LIST + i]
        return (
            pltpu.make_async_copy(tiles_hbm.at[t], tiles.at[slot], tile_sem.at[slot]),
            pltpu.make_async_copy(g_hbm.at[keys[1, t]], g.at[slot], g_sem.at[slot]),
        )

    def begin(i, _):
        for c in copies(i):
            c.start()
        return 0

    lax.fori_loop(0, jnp.minimum(n, REST_SLOTS), begin, 0)
    out_ref[...] = back_ref[...]

    def some(k, _):
        first = k * REST_UNROLL
        for u in range(REST_UNROLL):

            @pl.when(first + u < n)
            def _():
                for c in copies(first + u):
                    c.wait()

        products = []
        for u in range(REST_UNROLL):
            i = jnp.minimum(first + u, n - 1)
            slot = lax.rem(i, REST_SLOTS)
            hi, lo = split(tiles[slot] * jnp.where(first + u < n, 1.0, 0.0))
            ghi, glo = split(jnp.concatenate([g[slot, 0:TILE, :], g[slot, TILE:, :]], axis=1))
            a = jnp.concatenate([hi, lo, hi], axis=0)
            products.append((i, mm(a, jnp.concatenate([ghi, ghi, glo], axis=0), ((0,), (0,)))))
        for i, p in products:
            rows = pl.ds(pl.multiple_of(source[0, plan[PLAN_LIST + i]] * TILE, TILE), TILE)
            out_ref[rows, :] += p
        for u in range(REST_UNROLL):

            @pl.when(first + u + REST_SLOTS < n)
            def _():
                begin(first + u + REST_SLOTS, 0)

        return 0

    lax.fori_loop(0, lax.div(n + REST_UNROLL - 1, REST_UNROLL), some, 0)


def backward_rest(plan, source, keys, g, values, back):
    return pl.pallas_call(
        rest_kernel,
        out_shape=jax.ShapeDtypeStruct(back.shape, F32),
        in_specs=[SM, SM, SM, ANY, ANY, VM],
        out_specs=VM,
        scratch_shapes=[
            pltpu.VMEM((REST_SLOTS, TILE, TILE), F32),
            pltpu.VMEM((REST_SLOTS, 2 * TILE, TILE), F32),
            DMA((REST_SLOTS,)),
            DMA((REST_SLOTS,)),
        ],
        compiler_params=pltpu.CompilerParams(vmem_limit_bytes=VMEM_LIMIT),
        name="backward_rest",
    )(plan, source, keys, g, values, back)


def scatter_kernel(
    back_hbm, part_ref, out_hbm, gw_hbm,
    back_ref, out_ref, near, cross, send_buf, gws, send, recv, ar_send, ar_recv, load_sem, out_sem,
):
    row, col = lax.axis_index("row"), lax.axis_index("col")
    hi, core = lax.div(row, 2), lax.rem(row, 2)
    x, y, z = lax.div(col, 8), lax.rem(lax.div(col, 2), 4), lax.rem(col, 2)
    column = lambda xx, yy, zz: xx * 8 + yy * 2 + zz
    ahead = lambda p, d: lax.rem(p + d, 4)
    x_others = [(row, column(ahead(x, d), y, z)) for d in range(1, 4)]
    zg = hi * 2 + z
    z_others = []
    for d in range(1, 4):
        to = ahead(zg, d)
        z_others.append((lax.div(to, 2) * 2 + core, column(x, y, lax.rem(to, 2))))
    mate = (hi * 2 + (1 - core), col)
    far = z_others[1]
    peers = [mate] + x_others + z_others
    greet(peers)
    load = pltpu.make_async_copy(back_hbm, back_ref, load_sem)
    load.start()
    enter(peers)
    n = out_ref.shape[0]
    m = n // PIECES
    at = lambda r, c: pl.ds(pl.multiple_of(r * n + c * m, m), m)
    piece = lambda c: pl.ds(c * m, m)
    far_row, far_mate = (1 - hi) * 2 + core, (1 - hi) * 2 + (1 - core)
    write = lambda c: pltpu.make_async_copy(out_ref.at[piece(c)], out_hbm.at[piece(c)], out_sem.at[c])
    first, second, third = [], [], []
    for c in range(PIECES):
        src = back_ref.at[at(far_mate, c)]
        first.append(remote(src, near.at[0, piece(c)], send.at[0, c], recv.at[0, c], mate))
        src = back_ref.at[at(hi * 2 + (1 - core), c)]
        second.append(remote(src, near.at[1, piece(c)], send.at[1, c], recv.at[1, c], mate))
        third.append(remote(send_buf.at[piece(c)], cross.at[piece(c)], send.at[2, c], recv.at[2, c], far))
    load.wait()
    for c in first + second:
        c.start()

    hop = lambda i, ref, device: remote(ref, ref, ar_send.at[i], ar_recv.at[i], device)
    gws[core, x, zg] = part_ref[...]
    c5 = [hop(d, gws.at[core, x, zg], z_others[d]) for d in range(3)]
    c6 = [hop(3 + d, gws.at[core, x], x_others[d]) for d in range(3)]
    c7 = [hop(6, gws.at[core], mate)]
    for c in c5:
        c.start()
    for c in range(PIECES):
        first[c].wait_recv()
        send_buf[piece(c), :] = back_ref[at(far_row, c), :] + near[0, piece(c), :]
        third[c].start()
    for d in range(3):
        hop(d, gws.at[core, x, ahead(zg, 3 - d)], z_others[d]).wait_recv()
    for c in c6:
        c.start()
    for d in range(3):
        hop(3 + d, gws.at[core, ahead(x, 3 - d)], x_others[d]).wait_recv()
    for c in c7:
        c.start()
    for c in range(PIECES):
        second[c].wait_recv()
        third[c].wait_recv()
        out_ref[piece(c), :] = back_ref[at(row, c), :] + near[1, piece(c), :] + cross[piece(c), :]
        write(c).start()
    hop(6, gws.at[1 - core], mate).wait_recv()
    gw_write = pltpu.make_async_copy(gws, gw_hbm, out_sem.at[PIECES])
    gw_write.start()
    for c in range(PIECES):
        write(c).wait()
    gw_write.wait()
    for c in first + second + third + c5 + c6 + c7:
        c.wait_send()


def scatter_rows(back, part):
    n = back.shape[0] // 4
    parts = (2, 4, 4, PART_ROWS, TILE)
    back, gw = pl.pallas_call(
        scatter_kernel,
        out_shape=(jax.ShapeDtypeStruct((n, WIDTH), F32), jax.ShapeDtypeStruct(parts, F32)),
        in_specs=[ANY, VM],
        out_specs=(ANY, ANY),
        scratch_shapes=[
            pltpu.VMEM(back.shape, F32),
            pltpu.VMEM((n, WIDTH), F32),
            pltpu.VMEM((2, n, WIDTH), F32),
            pltpu.VMEM((n, WIDTH), F32),
            pltpu.VMEM((n, WIDTH), F32),
            pltpu.VMEM(parts, F32),
            DMA((3, PIECES)),
            DMA((3, PIECES)),
            DMA((7,)),
            DMA((7,)),
            DMA,
            DMA((PIECES + 1,)),
        ],
        compiler_params=pltpu.CompilerParams(collective_id=2, has_side_effects=True),
        name="scatter_rows",
    )(back, part)
    return back, gw.reshape(PARTS * PART_ROWS, TILE)


def finish_kernel(kept, direct, back, gw, kept_out, grad_x, grad_ws, grad_wn, grad_bias):
    kept_out[...] = kept[...]
    grad_x[...] = direct[...] + back[...]
    for i, out in enumerate((grad_ws, grad_wn)):
        for half in range(2):
            first = (2 * i + half) * WIDTH
            out[:, half * TILE : (half + 1) * TILE] = gw[first : first + WIDTH, :]
    for half in range(2):
        grad_bias[:, half * TILE : (half + 1) * TILE] = gw[4 * WIDTH + half : 4 * WIDTH + half + 1, :]


def finish(kept, direct, back, gw):
    rows, square = jax.ShapeDtypeStruct(direct.shape, F32), jax.ShapeDtypeStruct((WIDTH, WIDTH), F32)
    return pl.pallas_call(
        finish_kernel,
        out_shape=(rows, rows, square, square, jax.ShapeDtypeStruct((1, WIDTH), F32)),
        in_specs=[VM] * 4,
        out_specs=(VM,) * 5,
        name="finish",
    )(kept, direct, back, gw)


def body(x, ws, wn, bias, tile_values, tile_dest, tile_source, tile_count, cot):
    values = tile_values.reshape(SLOTS, TILE, TILE)
    dest, source = tile_dest.reshape(1, SLOTS), tile_source.reshape(1, SLOTS)
    count = tile_count.reshape(1)
    slab, keys = gather_rows(count, dest, source, x)
    part, plan = forward_tiles(dest, source, keys, count, slab, values)
    layer_out, direct, g, gw_part, back = exchange(plan, part, x, ws, wn, bias, cot, values)
    back = backward_rest(plan, source, keys, g, values, back)
    back, gw = scatter_rows(back, gw_part)
    layer_out, grad_x, grad_ws, grad_wn, grad_bias = finish(layer_out, direct, back, gw)
    return layer_out, grad_x, grad_ws, grad_wn, grad_bias.reshape(WIDTH)


def solution(mesh):
    in_specs = (
        P(("col", "row"), None),
        P(),
        P(),
        P(),
        P("row", "col", None, None, None),
        P("row", "col", None),
        P("row", "col", None),
        P("row", "col"),
        P(("col", "row"), None),
    )
    out_specs = (P(("col", "row"), None), P(("col", "row"), None), P(), P(), P())
    return jax.shard_map(body, mesh=mesh, in_specs=in_specs, out_specs=out_specs, check_vma=False)
```

```python
import functools

import jax
import jax.numpy as jnp
from jax import lax
from jax.experimental import pallas as pl
from jax.experimental.pallas import tpu as pltpu
from jax.sharding import PartitionSpec as P

EPSILON = 1e-05
F32 = jnp.float32
BF16 = jnp.bfloat16
MESH = pl.DeviceIdType.MESH
TILE = 128
WIDTH = 256
SLOTS = 192
DESTS = 64
SOURCES = 8
ROWS = 264
CHUNK = 16
CHUNKS = SLOTS // CHUNK
UNROLL = 16
PIECES = 4
FIT = 8
KEYS = 4 * SOURCES
PLAN_TILE, PLAN_BLOCK, PLAN_COUNT = 0, KEYS * FIT, 2 * KEYS * FIT
PLAN_REST, PLAN_LIST = PLAN_COUNT + KEYS, PLAN_COUNT + 2 * KEYS
PLAN_SIZE = 1024
PLAN_VOID = PLAN_SIZE - 1
REST_SLOTS = 16
REST_UNROLL = 4
VMEM_LIMIT = 60 * 1024 * 1024

VM = pl.BlockSpec(memory_space=pltpu.VMEM)
SM = pl.BlockSpec(memory_space=pltpu.SMEM)
ANY = pl.BlockSpec(memory_space=pl.ANY)
DMA = pltpu.SemaphoreType.DMA


def split(a):
    hi = a.astype(BF16)
    return hi, (a - hi.astype(F32)).astype(BF16)


def mm(a, b, dims=((1,), (0,))):
    return lax.dot_general(a, b, (dims, ((), ())), preferred_element_type=F32)


def dot3(a, b, dims=((1,), (0,))):
    ah, al = split(a)
    bh, bl = split(b)
    return mm(ah, bh, dims) + (mm(ah, bl, dims) + mm(al, bh, dims))


def greet(devices):
    barrier = pltpu.get_barrier_semaphore()
    for device in devices:
        pl.semaphore_signal(barrier, inc=1, device_id=device, device_id_type=MESH)


def enter(devices):
    pl.semaphore_wait(pltpu.get_barrier_semaphore(), len(devices))


def remote(src, dst, send, recv, device):
    return pltpu.make_async_remote_copy(
        src_ref=src, dst_ref=dst, send_sem=send, recv_sem=recv, device_id=device, device_id_type=MESH
    )


def arrival(q, col):
    x, y, z = lax.div(col, 8), lax.rem(lax.div(col, 2), 4), lax.rem(col, 2)
    bx, by, order = lax.shift_right_logical(q, 4), lax.shift_right_logical(q, 2) & 3, q & 1
    other = (lax.shift_right_logical(q, 1) & 1) ^ z
    which = jnp.where(order == 0, by - y, bx - x) & 3
    wide = jnp.where(order == 0, bx, by)
    half = lax.shift_right_logical(which, 1)
    local = (which & 1) ^ half
    return other * 2 + half, (local * 4 + wide) * 2 + order


def gather_kernel(count, dest_ref, source_ref, x_ref, out_ref, keys_out, local_sem, send, recv):
    row, col = lax.axis_index("row"), lax.axis_index("col")
    hi, core = lax.div(row, 2), lax.rem(row, 2)
    mate = hi * 2 + (1 - core)
    far = (1 - hi) * 2 + core
    peers = [(mate, col), (far, col)]
    greet(peers)
    enter(peers)
    n = x_ref.shape[0]
    m = n // PIECES
    at = lambda r, c: out_ref.at[pl.ds(pl.multiple_of(r * n + c * m, m), m)]
    piece = lambda c: x_ref.at[pl.ds(c * m, m)]
    own = pltpu.make_async_copy(x_ref, out_ref.at[pl.ds(pl.multiple_of(row * n, n), n)], local_sem)
    across = [remote(piece(c), at(row, c), send.at[0, c], recv.at[0, c], (far, col)) for c in range(PIECES)]
    beside = [remote(piece(c), at(row, c), send.at[1, c], recv.at[1, c], (mate, col)) for c in range(PIECES)]
    onward = [remote(at(far, c), at(far, c), send.at[2, c], recv.at[2, c], (mate, col)) for c in range(PIECES)]
    for c in across + beside:
        c.start()
    own.start()
    dest = dest_ref[...]
    quarter, block = arrival(dest, col)
    listed = lax.broadcasted_iota(jnp.int32, dest.shape, 1) < count[0]
    keys_out[0:1, :] = jnp.where(listed, quarter * SOURCES + source_ref[...], KEYS)
    keys_out[1:2, :] = quarter * 16 + block
    for c in range(PIECES):
        across[c].wait_recv()
        onward[c].start()
    for c in beside + onward:
        c.wait_recv()
    own.wait()
    for c in across + beside + onward:
        c.wait_send()


def gather_rows(count, dest, source, x):
    return pl.pallas_call(
        gather_kernel,
        out_shape=(jax.ShapeDtypeStruct((4 * x.shape[0], x.shape[1]), F32), jax.ShapeDtypeStruct((2, SLOTS), jnp.int32)),
        in_specs=[SM, VM, VM, VM],
        out_specs=(VM, VM),
        scratch_shapes=[DMA, DMA((3, PIECES)), DMA((3, PIECES))],
        compiler_params=pltpu.CompilerParams(collective_id=0, has_side_effects=True),
        name="gather_rows",
    )(count, dest, source, x)


def tile_copy(tiles_hbm, tiles, sems, c):
    at = pl.ds(c * CHUNK, CHUNK)
    return pltpu.make_async_copy(tiles_hbm.at[at], tiles.at[at], sems.at[c])


def forward_kernel(
    dest, source, keys, count, x_ref, tiles_hbm, out_hbm, plan, tiles, acc, total, xs, held, sems, out_sem
):
    for c in range(CHUNKS):
        tile_copy(tiles_hbm, tiles, sems, c).start()
    live = count[0]
    for s in range(SOURCES):
        hi, lo = split(x_ref[s * TILE : (s + 1) * TILE, :])
        xs[s, 0:TILE, :] = hi
        xs[s, TILE : 2 * TILE, :] = hi
        xs[s, 2 * TILE :, :] = lo

    def clear(d, _):
        acc[d] = jnp.zeros((ROWS, TILE), F32)
        total[d] = jnp.zeros((TILE, TILE), F32)
        for u in range(2 * KEYS * FIT // DESTS):
            plan[jnp.minimum(d, DESTS - 1) * (2 * KEYS * FIT // DESTS) + u] = 0
        held[jnp.minimum(d, KEYS + 1)] = 0
        return 0

    lax.fori_loop(0, DESTS + 1, clear, 0)

    def enlist(t):
        key = keys[0, t]
        n, rest = held[key], held[KEYS + 1]
        late = jnp.logical_and(key < KEYS, n >= FIT)
        fits = jnp.logical_and(key < KEYS, n < FIT)
        slot = jnp.where(fits, key * FIT + n, PLAN_VOID - PLAN_BLOCK)
        plan[jnp.where(late, PLAN_LIST + rest, PLAN_TILE + slot)] = t
        plan[PLAN_BLOCK + slot] = keys[1, t]
        held[key] = n + 1
        held[KEYS + 1] = rest + jnp.where(late, 1, 0)

    def one(t):
        enlist(t)
        s = source[0, t]
        d = jnp.where(t < live, dest[0, t], DESTS)
        a = tiles[t]
        hi, lo = split(a)
        p = mm(jnp.concatenate([hi, lo, hi], axis=1), xs[s])
        acc[d, 0:TILE, :] += p[:, 0:TILE]
        acc[d, TILE : 2 * TILE, :] += p[:, TILE:]
        total[d] += a

    def group(g, _):
        for u in range(UNROLL):
            one(g * UNROLL + u)
        return 0

    def chunk(c, _):
        tile_copy(tiles_hbm, tiles, sems, c).wait()
        per = CHUNK // UNROLL
        return lax.fori_loop(c * per, (c + 1) * per, group, 0)

    lax.fori_loop(0, CHUNKS, chunk, 0)
    ones = jnp.ones((8, 2 * TILE), BF16)
    per = DESTS // 8

    def write(g):
        at = pl.ds(g * per, per)
        return pltpu.make_async_copy(acc.at[at], out_hbm.at[at], out_sem.at[g])

    def degrees(g, _):
        for u in range(per):
            d = g * per + u
            hi, lo = split(total[d])
            acc[d, 2 * TILE :, :] = mm(ones, jnp.concatenate([hi, lo], axis=1), ((1,), (1,)))
        write(g).start()
        return 0

    lax.fori_loop(0, 8, degrees, 0)

    def counts(k, _):
        plan[PLAN_COUNT + k] = jnp.minimum(held[k], FIT)
        return 0

    lax.fori_loop(0, KEYS, counts, 0)
    plan[PLAN_REST] = held[KEYS + 1]
    for g in range(8):
        write(g).wait()


def forward_tiles(dest, source, keys, count, slab, values):
    return pl.pallas_call(
        forward_kernel,
        out_shape=(jax.ShapeDtypeStruct((DESTS, ROWS, TILE), F32), jax.ShapeDtypeStruct((PLAN_SIZE,), jnp.int32)),
        in_specs=[SM, SM, SM, SM, VM, ANY],
        out_specs=(ANY, SM),
        scratch_shapes=[
            pltpu.VMEM((SLOTS, TILE, TILE), F32),
            pltpu.VMEM((DESTS + 1, ROWS, TILE), F32),
            pltpu.VMEM((DESTS + 1, TILE, TILE), F32),
            pltpu.VMEM((SOURCES, 3 * TILE, WIDTH), BF16),
            pltpu.SMEM((KEYS + 2,), jnp.int32),
            DMA((CHUNKS,)),
            DMA((8,)),
        ],
        compiler_params=pltpu.CompilerParams(vmem_limit_bytes=VMEM_LIMIT),
        cost_estimate=pl.CostEstimate(
            flops=SLOTS * 6 * TILE * TILE * WIDTH, bytes_accessed=22_000_000, transcendentals=0
        ),
        name="forward_tiles",
    )(dest, source, keys, count, slab, values)


def rms_silu(pre, cot):
    sig = 1.0 / (1.0 + jnp.exp(-pre))
    s = pre * sig
    r = lax.rsqrt(jnp.mean(s * s, axis=-1, keepdims=True) + EPSILON)
    inner = jnp.mean(cot * s, axis=-1, keepdims=True)
    ds = r * cot - s * (r * r * r * inner)
    return s * r, ds * sig * (1.0 + pre * (1.0 - sig))


PARTS = 32
PART_ROWS = 40
AR_SENDS = 10
FIRST = 64
SUM_ROWS = (((0, 136), (136, 128)), ((FIRST, 104), (FIRST + 104, 96)))
GATH_ROWS = (((0, 128), (128, 128)), ((FIRST, 96), (FIRST + 96, 96)))
SLICES = 20


def exchange_kernel(
    plan, part_hbm, x_ref, ws_ref, wn_ref, bias_ref, cot_ref, tiles_hbm,
    layer_out, direct_out, g_out, gw_out, back_out,
    acc, relays, arrivals, zfirst, zlast, g0, g1, g2, g3, tiles, own_term, gwp, r1, r2, r3, r4, own_part,
    load_sem, rs_send, rs_recv, zs_send, zs_recv, ag_send, ag_recv, zg_send, zg_recv, ar_send, ar_recv, out_sem, tile_sem,
):
    quarters = (g0, g1, g2, g3)
    row, col = lax.axis_index("row"), lax.axis_index("col")
    zh, core = lax.div(row, 2), lax.rem(row, 2)
    x, y, z = lax.div(col, 8), lax.rem(lax.div(col, 2), 4), lax.rem(col, 2)
    column = lambda xx, yy, zz: xx * 8 + yy * 2 + zz
    ahead = lambda p, d: lax.rem(p + d, 4)
    x_others = [(row, column(ahead(x, d), y, z)) for d in range(1, 4)]
    y_others = [(row, column(x, ahead(y, d), z)) for d in range(1, 4)]
    z_mate = (row, column(x, y, 1 - z))
    core_mate = (zh * 2 + (1 - core), col)
    far = (1 - zh) * 2 + core
    z_others = [z_mate, (far, col), (far, column(x, y, 1 - z))]
    zs = (z, 1 - z)

    def index(order, wide, narrow, mine):
        xx, yy = (wide, narrow) if order == 0 else (narrow, wide)
        return (xx, yy, zs[mine], order)

    def at_place(order, w, which, mine, j):
        p, q = (x, y) if order == 0 else (y, x)
        return index(order, ahead(p, j), ahead(q, which), mine) if w == 0 else index(order, p, ahead(q, j), mine)

    def ring(order, w):
        others = x_others if order == w else y_others
        return others[0], others[2]

    def number(order, w, which, mine):
        return (order * 2 + mine) * 5 + (which if w == 0 else 4)

    class Sum:
        def __init__(self, order, w, which, mine):
            self.n = number(order, w, which, mine)
            self.blk = lambda j: at_place(order, w, which, mine, j % 4)
            self.top, self.low = SUM_ROWS[mine]
            up, down = ring(order, w)
            self.copies = []
            for i, (j, rows, to, device) in enumerate(
                (
                    (2, self.top, relays.at[self.n, 0, pl.ds(0, self.top[1])], up),
                    (2, self.low, relays.at[self.n, 1, pl.ds(0, self.low[1])], down),
                    (1, self.low, arrivals.at[self.n, 0, pl.ds(*self.low)], up),
                    (3, self.top, arrivals.at[self.n, 1, pl.ds(*self.top)], down),
                    (1, self.top, arrivals.at[self.n, 0, pl.ds(*self.top)], up),
                    (3, self.low, arrivals.at[self.n, 1, pl.ds(*self.low)], down),
                )
            ):
                src = acc.at[(*self.blk(j), pl.ds(*rows))]
                self.copies.append(remote(src, to, rs_send.at[self.n], rs_recv.at[self.n, min(i, 2)], device))
            rows = pl.ds(self.top[0], self.top[1] + self.low[1])
            come, gone = arrivals.at[self.n, :, rows], acc.at[0, pl.ds(0, 3), 0, 0, rows]
            self.come = remote(come, come, rs_send.at[self.n], rs_recv.at[self.n, 2], up)
            self.gone = remote(gone, gone, rs_send.at[self.n], rs_recv.at[self.n, 2], up)

        def issue(self):
            for c in self.copies[:4]:
                c.start()

        def relay(self):
            for i, (j, rows) in enumerate(((1, self.top), (3, self.low))):
                self.copies[i].wait_recv()
                at = (*self.blk(j), pl.ds(*rows), slice(None))
                acc[at] += relays[self.n, i, 0 : rows[1], :]
                self.copies[4 + i].start()

        def finish(self):
            self.come.wait_recv()
            rows = pl.ds(self.top[0], self.top[1] + self.low[1])
            at = (*self.blk(0), rows, slice(None))
            acc[at] += arrivals[self.n, 0, rows, :] + arrivals[self.n, 1, rows, :]

        def drain(self):
            self.gone.wait_send()

    def quarter_of(which, mine):
        return mine * 2 + which // 2, (which & 1) ^ (which // 2)

    def held(order, wide, which, mine):
        quarter, local = quarter_of(which, mine)
        return quarters[quarter].at[local, wide, order]

    class Gather:
        def __init__(self, order, w, which, mine):
            n = number(order, w, which, mine)
            p = x if order == 0 else y

            def blk(j):
                return held(order, ahead(p, j), which, mine) if w == 0 else held(order, p, j, mine)

            top, low = GATH_ROWS[mine]
            up, down = ring(order, w)
            self.out, self.come = [], []
            for i, (leaves, comes, rows, device) in enumerate(
                (
                    (0, 3, top, up),
                    (0, 1, low, down),
                    (0, 3, low, up),
                    (0, 1, top, down),
                    (3, 2, top, up),
                    (1, 2, low, down),
                )
            ):
                src, come = blk(leaves).at[pl.ds(*rows)], blk(comes).at[pl.ds(*rows)]
                dst = src if w == 0 else come
                kind = i if i < 2 else i // 2 + 1
                self.out.append(remote(src, dst, ag_send.at[n], ag_recv.at[n, kind], device))
                if i < 2:
                    self.come.append(remote(come, come, ag_send.at[n], ag_recv.at[n, kind], device))
            rows = pl.ds(top[0], top[1] + low[1])
            one, three = g0.at[0, 0, 0, rows], g0.at[0, pl.ds(0, 3), 0, rows]
            self.beside = remote(one, one, ag_send.at[n], ag_recv.at[n, 2], up)
            self.across = remote(blk(2).at[rows], blk(2).at[rows], ag_send.at[n], ag_recv.at[n, 3], up)
            self.gone = remote(three, three, ag_send.at[n], ag_recv.at[n, 3], up)

        def issue(self):
            for c in self.out[:4]:
                c.start()

        def relay(self):
            for i in range(2):
                self.come[i].wait_recv()
                self.out[4 + i].start()

        def near(self):
            self.beside.wait_recv()

        def finish(self):
            self.across.wait_recv()

        def drain(self):
            self.gone.wait_send()

    def strip(ref, order, which, mine, rows=None):
        q = ahead(y if order == 0 else x, which)
        lead = (slice(None), q) if order == 0 else (q, slice(None))
        return ref.at[(*lead, zs[mine], order) + (() if rows is None else (pl.ds(*rows),))]

    def load(order, which, mine):
        n = order * 8 + mine * 4 + which
        return pltpu.make_async_copy(strip(part_hbm, order, which, mine), strip(acc, order, which, mine), load_sem.at[n])

    def z_first(order, which):
        to = zfirst.at[order, which]
        i = order * 4 + which
        return remote(strip(part_hbm, order, which, 1, (0, FIRST)), to, zs_send.at[i], zs_recv.at[i], z_mate)

    def z_last(order):
        rows = pl.ds(FIRST, ROWS - FIRST)
        src = acc.at[(*at_place(order, 0, 0, 1, 0), rows)]
        return remote(src, zlast.at[order, rows], zs_send.at[8 + order], zs_recv.at[8 + order], z_mate)

    turn = [(2, 1), (1, 1), (3, 1), (2, 0), (0, 1), (1, 0), (3, 0), (0, 0)]
    peers = [core_mate] + x_others + y_others + z_others
    greet(peers)
    for which, mine in turn:
        for order in range(2):
            load(order, which, mine).start()
    tile_load = pltpu.make_async_copy(tiles_hbm, tiles, tile_sem)
    tile_load.start()
    enter(peers)
    for which in (2, 1, 3, 0):
        for order in range(2):
            z_first(order, which).start()

    wide = [[Sum(order, 0, which, mine) for order in range(2)] for which, mine in turn]
    narrow = [[Sum(order, 1, 0, mine) for order in range(2)] for mine in range(2)]

    def each(pair, action):
        for s in pair:
            getattr(s, action)()

    def sum_issue(i):
        which, mine = turn[i]
        for order in range(2):
            load(order, which, mine).wait()
            if mine == 0:
                z_first(order, which).wait_recv()
                p = y if order == 0 else x
                for j in range(4):
                    at = (*index(order, j, ahead(p, which), 0), pl.ds(0, FIRST), slice(None))
                    acc[at] += zfirst[order, which, j]
            wide[i][order].issue()

    for i in range(len(turn) + 1):
        if i < len(turn):
            sum_issue(i)
        if i == 0:
            own_term[...] = dot3(x_ref[...], ws_ref[...])
        if i >= 1:
            each(wide[i - 1], "relay")
        if i == 5:
            for n in range(3):
                each(wide[n], "finish")
            each(narrow[1], "issue")
        if i == 6:
            each(narrow[1], "relay")
        if i == 7:
            each(wide[4], "finish")
            each(narrow[1], "finish")
            for order in range(2):
                z_last(order).start()
    for n in (3, 5, 6):
        each(wide[n], "finish")
    each(narrow[0], "issue")
    each(wide[7], "finish")
    each(narrow[0], "relay")
    each(narrow[0], "finish")

    x_own = x_ref[...]
    ws, wn = ws_ref[...], wn_ref[...]
    sums, inv = [], []
    for order in range(2):
        z_last(order).wait_recv()
        own = at_place(order, 0, 0, 0, 0)
        s = jnp.concatenate([acc[(*own, pl.ds(0, FIRST))], acc[(*own, pl.ds(FIRST, ROWS - FIRST))] + zlast[order, FIRST:, :]], axis=0)
        degree = jnp.transpose(jnp.broadcast_to(s[2 * TILE : 2 * TILE + 1, :], (TILE, TILE)))
        root = lax.rsqrt(1.0 + degree)
        inv.append(jnp.concatenate([root, root], axis=1))
        sums.append(jnp.concatenate([s[0:TILE], s[TILE : 2 * TILE]], axis=1))
    inv = jnp.concatenate(inv, axis=0)
    neighbour = jnp.concatenate(sums, axis=0) * inv
    pre = own_term[...] + dot3(neighbour, wn) + bias_ref[...]
    out, grad_pre = rms_silu(pre, cot_ref[...])
    layer_out[...] = out
    spread = dot3(grad_pre, wn, ((1,), (1,))) * inv
    for order in range(2):
        for half in range(2):
            held(order, x if order == 0 else y, 0, 0)[half * TILE : (half + 1) * TILE, :] = spread[
                order * TILE : (order + 1) * TILE, half * TILE : (half + 1) * TILE
            ]

    def give(order):
        src, dst = [held(order, x if order == 0 else y, 0, mine).at[pl.ds(FIRST, 2 * TILE - FIRST)] for mine in range(2)]
        return remote(src, dst, zg_send.at[8 + order], zg_recv.at[8 + order], z_mate)

    def strip_held(order, which, mine):
        quarter, local = quarter_of(which, mine)
        return quarters[quarter].at[local, :, order]

    def z_after(order, which):
        i = order * 4 + which
        src, dst = [strip_held(order, which, mine).at[:, pl.ds(0, FIRST)] for mine in range(2)]
        return remote(src, dst, zg_send.at[i], zg_recv.at[i], z_mate)

    def write(order, which, mine):
        n = order * 8 + mine * 4 + which
        quarter, local = quarter_of(which, mine)
        return pltpu.make_async_copy(strip_held(order, which, mine), g_out.at[quarter, local, :, order], out_sem.at[n])

    def products(quarter, sources):
        for s in sources:
            key = quarter * SOURCES + s
            n = plan[PLAN_COUNT + key]
            total = None
            for i in range(FIT):
                t, b = plan[PLAN_TILE + key * FIT + i], plan[PLAN_BLOCK + key * FIT + i]
                a = tiles[t] * jnp.where(i < n, 1.0, 0.0)
                hi, lo = split(a)
                g = quarters[quarter][lax.shift_right_logical(b, 3) & 1, lax.shift_right_logical(b, 1) & 3, b & 1]
                ghi, glo = split(jnp.concatenate([g[0:TILE], g[TILE:]], axis=1))
                p = mm(jnp.concatenate([hi, lo, hi], axis=0), jnp.concatenate([ghi, ghi, glo], axis=0), ((0,), (0,)))
                total = p if total is None else total + p
            at = slice(s * TILE, (s + 1) * TILE)
            back_out[at, :] = total if quarter == 0 else back_out[at, :] + total

    gwide = {(which, mine): [Gather(order, 0, which, mine) for order in range(2)] for which in range(4) for mine in range(2)}
    gnarrow = [[Gather(order, 1, 0, mine) for order in range(2)] for mine in range(2)]

    def done(which, mine):
        each(gwide[which, mine], "near")
        each(gwide[which, mine], "finish")
        for order in range(2):
            if mine == 0:
                z_after(order, which).start()
                write(order, which, 0).start()

    for order in range(2):
        give(order).start()
    each(gnarrow[0], "issue")
    each(gwide[0, 0], "issue")

    gs = dot3(x_own, grad_pre, ((0,), (0,)))
    gn = dot3(neighbour, grad_pre, ((0,), (0,)))
    flat = [gs[:, 0:TILE], gs[:, TILE:], gn[:, 0:TILE], gn[:, TILE:]]
    gb = jnp.sum(grad_pre, axis=0, keepdims=True)
    blank = jnp.zeros((PARTS * PART_ROWS - 4 * WIDTH - 2, TILE), F32)
    gwp[...] = jnp.concatenate(flat + [gb[:, 0:TILE], gb[:, TILE:], blank], axis=0).reshape(gwp.shape)

    hop = lambda i, src, dst, device: remote(src, dst, ar_send.at[i], ar_recv.at[i], device)
    zg = zh * 2 + z
    c1 = [hop(0, gwp.at[1 - core], r1, core_mate)]
    z_ring = []
    for d in range(1, 4):
        to = ahead(zg, d)
        z_ring.append((lax.div(to, 2) * 2 + core, column(x, y, lax.rem(to, 2))))
    c2 = [hop(d, gwp.at[core, ahead(zg, d)], r2.at[d - 1], z_ring[d - 1]) for d in range(1, 4)]
    c3 = [hop(3 + d, gwp.at[core, zg, ahead(x, d)], r3.at[d - 1], x_others[d - 1]) for d in range(1, 4)]
    c4 = [hop(6 + d, own_part, r4.at[y], y_others[d - 1]) for d in range(1, 4)]
    c4_come = [hop(6 + d, own_part, r4.at[ahead(y, 4 - d)], y_others[d - 1]) for d in range(1, 4)]

    def launch(copies):
        for c in copies:
            c.start()

    def land(copies):
        for c in copies:
            c.wait()

    def phase1():
        land(c1)
        gwp[core] += r1[...]
        launch(c2)

    def phase2():
        land(c2)
        gwp[core, zg] += (r2[0] + r2[1]) + r2[2]
        launch(c3)

    def phase3():
        land(c3)
        own_part[...] = gwp[core, zg, x] + r3[0] + r3[1] + r3[2]
        launch(c4)

    def phase4():
        for c in c4_come:
            c.wait_recv()
        for c in c4:
            c.wait_send()
        terms = [jnp.where(y == i, own_part[...], r4[i]) for i in range(4)]
        gw_out[...] = (terms[0] + terms[1]) + (terms[2] + terms[3])

    launch(c1)
    direct_out[...] = dot3(grad_pre, ws, ((1,), (1,)))

    each(gnarrow[0], "relay")
    each(gwide[0, 0], "relay")
    each(gnarrow[0], "near")
    each(gwide[1, 0], "issue")
    for order in range(2):
        give(order).wait_recv()
    each(gnarrow[1], "issue")
    each(gwide[3, 0], "issue")
    each(gwide[1, 0], "relay")
    phase1()
    each(gnarrow[1], "relay")
    each(gnarrow[0], "finish")
    each(gwide[2, 0], "issue")
    each(gwide[3, 0], "relay")
    done(0, 0)
    each(gwide[0, 1], "issue")
    each(gwide[2, 0], "relay")
    done(1, 0)
    each(gnarrow[1], "near")
    each(gwide[1, 1], "issue")
    each(gwide[0, 1], "relay")
    tile_load.wait()
    products(0, (0, 1, 2))
    done(3, 0)
    phase2()
    each(gnarrow[1], "finish")
    each(gwide[3, 1], "issue")
    each(gwide[1, 1], "relay")
    products(0, (3, 4, 5))
    done(2, 0)
    each(gwide[2, 1], "issue")
    each(gwide[3, 1], "relay")
    products(0, (6, 7))
    phase3()
    each(gwide[2, 1], "relay")
    products(1, (0, 1, 2, 3))
    for which in range(4):
        if which == 2:
            products(1, (4, 5, 6, 7))
            products(2, range(SOURCES))
        done(which, 1)
        for order in range(2):
            z_after(order, which).wait_recv()
            write(order, which, 1).start()
    products(3, range(SOURCES))
    phase4()

    for pair in wide + narrow + list(gwide.values()) + gnarrow:
        each(pair, "drain")
    for order in range(2):
        z_last(order).wait_send()
        give(order).wait_send()
        for which in range(4):
            z_first(order, which).wait_send()
            z_after(order, which).wait_send()
    for which in range(4):
        for order in range(2):
            for own_z in range(2):
                write(order, which, own_z).wait()


def exchange(plan, part, x, ws, wn, bias, cot, values):
    n = x.shape[0]
    layout = (4, 4, 2, 2)
    out = pl.pallas_call(
        exchange_kernel,
        out_shape=(
            jax.ShapeDtypeStruct((n, WIDTH), F32),
            jax.ShapeDtypeStruct((n, WIDTH), F32),
            jax.ShapeDtypeStruct((4, 2, 4, 2, 2 * TILE, TILE), F32),
            jax.ShapeDtypeStruct((PART_ROWS, TILE), F32),
            jax.ShapeDtypeStruct((SOURCES * TILE, WIDTH), F32),
        ),
        in_specs=[SM, ANY, VM, VM, VM, VM, VM, ANY],
        out_specs=(VM, VM, ANY, VM, VM),
        scratch_shapes=[
            pltpu.VMEM((*layout, ROWS, TILE), F32),
            pltpu.VMEM((SLICES, 2, 136, TILE), F32),
            pltpu.VMEM((SLICES, 2, ROWS, TILE), F32),
            pltpu.VMEM((2, 4, 4, FIRST, TILE), F32),
            pltpu.VMEM((2, ROWS, TILE), F32),
            *[pltpu.VMEM((2, 4, 2, 2 * TILE, TILE), F32) for _ in range(4)],
            pltpu.VMEM((SLOTS, TILE, TILE), F32),
            pltpu.VMEM((n, WIDTH), F32),
            pltpu.VMEM((2, 4, 4, PART_ROWS, TILE), F32),
            pltpu.VMEM((4, 4, PART_ROWS, TILE), F32),
            pltpu.VMEM((3, 4, PART_ROWS, TILE), F32),
            pltpu.VMEM((3, PART_ROWS, TILE), F32),
            pltpu.VMEM((4, PART_ROWS, TILE), F32),
            pltpu.VMEM((PART_ROWS, TILE), F32),
            DMA((16,)),
            DMA((SLICES,)),
            DMA((SLICES, 3)),
            DMA((10,)),
            DMA((10,)),
            DMA((SLICES,)),
            DMA((SLICES, 4)),
            DMA((10,)),
            DMA((10,)),
            DMA((AR_SENDS,)),
            DMA((AR_SENDS,)),
            DMA((16,)),
            DMA,
        ],
        compiler_params=pltpu.CompilerParams(
            collective_id=1, has_side_effects=True, vmem_limit_bytes=VMEM_LIMIT
        ),
        name="exchange",
    )(plan, part.reshape(*layout, ROWS, TILE), x, ws, wn, bias.reshape(1, WIDTH), cot, values)
    layer_out, direct, g, gw, back = out
    return layer_out, direct, g.reshape(DESTS, 2 * TILE, TILE), gw, back


def rest_kernel(
    plan, source, keys, g_hbm, tiles_hbm, back_ref, out_ref, tiles, g, tile_sem, g_sem
):
    n = plan[PLAN_REST]

    def copies(i):
        slot = lax.rem(i, REST_SLOTS)
        t = plan[PLAN_LIST + i]
        return (
            pltpu.make_async_copy(tiles_hbm.at[t], tiles.at[slot], tile_sem.at[slot]),
            pltpu.make_async_copy(g_hbm.at[keys[1, t]], g.at[slot], g_sem.at[slot]),
        )

    def begin(i, _):
        for c in copies(i):
            c.start()
        return 0

    lax.fori_loop(0, jnp.minimum(n, REST_SLOTS), begin, 0)
    out_ref[...] = back_ref[...]

    def some(k, _):
        first = k * REST_UNROLL
        for u in range(REST_UNROLL):

            @pl.when(first + u < n)
            def _():
                for c in copies(first + u):
                    c.wait()

        products = []
        for u in range(REST_UNROLL):
            i = jnp.minimum(first + u, n - 1)
            slot = lax.rem(i, REST_SLOTS)
            hi, lo = split(tiles[slot] * jnp.where(first + u < n, 1.0, 0.0))
            ghi, glo = split(jnp.concatenate([g[slot, 0:TILE, :], g[slot, TILE:, :]], axis=1))
            a = jnp.concatenate([hi, lo, hi], axis=0)
            products.append((i, mm(a, jnp.concatenate([ghi, ghi, glo], axis=0), ((0,), (0,)))))
        for i, p in products:
            rows = pl.ds(pl.multiple_of(source[0, plan[PLAN_LIST + i]] * TILE, TILE), TILE)
            out_ref[rows, :] += p
        for u in range(REST_UNROLL):

            @pl.when(first + u + REST_SLOTS < n)
            def _():
                begin(first + u + REST_SLOTS, 0)

        return 0

    lax.fori_loop(0, lax.div(n + REST_UNROLL - 1, REST_UNROLL), some, 0)


def backward_rest(plan, source, keys, g, values, back):
    return pl.pallas_call(
        rest_kernel,
        out_shape=jax.ShapeDtypeStruct(back.shape, F32),
        in_specs=[SM, SM, SM, ANY, ANY, VM],
        out_specs=VM,
        scratch_shapes=[
            pltpu.VMEM((REST_SLOTS, TILE, TILE), F32),
            pltpu.VMEM((REST_SLOTS, 2 * TILE, TILE), F32),
            DMA((REST_SLOTS,)),
            DMA((REST_SLOTS,)),
        ],
        compiler_params=pltpu.CompilerParams(vmem_limit_bytes=VMEM_LIMIT),
        name="backward_rest",
    )(plan, source, keys, g, values, back)


def scatter_kernel(
    back_hbm, part_ref, out_hbm, gw_hbm,
    back_ref, out_ref, near, cross, send_buf, gws, send, recv, ar_send, ar_recv, load_sem, out_sem,
):
    row, col = lax.axis_index("row"), lax.axis_index("col")
    hi, core = lax.div(row, 2), lax.rem(row, 2)
    x, y, z = lax.div(col, 8), lax.rem(lax.div(col, 2), 4), lax.rem(col, 2)
    column = lambda xx, yy, zz: xx * 8 + yy * 2 + zz
    ahead = lambda p, d: lax.rem(p + d, 4)
    x_others = [(row, column(ahead(x, d), y, z)) for d in range(1, 4)]
    zg = hi * 2 + z
    z_others = []
    for d in range(1, 4):
        to = ahead(zg, d)
        z_others.append((lax.div(to, 2) * 2 + core, column(x, y, lax.rem(to, 2))))
    mate = (hi * 2 + (1 - core), col)
    far = z_others[1]
    peers = [mate] + x_others + z_others
    greet(peers)
    load = pltpu.make_async_copy(back_hbm, back_ref, load_sem)
    load.start()
    enter(peers)
    n = out_ref.shape[0]
    m = n // PIECES
    at = lambda r, c: pl.ds(pl.multiple_of(r * n + c * m, m), m)
    piece = lambda c: pl.ds(c * m, m)
    far_row, far_mate = (1 - hi) * 2 + core, (1 - hi) * 2 + (1 - core)
    write = lambda c: pltpu.make_async_copy(out_ref.at[piece(c)], out_hbm.at[piece(c)], out_sem.at[c])
    first, second, third = [], [], []
    for c in range(PIECES):
        src = back_ref.at[at(far_mate, c)]
        first.append(remote(src, near.at[0, piece(c)], send.at[0, c], recv.at[0, c], mate))
        src = back_ref.at[at(hi * 2 + (1 - core), c)]
        second.append(remote(src, near.at[1, piece(c)], send.at[1, c], recv.at[1, c], mate))
        third.append(remote(send_buf.at[piece(c)], cross.at[piece(c)], send.at[2, c], recv.at[2, c], far))
    load.wait()
    for c in first + second:
        c.start()

    hop = lambda i, ref, device: remote(ref, ref, ar_send.at[i], ar_recv.at[i], device)
    gws[core, zg, x] = part_ref[...]
    c5 = [hop(d, gws.at[core, zg, x], x_others[d]) for d in range(3)]
    c6 = [hop(3 + d, gws.at[core, zg], z_others[d]) for d in range(3)]
    c7 = [hop(6, gws.at[core], mate)]
    for c in c5:
        c.start()
    for c in range(PIECES):
        first[c].wait_recv()
        send_buf[piece(c), :] = back_ref[at(far_row, c), :] + near[0, piece(c), :]
        third[c].start()
    for d in range(3):
        hop(d, gws.at[core, zg, ahead(x, 3 - d)], x_others[d]).wait_recv()
    for c in c6:
        c.start()
    for d in range(3):
        hop(3 + d, gws.at[core, ahead(zg, 3 - d)], z_others[d]).wait_recv()
    for c in c7:
        c.start()
    for c in range(PIECES):
        second[c].wait_recv()
        third[c].wait_recv()
        out_ref[piece(c), :] = back_ref[at(row, c), :] + near[1, piece(c), :] + cross[piece(c), :]
        write(c).start()
    hop(6, gws.at[1 - core], mate).wait_recv()
    gw_write = pltpu.make_async_copy(gws, gw_hbm, out_sem.at[PIECES])
    gw_write.start()
    for c in range(PIECES):
        write(c).wait()
    gw_write.wait()
    for c in first + second + third + c5 + c6 + c7:
        c.wait_send()


def scatter_rows(back, part):
    n = back.shape[0] // 4
    parts = (2, 4, 4, PART_ROWS, TILE)
    back, gw = pl.pallas_call(
        scatter_kernel,
        out_shape=(jax.ShapeDtypeStruct((n, WIDTH), F32), jax.ShapeDtypeStruct(parts, F32)),
        in_specs=[ANY, VM],
        out_specs=(ANY, ANY),
        scratch_shapes=[
            pltpu.VMEM(back.shape, F32),
            pltpu.VMEM((n, WIDTH), F32),
            pltpu.VMEM((2, n, WIDTH), F32),
            pltpu.VMEM((n, WIDTH), F32),
            pltpu.VMEM((n, WIDTH), F32),
            pltpu.VMEM(parts, F32),
            DMA((3, PIECES)),
            DMA((3, PIECES)),
            DMA((7,)),
            DMA((7,)),
            DMA,
            DMA((PIECES + 1,)),
        ],
        compiler_params=pltpu.CompilerParams(collective_id=2, has_side_effects=True),
        name="scatter_rows",
    )(back, part)
    return back, gw.reshape(PARTS * PART_ROWS, TILE)


def finish_kernel(kept, direct, back, gw, kept_out, grad_x, grad_ws, grad_wn, grad_bias):
    kept_out[...] = kept[...]
    grad_x[...] = direct[...] + back[...]
    for i, out in enumerate((grad_ws, grad_wn)):
        for half in range(2):
            first = (2 * i + half) * WIDTH
            out[:, half * TILE : (half + 1) * TILE] = gw[first : first + WIDTH, :]
    for half in range(2):
        grad_bias[:, half * TILE : (half + 1) * TILE] = gw[4 * WIDTH + half : 4 * WIDTH + half + 1, :]


def finish(kept, direct, back, gw):
    rows, square = jax.ShapeDtypeStruct(direct.shape, F32), jax.ShapeDtypeStruct((WIDTH, WIDTH), F32)
    return pl.pallas_call(
        finish_kernel,
        out_shape=(rows, rows, square, square, jax.ShapeDtypeStruct((1, WIDTH), F32)),
        in_specs=[VM] * 4,
        out_specs=(VM,) * 5,
        name="finish",
    )(kept, direct, back, gw)


def body(x, ws, wn, bias, tile_values, tile_dest, tile_source, tile_count, cot):
    values = tile_values.reshape(SLOTS, TILE, TILE)
    dest, source = tile_dest.reshape(1, SLOTS), tile_source.reshape(1, SLOTS)
    count = tile_count.reshape(1)
    slab, keys = gather_rows(count, dest, source, x)
    part, plan = forward_tiles(dest, source, keys, count, slab, values)
    layer_out, direct, g, gw_part, back = exchange(plan, part, x, ws, wn, bias, cot, values)
    back = backward_rest(plan, source, keys, g, values, back)
    back, gw = scatter_rows(back, gw_part)
    layer_out, grad_x, grad_ws, grad_wn, grad_bias = finish(layer_out, direct, back, gw)
    return layer_out, grad_x, grad_ws, grad_wn, grad_bias.reshape(WIDTH)


def solution(mesh):
    in_specs = (
        P(("col", "row"), None),
        P(),
        P(),
        P(),
        P("row", "col", None, None, None),
        P("row", "col", None),
        P("row", "col", None),
        P("row", "col"),
        P(("col", "row"), None),
    )
    out_specs = (P(("col", "row"), None), P(("col", "row"), None), P(), P(), P())
    return jax.shard_map(body, mesh=mesh, in_specs=in_specs, out_specs=out_specs, check_vma=False)
```

```python
import functools

import jax
import jax.numpy as jnp
from jax import lax
from jax.experimental import pallas as pl
from jax.experimental.pallas import tpu as pltpu
from jax.sharding import PartitionSpec as P

EPSILON = 1e-05
F32 = jnp.float32
BF16 = jnp.bfloat16
MESH = pl.DeviceIdType.MESH
TILE = 128
WIDTH = 256
SLOTS = 192
DESTS = 64
SOURCES = 8
ROWS = 264
CHUNK = 16
CHUNKS = SLOTS // CHUNK
UNROLL = 16
PIECES = 4
FIT = 8
KEYS = 4 * SOURCES
PLAN_TILE, PLAN_BLOCK, PLAN_COUNT = 0, KEYS * FIT, 2 * KEYS * FIT
PLAN_REST, PLAN_LIST = PLAN_COUNT + KEYS, PLAN_COUNT + 2 * KEYS
PLAN_SIZE = 1024
PLAN_VOID = PLAN_SIZE - 1
REST_SLOTS = 16
REST_UNROLL = 4
VMEM_LIMIT = 60 * 1024 * 1024

VM = pl.BlockSpec(memory_space=pltpu.VMEM)
SM = pl.BlockSpec(memory_space=pltpu.SMEM)
ANY = pl.BlockSpec(memory_space=pl.ANY)
DMA = pltpu.SemaphoreType.DMA


def split(a):
    hi = a.astype(BF16)
    return hi, (a - hi.astype(F32)).astype(BF16)


def mm(a, b, dims=((1,), (0,))):
    return lax.dot_general(a, b, (dims, ((), ())), preferred_element_type=F32)


def dot3(a, b, dims=((1,), (0,))):
    ah, al = split(a)
    bh, bl = split(b)
    return mm(ah, bh, dims) + (mm(ah, bl, dims) + mm(al, bh, dims))


def greet(devices):
    barrier = pltpu.get_barrier_semaphore()
    for device in devices:
        pl.semaphore_signal(barrier, inc=1, device_id=device, device_id_type=MESH)


def enter(devices):
    pl.semaphore_wait(pltpu.get_barrier_semaphore(), len(devices))


def remote(src, dst, send, recv, device):
    return pltpu.make_async_remote_copy(
        src_ref=src, dst_ref=dst, send_sem=send, recv_sem=recv, device_id=device, device_id_type=MESH
    )


def arrival(q, col):
    x, y, z = lax.div(col, 8), lax.rem(lax.div(col, 2), 4), lax.rem(col, 2)
    bx, by, order = lax.shift_right_logical(q, 4), lax.shift_right_logical(q, 2) & 3, q & 1
    other = (lax.shift_right_logical(q, 1) & 1) ^ z
    which = jnp.where(order == 0, by - y, bx - x) & 3
    wide = jnp.where(order == 0, bx, by)
    half = lax.shift_right_logical(which, 1)
    local = (which & 1) ^ half
    return other * 2 + half, (local * 4 + wide) * 2 + order


def gather_kernel(count, dest_ref, source_ref, x_ref, out_ref, keys_out, local_sem, send, recv):
    row, col = lax.axis_index("row"), lax.axis_index("col")
    hi, core = lax.div(row, 2), lax.rem(row, 2)
    mate = hi * 2 + (1 - core)
    far = (1 - hi) * 2 + core
    peers = [(mate, col), (far, col)]
    greet(peers)
    enter(peers)
    n = x_ref.shape[0]
    m = n // PIECES
    at = lambda r, c: out_ref.at[pl.ds(pl.multiple_of(r * n + c * m, m), m)]
    piece = lambda c: x_ref.at[pl.ds(c * m, m)]
    own = pltpu.make_async_copy(x_ref, out_ref.at[pl.ds(pl.multiple_of(row * n, n), n)], local_sem)
    across = [remote(piece(c), at(row, c), send.at[0, c], recv.at[0, c], (far, col)) for c in range(PIECES)]
    beside = [remote(piece(c), at(row, c), send.at[1, c], recv.at[1, c], (mate, col)) for c in range(PIECES)]
    onward = [remote(at(far, c), at(far, c), send.at[2, c], recv.at[2, c], (mate, col)) for c in range(PIECES)]
    for c in across + beside:
        c.start()
    own.start()
    dest = dest_ref[...]
    quarter, block = arrival(dest, col)
    listed = lax.broadcasted_iota(jnp.int32, dest.shape, 1) < count[0]
    keys_out[0:1, :] = jnp.where(listed, quarter * SOURCES + source_ref[...], KEYS)
    keys_out[1:2, :] = quarter * 16 + block
    for c in range(PIECES):
        across[c].wait_recv()
        onward[c].start()
    for c in beside + onward:
        c.wait_recv()
    own.wait()
    for c in across + beside + onward:
        c.wait_send()


def gather_rows(count, dest, source, x):
    return pl.pallas_call(
        gather_kernel,
        out_shape=(jax.ShapeDtypeStruct((4 * x.shape[0], x.shape[1]), F32), jax.ShapeDtypeStruct((2, SLOTS), jnp.int32)),
        in_specs=[SM, VM, VM, VM],
        out_specs=(VM, VM),
        scratch_shapes=[DMA, DMA((3, PIECES)), DMA((3, PIECES))],
        compiler_params=pltpu.CompilerParams(collective_id=0, has_side_effects=True),
        name="gather_rows",
    )(count, dest, source, x)


def tile_copy(tiles_hbm, tiles, sems, c):
    at = pl.ds(c * CHUNK, CHUNK)
    return pltpu.make_async_copy(tiles_hbm.at[at], tiles.at[at], sems.at[c])


def forward_kernel(
    dest, source, keys, count, x_ref, tiles_hbm, out_hbm, plan, tiles, acc, total, xs, held, sems, out_sem
):
    for c in range(CHUNKS):
        tile_copy(tiles_hbm, tiles, sems, c).start()
    live = count[0]
    for s in range(SOURCES):
        hi, lo = split(x_ref[s * TILE : (s + 1) * TILE, :])
        xs[s, 0:TILE, :] = hi
        xs[s, TILE : 2 * TILE, :] = hi
        xs[s, 2 * TILE :, :] = lo

    def clear(d, _):
        acc[d] = jnp.zeros((ROWS, TILE), F32)
        total[d] = jnp.zeros((TILE, TILE), F32)
        for u in range(2 * KEYS * FIT // DESTS):
            plan[jnp.minimum(d, DESTS - 1) * (2 * KEYS * FIT // DESTS) + u] = 0
        held[jnp.minimum(d, KEYS + 1)] = 0
        return 0

    lax.fori_loop(0, DESTS + 1, clear, 0)

    def enlist(t):
        key = keys[0, t]
        n, rest = held[key], held[KEYS + 1]
        late = jnp.logical_and(key < KEYS, n >= FIT)
        fits = jnp.logical_and(key < KEYS, n < FIT)
        slot = jnp.where(fits, key * FIT + n, PLAN_VOID - PLAN_BLOCK)
        plan[jnp.where(late, PLAN_LIST + rest, PLAN_TILE + slot)] = t
        plan[PLAN_BLOCK + slot] = keys[1, t]
        held[key] = n + 1
        held[KEYS + 1] = rest + jnp.where(late, 1, 0)

    def one(t):
        enlist(t)
        s = source[0, t]
        d = jnp.where(t < live, dest[0, t], DESTS)
        a = tiles[t]
        hi, lo = split(a)
        p = mm(jnp.concatenate([hi, lo, hi], axis=1), xs[s])
        acc[d, 0:TILE, :] += p[:, 0:TILE]
        acc[d, TILE : 2 * TILE, :] += p[:, TILE:]
        total[d] += a

    def group(g, _):
        for u in range(UNROLL):
            one(g * UNROLL + u)
        return 0

    def chunk(c, _):
        tile_copy(tiles_hbm, tiles, sems, c).wait()
        per = CHUNK // UNROLL
        return lax.fori_loop(c * per, (c + 1) * per, group, 0)

    lax.fori_loop(0, CHUNKS, chunk, 0)
    ones = jnp.ones((8, 2 * TILE), BF16)
    per = DESTS // 8

    def write(g):
        at = pl.ds(g * per, per)
        return pltpu.make_async_copy(acc.at[at], out_hbm.at[at], out_sem.at[g])

    def degrees(g, _):
        for u in range(per):
            d = g * per + u
            hi, lo = split(total[d])
            acc[d, 2 * TILE :, :] = mm(ones, jnp.concatenate([hi, lo], axis=1), ((1,), (1,)))
        write(g).start()
        return 0

    lax.fori_loop(0, 8, degrees, 0)

    def counts(k, _):
        plan[PLAN_COUNT + k] = jnp.minimum(held[k], FIT)
        return 0

    lax.fori_loop(0, KEYS, counts, 0)
    plan[PLAN_REST] = held[KEYS + 1]
    for g in range(8):
        write(g).wait()


def forward_tiles(dest, source, keys, count, slab, values):
    return pl.pallas_call(
        forward_kernel,
        out_shape=(jax.ShapeDtypeStruct((DESTS, ROWS, TILE), F32), jax.ShapeDtypeStruct((PLAN_SIZE,), jnp.int32)),
        in_specs=[SM, SM, SM, SM, VM, ANY],
        out_specs=(ANY, SM),
        scratch_shapes=[
            pltpu.VMEM((SLOTS, TILE, TILE), F32),
            pltpu.VMEM((DESTS + 1, ROWS, TILE), F32),
            pltpu.VMEM((DESTS + 1, TILE, TILE), F32),
            pltpu.VMEM((SOURCES, 3 * TILE, WIDTH), BF16),
            pltpu.SMEM((KEYS + 2,), jnp.int32),
            DMA((CHUNKS,)),
            DMA((8,)),
        ],
        compiler_params=pltpu.CompilerParams(vmem_limit_bytes=VMEM_LIMIT),
        cost_estimate=pl.CostEstimate(
            flops=SLOTS * 6 * TILE * TILE * WIDTH, bytes_accessed=22_000_000, transcendentals=0
        ),
        name="forward_tiles",
    )(dest, source, keys, count, slab, values)


def rms_silu(pre, cot):
    sig = 1.0 / (1.0 + jnp.exp(-pre))
    s = pre * sig
    r = lax.rsqrt(jnp.mean(s * s, axis=-1, keepdims=True) + EPSILON)
    inner = jnp.mean(cot * s, axis=-1, keepdims=True)
    ds = r * cot - s * (r * r * r * inner)
    return s * r, ds * sig * (1.0 + pre * (1.0 - sig))


PARTS = 32
PART_ROWS = 40
AR_SENDS = 10
FIRST = 64
SUM_ROWS = (((0, 136), (136, 128)), ((FIRST, 104), (FIRST + 104, 96)))
GATH_ROWS = (((0, 128), (128, 128)), ((FIRST, 96), (FIRST + 96, 96)))
SLICES = 20


def exchange_kernel(
    plan, part_hbm, x_ref, ws_ref, wn_ref, bias_ref, cot_ref, tiles_hbm,
    layer_out, direct_out, g_out, gw_out, back_out,
    acc, relays, arrivals, zfirst, zlast, g0, g1, g2, g3, tiles, own_term, gwp, r1, r2, r3, r4, own_part,
    load_sem, rs_send, rs_recv, zs_send, zs_recv, ag_send, ag_recv, zg_send, zg_recv, ar_send, ar_recv, out_sem, tile_sem,
):
    quarters = (g0, g1, g2, g3)
    row, col = lax.axis_index("row"), lax.axis_index("col")
    zh, core = lax.div(row, 2), lax.rem(row, 2)
    x, y, z = lax.div(col, 8), lax.rem(lax.div(col, 2), 4), lax.rem(col, 2)
    column = lambda xx, yy, zz: xx * 8 + yy * 2 + zz
    ahead = lambda p, d: lax.rem(p + d, 4)
    x_others = [(row, column(ahead(x, d), y, z)) for d in range(1, 4)]
    y_others = [(row, column(x, ahead(y, d), z)) for d in range(1, 4)]
    z_mate = (row, column(x, y, 1 - z))
    core_mate = (zh * 2 + (1 - core), col)
    far = (1 - zh) * 2 + core
    z_others = [z_mate, (far, col), (far, column(x, y, 1 - z))]
    zs = (z, 1 - z)

    def index(order, wide, narrow, mine):
        xx, yy = (wide, narrow) if order == 0 else (narrow, wide)
        return (xx, yy, zs[mine], order)

    def at_place(order, w, which, mine, j):
        p, q = (x, y) if order == 0 else (y, x)
        return index(order, ahead(p, j), ahead(q, which), mine) if w == 0 else index(order, p, ahead(q, j), mine)

    def ring(order, w):
        others = x_others if order == w else y_others
        return others[0], others[2]

    def number(order, w, which, mine):
        return (order * 2 + mine) * 5 + (which if w == 0 else 4)

    class Sum:
        def __init__(self, order, w, which, mine):
            self.n = number(order, w, which, mine)
            self.blk = lambda j: at_place(order, w, which, mine, j % 4)
            self.top, self.low = SUM_ROWS[mine]
            up, down = ring(order, w)
            self.copies = []
            for i, (j, rows, to, device) in enumerate(
                (
                    (2, self.top, relays.at[self.n, 0, pl.ds(0, self.top[1])], up),
                    (2, self.low, relays.at[self.n, 1, pl.ds(0, self.low[1])], down),
                    (1, self.low, arrivals.at[self.n, 0, pl.ds(*self.low)], up),
                    (3, self.top, arrivals.at[self.n, 1, pl.ds(*self.top)], down),
                    (1, self.top, arrivals.at[self.n, 0, pl.ds(*self.top)], up),
                    (3, self.low, arrivals.at[self.n, 1, pl.ds(*self.low)], down),
                )
            ):
                src = acc.at[(*self.blk(j), pl.ds(*rows))]
                self.copies.append(remote(src, to, rs_send.at[self.n], rs_recv.at[self.n, min(i, 2)], device))
            rows = pl.ds(self.top[0], self.top[1] + self.low[1])
            come, gone = arrivals.at[self.n, :, rows], acc.at[0, pl.ds(0, 3), 0, 0, rows]
            self.come = remote(come, come, rs_send.at[self.n], rs_recv.at[self.n, 2], up)
            self.gone = remote(gone, gone, rs_send.at[self.n], rs_recv.at[self.n, 2], up)

        def issue(self):
            for c in self.copies[:4]:
                c.start()

        def relay(self):
            for i, (j, rows) in enumerate(((1, self.top), (3, self.low))):
                self.copies[i].wait_recv()
                at = (*self.blk(j), pl.ds(*rows), slice(None))
                acc[at] += relays[self.n, i, 0 : rows[1], :]
                self.copies[4 + i].start()

        def finish(self):
            self.come.wait_recv()
            rows = pl.ds(self.top[0], self.top[1] + self.low[1])
            at = (*self.blk(0), rows, slice(None))
            acc[at] += arrivals[self.n, 0, rows, :] + arrivals[self.n, 1, rows, :]

        def drain(self):
            self.gone.wait_send()

    def quarter_of(which, mine):
        return mine * 2 + which // 2, (which & 1) ^ (which // 2)

    def held(order, wide, which, mine):
        quarter, local = quarter_of(which, mine)
        return quarters[quarter].at[local, wide, order]

    class Gather:
        def __init__(self, order, w, which, mine):
            n = number(order, w, which, mine)
            p = x if order == 0 else y

            def blk(j):
                return held(order, ahead(p, j), which, mine) if w == 0 else held(order, p, j, mine)

            top, low = GATH_ROWS[mine]
            up, down = ring(order, w)
            self.out, self.come = [], []
            for i, (leaves, comes, rows, device) in enumerate(
                (
                    (0, 3, top, up),
                    (0, 1, low, down),
                    (0, 3, low, up),
                    (0, 1, top, down),
                    (3, 2, top, up),
                    (1, 2, low, down),
                )
            ):
                src, come = blk(leaves).at[pl.ds(*rows)], blk(comes).at[pl.ds(*rows)]
                dst = src if w == 0 else come
                kind = i if i < 2 else i // 2 + 1
                self.out.append(remote(src, dst, ag_send.at[n], ag_recv.at[n, kind], device))
                if i < 2:
                    self.come.append(remote(come, come, ag_send.at[n], ag_recv.at[n, kind], device))
            rows = pl.ds(top[0], top[1] + low[1])
            one, three = g0.at[0, 0, 0, rows], g0.at[0, pl.ds(0, 3), 0, rows]
            self.beside = remote(one, one, ag_send.at[n], ag_recv.at[n, 2], up)
            self.across = remote(blk(2).at[rows], blk(2).at[rows], ag_send.at[n], ag_recv.at[n, 3], up)
            self.gone = remote(three, three, ag_send.at[n], ag_recv.at[n, 3], up)

        def issue(self):
            for c in self.out[:4]:
                c.start()

        def relay(self):
            for i in range(2):
                self.come[i].wait_recv()
                self.out[4 + i].start()

        def near(self):
            self.beside.wait_recv()

        def finish(self):
            self.across.wait_recv()

        def drain(self):
            self.gone.wait_send()

    def strip(ref, order, which, mine, rows=None):
        q = ahead(y if order == 0 else x, which)
        lead = (slice(None), q) if order == 0 else (q, slice(None))
        return ref.at[(*lead, zs[mine], order) + (() if rows is None else (pl.ds(*rows),))]

    def load(order, which, mine):
        n = order * 8 + mine * 4 + which
        return pltpu.make_async_copy(strip(part_hbm, order, which, mine), strip(acc, order, which, mine), load_sem.at[n])

    def z_first(order, which):
        to = zfirst.at[order, which]
        i = order * 4 + which
        return remote(strip(part_hbm, order, which, 1, (0, FIRST)), to, zs_send.at[i], zs_recv.at[i], z_mate)

    def z_last(order):
        rows = pl.ds(FIRST, ROWS - FIRST)
        src = acc.at[(*at_place(order, 0, 0, 1, 0), rows)]
        return remote(src, zlast.at[order, rows], zs_send.at[8 + order], zs_recv.at[8 + order], z_mate)

    turn = [(2, 1), (1, 1), (3, 1), (2, 0), (0, 1), (1, 0), (3, 0), (0, 0)]
    peers = [core_mate] + x_others + y_others + z_others
    greet(peers)
    for which, mine in turn:
        for order in range(2):
            load(order, which, mine).start()
    tile_load = pltpu.make_async_copy(tiles_hbm, tiles, tile_sem)
    tile_load.start()
    enter(peers)
    for which in (2, 1, 3, 0):
        for order in range(2):
            z_first(order, which).start()

    wide = [[Sum(order, 0, which, mine) for order in range(2)] for which, mine in turn]
    narrow = [[Sum(order, 1, 0, mine) for order in range(2)] for mine in range(2)]

    def each(pair, action):
        for s in pair:
            getattr(s, action)()

    def sum_issue(i):
        which, mine = turn[i]
        for order in range(2):
            load(order, which, mine).wait()
            if mine == 0:
                z_first(order, which).wait_recv()
                p = y if order == 0 else x
                for j in range(4):
                    at = (*index(order, j, ahead(p, which), 0), pl.ds(0, FIRST), slice(None))
                    acc[at] += zfirst[order, which, j]
            wide[i][order].issue()

    for i in range(len(turn) + 1):
        if i < len(turn):
            sum_issue(i)
        if i == 0:
            own_term[...] = dot3(x_ref[...], ws_ref[...])
        if i >= 1:
            each(wide[i - 1], "relay")
        if i == 5:
            for n in range(3):
                each(wide[n], "finish")
            each(narrow[1], "issue")
        if i == 6:
            each(narrow[1], "relay")
        if i == 7:
            each(wide[4], "finish")
            each(narrow[1], "finish")
            for order in range(2):
                z_last(order).start()
    for n in (3, 5, 6):
        each(wide[n], "finish")
    each(narrow[0], "issue")
    each(wide[7], "finish")
    each(narrow[0], "relay")
    each(narrow[0], "finish")

    x_own = x_ref[...]
    ws, wn = ws_ref[...], wn_ref[...]
    sums, inv = [], []
    for order in range(2):
        z_last(order).wait_recv()
        own = at_place(order, 0, 0, 0, 0)
        s = jnp.concatenate([acc[(*own, pl.ds(0, FIRST))], acc[(*own, pl.ds(FIRST, ROWS - FIRST))] + zlast[order, FIRST:, :]], axis=0)
        degree = jnp.transpose(jnp.broadcast_to(s[2 * TILE : 2 * TILE + 1, :], (TILE, TILE)))
        root = lax.rsqrt(1.0 + degree)
        inv.append(jnp.concatenate([root, root], axis=1))
        sums.append(jnp.concatenate([s[0:TILE], s[TILE : 2 * TILE]], axis=1))
    inv = jnp.concatenate(inv, axis=0)
    neighbour = jnp.concatenate(sums, axis=0) * inv
    pre = own_term[...] + dot3(neighbour, wn) + bias_ref[...]
    out, grad_pre = rms_silu(pre, cot_ref[...])
    layer_out[...] = out
    spread = dot3(grad_pre, wn, ((1,), (1,))) * inv
    for order in range(2):
        for half in range(2):
            held(order, x if order == 0 else y, 0, 0)[half * TILE : (half + 1) * TILE, :] = spread[
                order * TILE : (order + 1) * TILE, half * TILE : (half + 1) * TILE
            ]

    def give(order):
        src, dst = [held(order, x if order == 0 else y, 0, mine).at[pl.ds(FIRST, 2 * TILE - FIRST)] for mine in range(2)]
        return remote(src, dst, zg_send.at[8 + order], zg_recv.at[8 + order], z_mate)

    def strip_held(order, which, mine):
        quarter, local = quarter_of(which, mine)
        return quarters[quarter].at[local, :, order]

    def z_after(order, which):
        i = order * 4 + which
        src, dst = [strip_held(order, which, mine).at[:, pl.ds(0, FIRST)] for mine in range(2)]
        return remote(src, dst, zg_send.at[i], zg_recv.at[i], z_mate)

    def write(order, which, mine):
        n = order * 8 + mine * 4 + which
        quarter, local = quarter_of(which, mine)
        return pltpu.make_async_copy(strip_held(order, which, mine), g_out.at[quarter, local, :, order], out_sem.at[n])

    def products(quarter, sources):
        for s in sources:
            key = quarter * SOURCES + s
            n = plan[PLAN_COUNT + key]
            total = None
            for i in range(FIT):
                t, b = plan[PLAN_TILE + key * FIT + i], plan[PLAN_BLOCK + key * FIT + i]
                a = tiles[t] * jnp.where(i < n, 1.0, 0.0)
                hi, lo = split(a)
                g = quarters[quarter][lax.shift_right_logical(b, 3) & 1, lax.shift_right_logical(b, 1) & 3, b & 1]
                ghi, glo = split(jnp.concatenate([g[0:TILE], g[TILE:]], axis=1))
                p = mm(jnp.concatenate([hi, lo, hi], axis=0), jnp.concatenate([ghi, ghi, glo], axis=0), ((0,), (0,)))
                total = p if total is None else total + p
            at = slice(s * TILE, (s + 1) * TILE)
            back_out[at, :] = total if quarter == 0 else back_out[at, :] + total

    gwide = {(which, mine): [Gather(order, 0, which, mine) for order in range(2)] for which in range(4) for mine in range(2)}
    gnarrow = [[Gather(order, 1, 0, mine) for order in range(2)] for mine in range(2)]

    def done(which, mine):
        each(gwide[which, mine], "near")
        each(gwide[which, mine], "finish")
        for order in range(2):
            if mine == 0:
                z_after(order, which).start()
                write(order, which, 0).start()

    for order in range(2):
        give(order).start()
    each(gnarrow[0], "issue")
    each(gwide[0, 0], "issue")

    gs = dot3(x_own, grad_pre, ((0,), (0,)))
    gn = dot3(neighbour, grad_pre, ((0,), (0,)))
    flat = [gs[:, 0:TILE], gs[:, TILE:], gn[:, 0:TILE], gn[:, TILE:]]
    gb = jnp.sum(grad_pre, axis=0, keepdims=True)
    blank = jnp.zeros((PARTS * PART_ROWS - 4 * WIDTH - 2, TILE), F32)
    gwp[...] = jnp.concatenate(flat + [gb[:, 0:TILE], gb[:, TILE:], blank], axis=0).reshape(gwp.shape)

    hop = lambda i, src, dst, device: remote(src, dst, ar_send.at[i], ar_recv.at[i], device)
    zg = zh * 2 + z
    c1 = [hop(0, gwp.at[1 - core], r1, core_mate)]
    z_ring = []
    for d in range(1, 4):
        to = ahead(zg, d)
        z_ring.append((lax.div(to, 2) * 2 + core, column(x, y, lax.rem(to, 2))))
    c2 = [hop(d, gwp.at[core, ahead(zg, d)], r2.at[d - 1], z_ring[d - 1]) for d in range(1, 4)]
    c3 = [hop(3 + d, gwp.at[core, zg, ahead(x, d)], r3.at[d - 1], x_others[d - 1]) for d in range(1, 4)]
    c4 = [hop(6 + d, own_part, r4.at[y], y_others[d - 1]) for d in range(1, 4)]
    c4_come = [hop(6 + d, own_part, r4.at[ahead(y, 4 - d)], y_others[d - 1]) for d in range(1, 4)]

    def launch(copies):
        for c in copies:
            c.start()

    def land(copies):
        for c in copies:
            c.wait()

    def phase1():
        land(c1)
        gwp[core] += r1[...]
        launch(c2)

    def phase2():
        land(c2)
        gwp[core, zg] += (r2[0] + r2[1]) + r2[2]
        launch(c3)

    def phase3():
        land(c3)
        own_part[...] = gwp[core, zg, x] + r3[0] + r3[1] + r3[2]
        launch(c4)

    def phase4():
        for c in c4_come:
            c.wait_recv()
        for c in c4:
            c.wait_send()
        terms = [jnp.where(y == i, own_part[...], r4[i]) for i in range(4)]
        gw_out[...] = (terms[0] + terms[1]) + (terms[2] + terms[3])

    launch(c1)
    direct_out[...] = dot3(grad_pre, ws, ((1,), (1,)))

    each(gnarrow[0], "relay")
    each(gwide[0, 0], "relay")
    each(gnarrow[0], "near")
    each(gwide[1, 0], "issue")
    for order in range(2):
        give(order).wait_recv()
    each(gnarrow[1], "issue")
    each(gwide[3, 0], "issue")
    each(gwide[1, 0], "relay")
    phase1()
    each(gnarrow[1], "relay")
    each(gnarrow[0], "finish")
    each(gwide[2, 0], "issue")
    each(gwide[3, 0], "relay")
    done(0, 0)
    each(gwide[0, 1], "issue")
    each(gwide[2, 0], "relay")
    done(1, 0)
    each(gnarrow[1], "near")
    each(gwide[1, 1], "issue")
    each(gwide[0, 1], "relay")
    tile_load.wait()
    products(0, (0, 1, 2))
    done(3, 0)
    phase2()
    each(gnarrow[1], "finish")
    each(gwide[3, 1], "issue")
    each(gwide[1, 1], "relay")
    products(0, (3, 4, 5))
    done(2, 0)
    each(gwide[2, 1], "issue")
    each(gwide[3, 1], "relay")
    products(0, (6, 7))
    phase3()
    each(gwide[2, 1], "relay")
    products(1, (0, 1, 2, 3))
    for which in range(4):
        if which == 2:
            products(1, (4, 5, 6, 7))
            products(2, range(SOURCES))
        done(which, 1)
        for order in range(2):
            z_after(order, which).wait_recv()
            write(order, which, 1).start()
    products(3, range(SOURCES))
    phase4()

    for pair in wide + narrow + list(gwide.values()) + gnarrow:
        each(pair, "drain")
    for order in range(2):
        z_last(order).wait_send()
        give(order).wait_send()
        for which in range(4):
            z_first(order, which).wait_send()
            z_after(order, which).wait_send()
    for which in range(4):
        for order in range(2):
            for own_z in range(2):
                write(order, which, own_z).wait()


def exchange(plan, part, x, ws, wn, bias, cot, values):
    n = x.shape[0]
    layout = (4, 4, 2, 2)
    out = pl.pallas_call(
        exchange_kernel,
        out_shape=(
            jax.ShapeDtypeStruct((n, WIDTH), F32),
            jax.ShapeDtypeStruct((n, WIDTH), F32),
            jax.ShapeDtypeStruct((4, 2, 4, 2, 2 * TILE, TILE), F32),
            jax.ShapeDtypeStruct((PART_ROWS, TILE), F32),
            jax.ShapeDtypeStruct((SOURCES * TILE, WIDTH), F32),
        ),
        in_specs=[SM, ANY, VM, VM, VM, VM, VM, ANY],
        out_specs=(VM, VM, ANY, VM, VM),
        scratch_shapes=[
            pltpu.VMEM((*layout, ROWS, TILE), F32),
            pltpu.VMEM((SLICES, 2, 136, TILE), F32),
            pltpu.VMEM((SLICES, 2, ROWS, TILE), F32),
            pltpu.VMEM((2, 4, 4, FIRST, TILE), F32),
            pltpu.VMEM((2, ROWS, TILE), F32),
            *[pltpu.VMEM((2, 4, 2, 2 * TILE, TILE), F32) for _ in range(4)],
            pltpu.VMEM((SLOTS, TILE, TILE), F32),
            pltpu.VMEM((n, WIDTH), F32),
            pltpu.VMEM((2, 4, 4, PART_ROWS, TILE), F32),
            pltpu.VMEM((4, 4, PART_ROWS, TILE), F32),
            pltpu.VMEM((3, 4, PART_ROWS, TILE), F32),
            pltpu.VMEM((3, PART_ROWS, TILE), F32),
            pltpu.VMEM((4, PART_ROWS, TILE), F32),
            pltpu.VMEM((PART_ROWS, TILE), F32),
            DMA((16,)),
            DMA((SLICES,)),
            DMA((SLICES, 3)),
            DMA((10,)),
            DMA((10,)),
            DMA((SLICES,)),
            DMA((SLICES, 4)),
            DMA((10,)),
            DMA((10,)),
            DMA((AR_SENDS,)),
            DMA((AR_SENDS,)),
            DMA((16,)),
            DMA,
        ],
        compiler_params=pltpu.CompilerParams(
            collective_id=1, has_side_effects=True, vmem_limit_bytes=VMEM_LIMIT
        ),
        name="exchange",
    )(plan, part.reshape(*layout, ROWS, TILE), x, ws, wn, bias.reshape(1, WIDTH), cot, values)
    layer_out, direct, g, gw, back = out
    return layer_out, direct, g.reshape(DESTS, 2 * TILE, TILE), gw, back


def rest_kernel(
    plan, source, keys, g_hbm, tiles_hbm, back_ref, out_ref, tiles, g, tile_sem, g_sem
):
    n = plan[PLAN_REST]

    def copies(i):
        slot = lax.rem(i, REST_SLOTS)
        t = plan[PLAN_LIST + i]
        return (
            pltpu.make_async_copy(tiles_hbm.at[t], tiles.at[slot], tile_sem.at[slot]),
            pltpu.make_async_copy(g_hbm.at[keys[1, t]], g.at[slot], g_sem.at[slot]),
        )

    def begin(i, _):
        for c in copies(i):
            c.start()
        return 0

    lax.fori_loop(0, jnp.minimum(n, REST_SLOTS), begin, 0)
    out_ref[...] = back_ref[...]

    def some(k, _):
        first = k * REST_UNROLL
        for u in range(REST_UNROLL):

            @pl.when(first + u < n)
            def _():
                for c in copies(first + u):
                    c.wait()

        products = []
        for u in range(REST_UNROLL):
            i = jnp.minimum(first + u, n - 1)
            slot = lax.rem(i, REST_SLOTS)
            hi, lo = split(tiles[slot] * jnp.where(first + u < n, 1.0, 0.0))
            ghi, glo = split(jnp.concatenate([g[slot, 0:TILE, :], g[slot, TILE:, :]], axis=1))
            a = jnp.concatenate([hi, lo, hi], axis=0)
            products.append((i, mm(a, jnp.concatenate([ghi, ghi, glo], axis=0), ((0,), (0,)))))
        for i, p in products:
            rows = pl.ds(pl.multiple_of(source[0, plan[PLAN_LIST + i]] * TILE, TILE), TILE)
            out_ref[rows, :] += p
        for u in range(REST_UNROLL):

            @pl.when(first + u + REST_SLOTS < n)
            def _():
                begin(first + u + REST_SLOTS, 0)

        return 0

    lax.fori_loop(0, lax.div(n + REST_UNROLL - 1, REST_UNROLL), some, 0)


def backward_rest(plan, source, keys, g, values, back):
    return pl.pallas_call(
        rest_kernel,
        out_shape=jax.ShapeDtypeStruct(back.shape, F32),
        in_specs=[SM, SM, SM, ANY, ANY, VM],
        out_specs=VM,
        scratch_shapes=[
            pltpu.VMEM((REST_SLOTS, TILE, TILE), F32),
            pltpu.VMEM((REST_SLOTS, 2 * TILE, TILE), F32),
            DMA((REST_SLOTS,)),
            DMA((REST_SLOTS,)),
        ],
        compiler_params=pltpu.CompilerParams(vmem_limit_bytes=VMEM_LIMIT),
        name="backward_rest",
    )(plan, source, keys, g, values, back)


def scatter_kernel(
    back_hbm, part_ref, out_hbm, gw_hbm,
    back_ref, out_ref, near, cross, send_buf, gws, send, recv, ar_send, ar_recv, load_sem, out_sem,
):
    row, col = lax.axis_index("row"), lax.axis_index("col")
    hi, core = lax.div(row, 2), lax.rem(row, 2)
    x, y, z = lax.div(col, 8), lax.rem(lax.div(col, 2), 4), lax.rem(col, 2)
    column = lambda xx, yy, zz: xx * 8 + yy * 2 + zz
    ahead = lambda p, d: lax.rem(p + d, 4)
    x_others = [(row, column(ahead(x, d), y, z)) for d in range(1, 4)]
    zg = hi * 2 + z
    z_others = []
    for d in range(1, 4):
        to = ahead(zg, d)
        z_others.append((lax.div(to, 2) * 2 + core, column(x, y, lax.rem(to, 2))))
    mate = (hi * 2 + (1 - core), col)
    far = z_others[1]
    peers = [mate] + x_others + z_others
    greet(peers)
    load = pltpu.make_async_copy(back_hbm, back_ref, load_sem)
    load.start()
    enter(peers)
    n = out_ref.shape[0]
    m = n // PIECES
    at = lambda r, c: pl.ds(pl.multiple_of(r * n + c * m, m), m)
    piece = lambda c: pl.ds(c * m, m)
    far_row, far_mate = (1 - hi) * 2 + core, (1 - hi) * 2 + (1 - core)
    write = lambda c: pltpu.make_async_copy(out_ref.at[piece(c)], out_hbm.at[piece(c)], out_sem.at[c])
    first, second, third = [], [], []
    for c in range(PIECES):
        src = back_ref.at[at(far_mate, c)]
        first.append(remote(src, near.at[0, piece(c)], send.at[0, c], recv.at[0, c], mate))
        src = back_ref.at[at(hi * 2 + (1 - core), c)]
        second.append(remote(src, near.at[1, piece(c)], send.at[1, c], recv.at[1, c], mate))
        third.append(remote(send_buf.at[piece(c)], cross.at[piece(c)], send.at[2, c], recv.at[2, c], far))
    hop = lambda i, ref, device: remote(ref, ref, ar_send.at[i], ar_recv.at[i], device)
    gws[core, zg, x] = part_ref[...]
    c5 = [hop(d, gws.at[core, zg, x], x_others[d]) for d in range(3)]
    c6 = [hop(3 + d, gws.at[core, zg], z_others[d]) for d in range(3)]
    c7 = [hop(6, gws.at[core], mate)]
    for c in c5:
        c.start()
    load.wait()
    for c in first + second:
        c.start()
    for c in range(PIECES):
        first[c].wait_recv()
        send_buf[piece(c), :] = back_ref[at(far_row, c), :] + near[0, piece(c), :]
        third[c].start()
    for d in range(3):
        hop(d, gws.at[core, zg, ahead(x, 3 - d)], x_others[d]).wait_recv()
    for c in c6:
        c.start()
    for d in range(3):
        hop(3 + d, gws.at[core, ahead(zg, 3 - d)], z_others[d]).wait_recv()
    for c in c7:
        c.start()
    for c in range(PIECES):
        second[c].wait_recv()
        third[c].wait_recv()
        out_ref[piece(c), :] = back_ref[at(row, c), :] + near[1, piece(c), :] + cross[piece(c), :]
        write(c).start()
    hop(6, gws.at[1 - core], mate).wait_recv()
    gw_write = pltpu.make_async_copy(gws, gw_hbm, out_sem.at[PIECES])
    gw_write.start()
    for c in range(PIECES):
        write(c).wait()
    gw_write.wait()
    for c in first + second + third + c5 + c6 + c7:
        c.wait_send()


def scatter_rows(back, part):
    n = back.shape[0] // 4
    parts = (2, 4, 4, PART_ROWS, TILE)
    back, gw = pl.pallas_call(
        scatter_kernel,
        out_shape=(jax.ShapeDtypeStruct((n, WIDTH), F32), jax.ShapeDtypeStruct(parts, F32)),
        in_specs=[ANY, VM],
        out_specs=(ANY, ANY),
        scratch_shapes=[
            pltpu.VMEM(back.shape, F32),
            pltpu.VMEM((n, WIDTH), F32),
            pltpu.VMEM((2, n, WIDTH), F32),
            pltpu.VMEM((n, WIDTH), F32),
            pltpu.VMEM((n, WIDTH), F32),
            pltpu.VMEM(parts, F32),
            DMA((3, PIECES)),
            DMA((3, PIECES)),
            DMA((7,)),
            DMA((7,)),
            DMA,
            DMA((PIECES + 1,)),
        ],
        compiler_params=pltpu.CompilerParams(collective_id=2, has_side_effects=True),
        name="scatter_rows",
    )(back, part)
    return back, gw.reshape(PARTS * PART_ROWS, TILE)


def finish_kernel(kept, direct, back, gw, kept_out, grad_x, grad_ws, grad_wn, grad_bias):
    kept_out[...] = kept[...]
    grad_x[...] = direct[...] + back[...]
    for i, out in enumerate((grad_ws, grad_wn)):
        for half in range(2):
            first = (2 * i + half) * WIDTH
            out[:, half * TILE : (half + 1) * TILE] = gw[first : first + WIDTH, :]
    for half in range(2):
        grad_bias[:, half * TILE : (half + 1) * TILE] = gw[4 * WIDTH + half : 4 * WIDTH + half + 1, :]


def finish(kept, direct, back, gw):
    rows, square = jax.ShapeDtypeStruct(direct.shape, F32), jax.ShapeDtypeStruct((WIDTH, WIDTH), F32)
    return pl.pallas_call(
        finish_kernel,
        out_shape=(rows, rows, square, square, jax.ShapeDtypeStruct((1, WIDTH), F32)),
        in_specs=[VM] * 4,
        out_specs=(VM,) * 5,
        name="finish",
    )(kept, direct, back, gw)


def body(x, ws, wn, bias, tile_values, tile_dest, tile_source, tile_count, cot):
    values = tile_values.reshape(SLOTS, TILE, TILE)
    dest, source = tile_dest.reshape(1, SLOTS), tile_source.reshape(1, SLOTS)
    count = tile_count.reshape(1)
    slab, keys = gather_rows(count, dest, source, x)
    part, plan = forward_tiles(dest, source, keys, count, slab, values)
    layer_out, direct, g, gw_part, back = exchange(plan, part, x, ws, wn, bias, cot, values)
    back = backward_rest(plan, source, keys, g, values, back)
    back, gw = scatter_rows(back, gw_part)
    layer_out, grad_x, grad_ws, grad_wn, grad_bias = finish(layer_out, direct, back, gw)
    return layer_out, grad_x, grad_ws, grad_wn, grad_bias.reshape(WIDTH)


def solution(mesh):
    in_specs = (
        P(("col", "row"), None),
        P(),
        P(),
        P(),
        P("row", "col", None, None, None),
        P("row", "col", None),
        P("row", "col", None),
        P("row", "col"),
        P(("col", "row"), None),
    )
    out_specs = (P(("col", "row"), None), P(("col", "row"), None), P(), P(), P())
    return jax.shard_map(body, mesh=mesh, in_specs=in_specs, out_specs=out_specs, check_vma=False)
```
